32 devices in a mesh: comp: 4 (over z), sub: 8 (over y, x, core).
Axes of the slice: x: 2, y: 2, z: 4, core: 2. Of those that a mesh axis runs over, the one named last changes fastest.
Arguments:
- atmos_profiles: bfloat16 [4, 72, 262144], P(None, None, ('comp', 'sub')), may hold values from -6 to 6
- atmos_mixing: bfloat16 [72, 72], replicated
- drag_factor: float32 [262144], P(('comp', 'sub')), may hold values from 0.5 to 1.5
- surface_before: float32 [4, 262144], P(None, ('comp', 'sub')), may hold values from -6 to 6
- downward_fluxes: float32 [4, 262144], P(None, ('comp', 'sub')), may hold values from -6 to 6
- land_weight: float32 [262144], P(('comp', 'sub')), may hold values from 0.05 to 1
- land_surface: float32 [4, 262144], P(None, ('comp', 'sub')), may hold values from -6 to 6
- ocean_state: float32 [4, 60, 262144], P(None, None, ('comp', 'sub')), may hold values from -6 to 6
- ocean_mixing: float32 [60, 60], replicated
- sea_mask: int32 [262144], P(('comp', 'sub')), may hold values 0 or 1
- exchange_slot: int32 [4, 262144], P(None, ('comp', 'sub')), may hold values from 0 to 65535, as said below
- parent_column: int32 [4, 262144], P(None, ('comp', 'sub')), may hold values from 0 to 8191, as said below
- ocean_weight: float32 [4, 262144], P(None, ('comp', 'sub')), may hold values from 0.1 to 1
- atmos_weight: float32 [4, 262144], P(None, ('comp', 'sub')), may hold values from 0.05 to 0.5
Outputs:
- atmos_updated: bfloat16 [4, 72, 262144], P(None, None, ('comp', 'sub'))
- ocean_updated: float32 [4, 60, 262144], P(None, None, ('comp', 'sub'))
- surface_state: float32 [4, 262144], P(None, ('comp', 'sub'))
The draws below stay inside these ranges and needn't reach their ends.
Inputs may be any that keep to these rules, and one draw needn't show every extreme that they name: Within the 8192 cells of one device block along the second dimension, all 32768 values are distinct, at most 2048 of them share one value of exchange_slot // 2048, and in every block some value of exchange_slot // 2048 is shared by exactly 2048 of them. In every aligned group of 128 cells along the second dimension (one k), the values are t * 128 + 0, 1, ..., 127 in order, for one t. In every aligned group of 128 cells along the second dimension (one k), all values share one value of parent_column // 128.
All inputs are finite; a program needn't handle non-finite values. No bound on the sum of `sea_mask` on one device may be relied on, other than what follows from the above.
Results may differ from the reference program's by a relative error of at most 0.001.
Values sent between devices are 32-bit elements; how exact they have to be, the bound alone decides.
No kernel may reach another device: no remote copies, remote signals or barrier semaphores. Data moves between devices by JAX's collectives and lax.ppermute only.
A program may use at most 128 MiB of HBM per device.

```python
import math
import jax
import jax.numpy as jnp
from jax import lax

LEVELS_ATMOS = 72
LEVELS_OCEAN = 60
INTERSECTIONS = 4
COLUMNS_DEV = 8192
CELLS_DEV = 8192
CAPACITY = 2048
TILE = 128
COLUMNS = 262144
CELLS = 262144
DEVICES = 32


def mixing_matrix(key, extent):
    main_key, rest_key = jax.random.split(key)
    main = jax.random.uniform(main_key, (extent,), jnp.float32, 0.5, 1.0)
    spread = jax.random.normal(rest_key, (extent, extent), jnp.float32) * (0.25 / math.sqrt(extent))
    return jnp.diag(main) + spread


def draw_atmos_mixing(key, part):
    return mixing_matrix(jax.random.fold_in(key, 3), LEVELS_ATMOS).astype(jnp.bfloat16)


def draw_ocean_mixing(key, part):
    return mixing_matrix(jax.random.fold_in(key, 5), LEVELS_OCEAN)


def slot_tables(key):
    tile_slots = DEVICES * CAPACITY // TILE
    tiles_dev = INTERSECTIONS * CELLS_DEV // TILE
    per_owner = CAPACITY // TILE

    def one_device(device_key):
        bias_key, full_key, score_key, order_key = jax.random.split(device_key, 4)
        source = jnp.arange(tile_slots, dtype=jnp.int32) // per_owner
        favour = jax.random.randint(bias_key, (DEVICES,), 0, 4) * 16384
        chosen = jax.random.randint(full_key, (), 0, DEVICES)
        scores = jax.random.randint(score_key, (tile_slots,), 0, 16384) + favour[source]
        scores = scores + jnp.where(source == chosen, 131072, 0)
        picked = jnp.argsort(-scores, stable=True)[:tiles_dev]
        shuffle = jax.random.permutation(order_key, tiles_dev)
        starts = picked[shuffle].astype(jnp.int32) * TILE
        lanes = jnp.arange(TILE, dtype=jnp.int32)
        return (starts[:, None] + lanes[None, :]).reshape(INTERSECTIONS, CELLS_DEV)
    tables = jax.vmap(one_device)(jax.random.split(key, DEVICES))
    return tables.transpose(1, 0, 2).reshape(INTERSECTIONS, DEVICES * CELLS_DEV)


def draw_exchange_slot(key, part):
    return slot_tables(jax.random.fold_in(key, 11))


def draw_parent_column(key, part):
    window_key, lane_key = jax.random.split(jax.random.fold_in(key, 13))
    window = jax.random.randint(window_key, (INTERSECTIONS, CELLS // TILE), 0, COLUMNS_DEV // TILE)
    lanes = jax.random.randint(lane_key, (INTERSECTIONS, CELLS), 0, TILE)
    return (jnp.repeat(window, TILE, axis=1) * TILE + lanes).astype(jnp.int32)


def set_ends(array, key, least, largest):
    index_at = [jax.random.randint(jax.random.fold_in(key, axis), (), 0, length) for axis, length in enumerate(array.shape)]
    widest = array.shape.index(max(array.shape))
    beside = index_at[:widest] + [(index_at[widest] + 1) % array.shape[widest]] + index_at[widest + 1:]
    return array.at[tuple(index_at)].set(least).at[tuple(beside)].set(largest)


def levels(stream_key, shape, cuts, least, top_value):
    loudness = 1.0
    for position, parts in cuts:
        draws = jax.random.uniform(jax.random.fold_in(jax.random.fold_in(stream_key, 6), position), (parts,), jnp.float32, least / len(cuts), top_value / len(cuts))
        loudness = loudness * jnp.repeat(jnp.exp(draws), shape[position] // parts).reshape((-1,) + (1,) * (len(shape) - 1 - position))
    return loudness


def normal_values(key, dims, deviation, bound, cuts=(), kind=jnp.bfloat16):
    values = deviation * jax.random.normal(key, dims, jnp.float32)
    if cuts:
        values = values * levels(key, dims, cuts, -0.22, 0.18)
    return jnp.clip(values, -bound, bound).astype(kind)


def setup_inputs(seed: int = 0) -> dict:
    streams_of = jax.random.split(jax.random.key(seed), 15)
    atmos_profiles = normal_values(streams_of[0], (4, LEVELS_ATMOS, COLUMNS), 1.0, 6.0, ((2, 32),))
    atmos_mixing = draw_atmos_mixing(jax.random.fold_in(streams_of[14], 71), 0)
    drag_factor = jnp.clip(jnp.exp(math.log(1.5) - 1.0986123 * jax.random.uniform(streams_of[2], (COLUMNS,), jnp.float32) ** levels(streams_of[2], (COLUMNS,), ((0, 32),), -0.2, 0.2)), 0.5, 1.5)
    surface_before = normal_values(streams_of[3], (4, COLUMNS), 1.0, 6.0, ((1, 32),), jnp.float32)
    downward_fluxes = normal_values(streams_of[4], (4, COLUMNS), 1.0, 6.0, ((1, 32),), jnp.float32)
    land_weight = jnp.clip(jnp.exp(math.log(1.0) - 2.9957323 * jax.random.uniform(streams_of[5], (COLUMNS,), jnp.float32) ** levels(streams_of[5], (COLUMNS,), ((0, 32),), -0.2, 0.2)), 0.05, 1.0)
    land_surface = normal_values(streams_of[6], (4, COLUMNS), 1.0, 6.0, ((1, 32),), jnp.float32)
    ocean_state = normal_values(streams_of[7], (4, LEVELS_OCEAN, CELLS), 1.0, 6.0, ((2, 32),), jnp.float32)
    ocean_mixing = draw_ocean_mixing(jax.random.fold_in(streams_of[14], 71), 0)
    sea_mask = set_ends((jax.random.randint(streams_of[9], (CELLS,), 0, 4) < 3).astype(jnp.int32), jax.random.fold_in(streams_of[9], 1), 0, 1)
    exchange_slot = draw_exchange_slot(jax.random.fold_in(streams_of[14], 71), 0)
    parent_column = draw_parent_column(jax.random.fold_in(streams_of[14], 71), 0)
    ocean_weight = jnp.clip(jnp.exp(math.log(1.0) - 2.3025851 * jax.random.uniform(streams_of[12], (INTERSECTIONS, CELLS), jnp.float32) ** levels(streams_of[12], (INTERSECTIONS, CELLS), ((1, 32),), -0.2, 0.2)), 0.1, 1.0)
    atmos_weight = jnp.clip(jnp.exp(math.log(0.5) - 2.3025851 * jax.random.uniform(streams_of[13], (INTERSECTIONS, CELLS), jnp.float32) ** levels(streams_of[13], (INTERSECTIONS, CELLS), ((1, 32),), -0.2, 0.2)), 0.05, 0.5)
    return {"atmos_profiles": atmos_profiles, "atmos_mixing": atmos_mixing, "drag_factor": drag_factor, "surface_before": surface_before, "downward_fluxes": downward_fluxes, "land_weight": land_weight, "land_surface": land_surface, "ocean_state": ocean_state, "ocean_mixing": ocean_mixing, "sea_mask": sea_mask, "exchange_slot": exchange_slot, "parent_column": parent_column, "ocean_weight": ocean_weight, "atmos_weight": atmos_weight}


couple_rate = 0.5

def surface_fluxes(atmos_profiles, drag_factor, surface_before, downward_fluxes):
    bottom = atmos_profiles[:, -1, :].astype(jnp.float32)
    east_gap = bottom[2] - surface_before[2]
    north_gap = bottom[3] - surface_before[3]
    wind_speed = jnp.sqrt(1.0 + east_gap * east_gap + north_gap * north_gap)
    transfer = drag_factor * wind_speed
    sensible = transfer * (surface_before[0] - bottom[0])
    latent = transfer * (surface_before[1] - bottom[1])
    return jnp.stack([sensible, latent, transfer * east_gap, transfer * north_gap, downward_fluxes[0], downward_fluxes[1], downward_fluxes[2], downward_fluxes[3]])

def diffuse_atmos(atmos_profiles, atmos_mixing, fluxes):
    lowest = atmos_mixing[:, -1].astype(jnp.float32)
    tendency = couple_rate * jnp.stack([fluxes[0], fluxes[1], -fluxes[2], -fluxes[3]])
    result = []
    for member in range(4):
        mixed_rows = jnp.dot(atmos_mixing, atmos_profiles[member], preferred_element_type=jnp.float32)
        result.append(mixed_rows + lowest[:, None] * tendency[member][None, :])
    return jnp.stack(result).astype(jnp.bfloat16)

def forcing_rows(fluxes):
    return couple_rate * jnp.stack([fluxes[4] + fluxes[5] - fluxes[0] - fluxes[1], fluxes[1] - fluxes[6] - fluxes[7], fluxes[2], fluxes[3]])

def reference(atmos_profiles, atmos_mixing, drag_factor, surface_before, downward_fluxes, land_weight, land_surface, ocean_state, ocean_mixing, sea_mask, exchange_slot, parent_column, ocean_weight, atmos_weight):
    fluxes = surface_fluxes(atmos_profiles, drag_factor, surface_before, downward_fluxes)
    atmos_updated = diffuse_atmos(atmos_profiles, atmos_mixing, fluxes)
    column_forcing = forcing_rows(fluxes)
    parent = exchange_slot // CAPACITY * COLUMNS_DEV + parent_column
    flat_parent = parent.reshape(-1).astype(jnp.int32)
    at_cells = jnp.take(column_forcing, flat_parent, axis=1).reshape(4, INTERSECTIONS, CELLS)
    forcing = lax.optimization_barrier(jnp.sum(ocean_weight[None] * at_cells, axis=1)) / lax.optimization_barrier(jnp.sum(ocean_weight, axis=0))[None]
    loaded = ocean_state.at[:, 0, :].add(forcing)
    mixed_state = jnp.stack([jnp.dot(ocean_mixing, loaded[member], precision=lax.Precision.HIGHEST) for member in range(4)])
    ocean_updated = jnp.where(sea_mask[None, None, :] == 1, mixed_state, ocean_state)
    sea_share = atmos_weight * sea_mask.astype(jnp.float32)[None, :]
    outgoing = jnp.concatenate([sea_share[None] * ocean_updated[:, 0, :][:, None, :], sea_share[None]], axis=0)
    summed = jnp.zeros((5, COLUMNS), jnp.float32).at[:, flat_parent].add(outgoing.reshape(5, -1))
    surface_state = (summed[:4] + land_weight[None] * land_surface) / (summed[4] + land_weight)[None]
    return (atmos_updated, ocean_updated, surface_state)
```

```python
import functools

import jax
import jax.numpy as jnp
from jax import lax
from jax.experimental import pallas as pl
from jax.experimental.pallas import tpu as pltpu
from jax.sharding import PartitionSpec as P

couple_rate = 0.5
LANES = 128
VMEM_BYTES = 56 * 1024 * 1024
params = pltpu.CompilerParams(vmem_limit_bytes=VMEM_BYTES)
vmem = pl.BlockSpec(memory_space=pltpu.VMEM)
smem = pl.BlockSpec(memory_space=pltpu.SMEM)
AXES = ("comp", "sub")


def window(index):
    return pl.ds(pl.multiple_of(index * LANES, LANES), LANES)


def surface_rates(bottom, drag_factor, surface_before, downward):
    east = bottom[2] - surface_before[2]
    north = bottom[3] - surface_before[3]
    transfer = drag_factor * jnp.sqrt(1.0 + east * east + north * north)
    sensible = transfer * (surface_before[0] - bottom[0])
    latent = transfer * (surface_before[1] - bottom[1])
    east_stress = couple_rate * (transfer * east)
    north_stress = couple_rate * (transfer * north)
    forcing = jnp.stack(
        [
            couple_rate * (downward[0] + downward[1] - sensible - latent),
            couple_rate * (latent - downward[2] - downward[3]),
            east_stress,
            north_stress,
        ]
    )
    tendency = jnp.stack(
        [couple_rate * sensible, couple_rate * latent, -east_stress, -north_stress]
    )
    return forcing, tendency


def atmos_kernel(mix_ref, tend_ref, x_ref, out_ref):
    mix = mix_ref[...]
    lowest = mix[:, mix.shape[1] - 1 :].astype(jnp.float32)
    for member in range(x_ref.shape[0]):
        mixed = jnp.dot(mix, x_ref[member], preferred_element_type=jnp.float32)
        out_ref[member] = (mixed + lowest * tend_ref[member : member + 1, :]).astype(jnp.bfloat16)


def diffuse_atmos(profiles, mixing, tendency):
    fields, levels, columns = profiles.shape
    block = min(1024, columns)
    return pl.pallas_call(
        atmos_kernel,
        grid=(columns // block,),
        in_specs=[
            pl.BlockSpec((levels, levels), lambda i: (0, 0)),
            pl.BlockSpec((fields, block), lambda i: (0, i)),
            pl.BlockSpec((fields, levels, block), lambda i: (0, 0, i)),
        ],
        out_specs=pl.BlockSpec((fields, levels, block), lambda i: (0, 0, i)),
        out_shape=jax.ShapeDtypeStruct(profiles.shape, jnp.bfloat16),
        compiler_params=params,
        cost_estimate=pl.CostEstimate(
            flops=2 * fields * levels * levels * columns,
            bytes_accessed=4 * fields * levels * columns,
            transcendentals=0,
        ),
        name="diffuse_atmos",
    )(mixing, tendency, profiles)


def top_kernel(mix_ref, x_ref, out_ref):
    levels = x_ref.shape[0]
    total = mix_ref[0, 0] * x_ref[0]
    for level in range(1, levels):
        total = total + mix_ref[0, level] * x_ref[level]
    out_ref[...] = total


def top_level(state, mixing):
    levels, fields, cells = state.shape
    block = min(1024, cells)
    return pl.pallas_call(
        top_kernel,
        grid=(cells // block,),
        in_specs=[smem, pl.BlockSpec((levels, fields, block), lambda i: (0, 0, i))],
        out_specs=pl.BlockSpec((fields, block), lambda i: (0, i)),
        out_shape=jax.ShapeDtypeStruct((fields, cells), jnp.float32),
        compiler_params=params,
        cost_estimate=pl.CostEstimate(
            flops=2 * fields * levels * cells,
            bytes_accessed=4 * fields * levels * cells,
            transcendentals=0,
        ),
        name="top_level",
    )(mixing[0:1], state)


def scatter_lanes(values, lanes, column_ids):
    hot = jnp.where(column_ids == lanes, 1.0, 0.0).astype(jnp.bfloat16)
    high = values.astype(jnp.bfloat16).astype(jnp.float32)
    rows = values.shape[0]
    parts = jnp.concatenate([high, values - high], axis=0).astype(jnp.bfloat16)
    spread = lax.dot_general(
        parts, hot, (((1,), (1,)), ((), ())), preferred_element_type=jnp.float32
    )
    return spread[:rows] + spread[rows:]


def share_kernel(per_owner, place_ref, column_ref, weight_ref, mask_ref, wins_ref, out_ref):
    intersections, cells = column_ref.shape
    windows = cells // LANES
    out_ref[...] = jnp.zeros(out_ref.shape, jnp.float32)
    out_ref[:, :, per_owner * LANES :] = wins_ref[...]
    column_ids = lax.broadcasted_iota(jnp.int32, (LANES, LANES), 0)

    def body(spot, carry):
        mask = mask_ref[:, window(spot)].astype(jnp.float32)
        lanes = column_ref[:, window(spot)] & (LANES - 1)
        share = weight_ref[:, window(spot)] * mask
        for k in range(intersections):
            place = place_ref[k * windows + spot]
            row = jnp.broadcast_to(share[k : k + 1], (4, LANES))
            spread = scatter_lanes(row, lanes[k : k + 1], column_ids)
            out_ref[place // per_owner, :, window(place % per_owner)] = spread[0:1]
        return carry

    lax.fori_loop(0, windows, body, 0, unroll=2)


def middle_kernel(
    per_owner,
    place_ref,
    window_ref,
    corner_ref,
    gathered_ref,
    column_ref,
    ocean_weight_ref,
    atmos_weight_ref,
    mask_ref,
    base_ref,
    state_ref,
    forcing_ref,
    send_ref,
):
    intersections, cells = column_ref.shape
    windows = cells // LANES
    fields = base_ref.shape[0]
    send_ref[...] = jnp.zeros(send_ref.shape, jnp.float32)
    column_ids = lax.broadcasted_iota(jnp.int32, (LANES, LANES), 0)
    corner = corner_ref[0, 0]

    def body(spot, carry):
        here = window(spot)
        lanes = column_ref[:, here] & (LANES - 1)
        ocean_weight = ocean_weight_ref[:, here]
        total = jnp.zeros((fields, LANES), jnp.float32)
        weight = jnp.zeros((1, LANES), jnp.float32)
        for k in range(intersections):
            tile = k * windows + spot
            owner = place_ref[tile] // per_owner
            rows = gathered_ref[owner, :, window(window_ref[tile])]
            picked = jnp.take_along_axis(
                rows,
                jnp.broadcast_to(lanes[k : k + 1], (fields, LANES)),
                axis=1,
                mode="promise_in_bounds",
            )
            total = total + ocean_weight[k : k + 1] * picked
            weight = weight + ocean_weight[k : k + 1]
        forcing = total / weight
        forcing_ref[:, here] = forcing
        mask = mask_ref[:, here]
        surface = jnp.where(mask == 1, base_ref[:, here] + corner * forcing, state_ref[0, :, here])
        share = atmos_weight_ref[:, here] * mask.astype(jnp.float32)
        for k in range(intersections):
            place = place_ref[k * windows + spot]
            spread = scatter_lanes(share[k : k + 1] * surface, lanes[k : k + 1], column_ids)
            send_ref[place // per_owner, :, window(place % per_owner)] = spread
        return carry

    lax.fori_loop(0, windows, body, 0, unroll=2)


def ocean_kernel(fields, mix_ref, forcing_ref, mask_ref, x_ref, out_ref):
    levels, _, block = x_ref.shape
    x = x_ref[...]
    flat = x.reshape(levels * fields, block)
    row = lax.broadcasted_iota(jnp.int32, flat.shape, 0)
    push = jnp.concatenate(
        [forcing_ref[...], jnp.zeros((flat.shape[0] - fields, block), jnp.float32)], axis=0
    )
    loaded = flat + push
    high = loaded.astype(jnp.bfloat16)
    low = (loaded - high.astype(jnp.float32)).astype(jnp.bfloat16)
    mix = mix_ref[...]
    mix_high = mix.astype(jnp.bfloat16)
    mix_low = (mix - mix_high.astype(jnp.float32)).astype(jnp.bfloat16)
    mixed = (
        jnp.dot(mix_high, high, preferred_element_type=jnp.float32)
        + jnp.dot(mix_high, low, preferred_element_type=jnp.float32)
        + jnp.dot(mix_low, high, preferred_element_type=jnp.float32)
    )
    out_ref[...] = jnp.where(mask_ref[...] == 1, mixed, flat).reshape(levels, fields, block)


def diffuse_ocean(state, mixing, forcing, mask):
    levels, fields, cells = state.shape
    block = min(1024, cells)
    wide = jnp.kron(mixing, jnp.eye(fields, dtype=jnp.float32))
    return pl.pallas_call(
        functools.partial(ocean_kernel, fields),
        grid=(cells // block,),
        in_specs=[
            pl.BlockSpec(wide.shape, lambda i: (0, 0)),
            pl.BlockSpec((fields, block), lambda i: (0, i)),
            pl.BlockSpec((1, block), lambda i: (0, i)),
            pl.BlockSpec((levels, fields, block), lambda i: (0, 0, i)),
        ],
        out_specs=pl.BlockSpec((levels, fields, block), lambda i: (0, 0, i)),
        out_shape=jax.ShapeDtypeStruct(state.shape, jnp.float32),
        compiler_params=params,
        cost_estimate=pl.CostEstimate(
            flops=6 * (fields * levels) ** 2 * cells,
            bytes_accessed=8 * fields * levels * cells,
            transcendentals=0,
        ),
        name="diffuse_ocean",
    )(wide, forcing, mask, state)


def final_kernel(
    per_owner, wins_ref, share_ref, back_ref, land_weight_ref, land_ref, out_ref, *sums
):
    devices = back_ref.shape[0]
    for ref in sums:
        ref[...] = jnp.zeros(ref.shape, jnp.float32)
    chains = len(sums) // 2
    stride = devices // chains

    def body(step, carry):
        for slot in range(per_owner):
            for chain in range(chains):
                source = chain * stride + step
                spot = window(wins_ref[source * per_owner + slot])
                from_ = slice(slot * LANES, (slot + 1) * LANES)
                sums[chain][:, spot] += back_ref[source, :, from_]
                sums[chains + chain][:, spot] += share_ref[source, :, from_]
        return carry

    lax.fori_loop(0, stride, body, 0)
    total = land_weight_ref[...] * land_ref[...]
    weight = land_weight_ref[...]
    for chain in range(chains):
        total = total + sums[chain][...]
        weight = weight + sums[chains + chain][...]
    out_ref[...] = total / weight


def per_device(
    atmos_profiles,
    atmos_mixing,
    drag_factor,
    surface_before,
    downward_fluxes,
    land_weight,
    land_surface,
    ocean_state,
    ocean_mixing,
    sea_mask,
    exchange_slot,
    parent_column,
    ocean_weight,
    atmos_weight,
):
    devices = lax.axis_size("comp") * lax.axis_size("sub")
    fields, _, columns = atmos_profiles.shape
    intersections, cells = exchange_slot.shape
    capacity = 2 * intersections * cells // devices
    per_owner = capacity // LANES
    slots = devices * per_owner
    tiles = intersections * cells // LANES
    mask = sea_mask.reshape(1, cells)
    state = ocean_state.transpose(1, 0, 2)

    bottom = atmos_profiles[:, -1, :].astype(jnp.float32)
    forcing_rows, tendency = surface_rates(bottom, drag_factor, surface_before, downward_fluxes)
    gathered = lax.all_gather(forcing_rows, AXES, axis=0, tiled=False)

    place = exchange_slot.reshape(tiles, LANES)[:, 0] // LANES
    tile_window = parent_column.reshape(tiles, LANES)[:, 0] // LANES
    slot_window = jnp.sum(
        jnp.where(
            place[None, :] == jnp.arange(slots, dtype=jnp.int32)[:, None], tile_window[None, :], 0
        ),
        axis=1,
    )
    wins = jnp.pad(
        slot_window.astype(jnp.float32).reshape(devices, 1, per_owner),
        ((0, 0), (0, 0), (0, LANES - per_owner)),
    )
    share_send = pl.pallas_call(
        functools.partial(share_kernel, per_owner),
        in_specs=[smem, vmem, vmem, vmem, vmem],
        out_specs=vmem,
        out_shape=jax.ShapeDtypeStruct((devices, 1, (per_owner + 1) * LANES), jnp.float32),
        compiler_params=params,
        name="share_windows",
    )(place, parent_column, atmos_weight, mask, wins)
    share_back = lax.all_to_all(share_send, AXES, split_axis=0, concat_axis=0, tiled=True)
    back_windows = (
        share_back[:, 0, per_owner * LANES : per_owner * LANES + per_owner] + 0.5
    ).astype(jnp.int32).reshape(slots)

    atmos_updated = diffuse_atmos(atmos_profiles, atmos_mixing, tendency)
    base = top_level(state, ocean_mixing)

    forcing, send = pl.pallas_call(
        functools.partial(middle_kernel, per_owner),
        grid=(1,),
        in_specs=[
            smem,
            smem,
            smem,
            pl.BlockSpec((devices, fields, columns), lambda i: (0, 0, 0)),
            pl.BlockSpec((intersections, cells), lambda i: (0, 0)),
            pl.BlockSpec((intersections, cells), lambda i: (0, 0)),
            pl.BlockSpec((intersections, cells), lambda i: (0, 0)),
            pl.BlockSpec((1, cells), lambda i: (0, 0)),
            pl.BlockSpec((fields, cells), lambda i: (0, 0)),
            pl.BlockSpec((1, fields, cells), lambda i: (0, 0, 0)),
        ],
        out_specs=[
            pl.BlockSpec((fields, cells), lambda i: (0, 0)),
            pl.BlockSpec((devices, fields, capacity), lambda i: (0, 0, 0)),
        ],
        out_shape=[
            jax.ShapeDtypeStruct((fields, cells), jnp.float32),
            jax.ShapeDtypeStruct((devices, fields, capacity), jnp.float32),
        ],
        compiler_params=params,
        name="forcing_and_windows",
    )(
        place,
        tile_window,
        ocean_mixing[0:1, 0:1],
        gathered,
        parent_column,
        ocean_weight,
        atmos_weight,
        mask,
        base,
        state,
    )
    back = lax.all_to_all(send, AXES, split_axis=0, concat_axis=0, tiled=True)
    ocean_updated = diffuse_ocean(state, ocean_mixing, forcing, mask).transpose(1, 0, 2)

    chains = 4
    surface_state = pl.pallas_call(
        functools.partial(final_kernel, per_owner),
        in_specs=[smem, vmem, vmem, vmem, vmem],
        out_specs=vmem,
        out_shape=jax.ShapeDtypeStruct((fields, columns), jnp.float32),
        scratch_shapes=[pltpu.VMEM((fields, columns), jnp.float32)] * chains
        + [pltpu.VMEM((1, columns), jnp.float32)] * chains,
        compiler_params=params,
        name="surface_state",
    )(back_windows, share_back, back, land_weight.reshape(1, columns), land_surface)
    return (atmos_updated, ocean_updated, surface_state)


def solution(mesh):
    split = P(None, AXES)
    return jax.shard_map(
        per_device,
        mesh=mesh,
        in_specs=(
            P(None, None, AXES),
            P(),
            P(AXES),
            split,
            split,
            P(AXES),
            split,
            P(None, None, AXES),
            P(),
            P(AXES),
            split,
            split,
            split,
            split,
        ),
        out_specs=(P(None, None, AXES), P(None, None, AXES), split),
        check_vma=False,
    )
```

```python
import functools

import jax
import jax.numpy as jnp
from jax import lax
from jax.experimental import pallas as pl
from jax.experimental.pallas import tpu as pltpu
from jax.sharding import PartitionSpec as P

couple_rate = 0.5
LANES = 128
VMEM_BYTES = 56 * 1024 * 1024
params = pltpu.CompilerParams(vmem_limit_bytes=VMEM_BYTES)
vmem = pl.BlockSpec(memory_space=pltpu.VMEM)
smem = pl.BlockSpec(memory_space=pltpu.SMEM)
AXES = ("far", "near", "sub")


def window(index):
    return pl.ds(pl.multiple_of(index * LANES, LANES), LANES)


def flux_kernel(bottom_ref, drag_ref, before_ref, down_ref, forcing_ref, tend_ref):
    def row(ref, index):
        return ref[index : index + 1, :]

    east = row(bottom_ref, 2) - row(before_ref, 2)
    north = row(bottom_ref, 3) - row(before_ref, 3)
    transfer = drag_ref[...] * jnp.sqrt(1.0 + east * east + north * north)
    sensible = transfer * (row(before_ref, 0) - row(bottom_ref, 0))
    latent = transfer * (row(before_ref, 1) - row(bottom_ref, 1))
    east_stress = couple_rate * (transfer * east)
    north_stress = couple_rate * (transfer * north)
    forcing_ref[0:1, :] = couple_rate * (
        row(down_ref, 0) + row(down_ref, 1) - sensible - latent
    )
    forcing_ref[1:2, :] = couple_rate * (latent - row(down_ref, 2) - row(down_ref, 3))
    forcing_ref[2:3, :] = east_stress
    forcing_ref[3:4, :] = north_stress
    tend_ref[0:1, :] = couple_rate * sensible
    tend_ref[1:2, :] = couple_rate * latent
    tend_ref[2:3, :] = -east_stress
    tend_ref[3:4, :] = -north_stress


def atmos_kernel(mix_ref, tend_ref, x_ref, out_ref):
    mix = mix_ref[...]
    lowest = mix[:, mix.shape[1] - 1 :].astype(jnp.float32)
    for member in range(x_ref.shape[0]):
        mixed = jnp.dot(mix, x_ref[member], preferred_element_type=jnp.float32)
        out_ref[member] = (mixed + lowest * tend_ref[member : member + 1, :]).astype(jnp.bfloat16)


def diffuse_atmos(profiles, mixing, tendency):
    fields, levels, columns = profiles.shape
    block = min(1024, columns)
    return pl.pallas_call(
        atmos_kernel,
        grid=(columns // block,),
        in_specs=[
            pl.BlockSpec((levels, levels), lambda i: (0, 0)),
            pl.BlockSpec((fields, block), lambda i: (0, i)),
            pl.BlockSpec((fields, levels, block), lambda i: (0, 0, i)),
        ],
        out_specs=pl.BlockSpec((fields, levels, block), lambda i: (0, 0, i)),
        out_shape=jax.ShapeDtypeStruct(profiles.shape, jnp.bfloat16),
        compiler_params=params,
        cost_estimate=pl.CostEstimate(
            flops=2 * fields * levels * levels * columns,
            bytes_accessed=4 * fields * levels * columns,
            transcendentals=0,
        ),
        name="diffuse_atmos",
    )(mixing, tendency, profiles)


def top_kernel(mix_ref, x_ref, out_ref):
    levels = x_ref.shape[0]
    total = mix_ref[0, 0] * x_ref[0]
    for level in range(1, levels):
        total = total + mix_ref[0, level] * x_ref[level]
    out_ref[...] = total


def top_level(state, mixing):
    levels, fields, cells = state.shape
    block = min(1024, cells)
    return pl.pallas_call(
        top_kernel,
        grid=(cells // block,),
        in_specs=[smem, pl.BlockSpec((levels, fields, block), lambda i: (0, 0, i))],
        out_specs=pl.BlockSpec((fields, block), lambda i: (0, i)),
        out_shape=jax.ShapeDtypeStruct((fields, cells), jnp.float32),
        compiler_params=params,
        cost_estimate=pl.CostEstimate(
            flops=2 * fields * levels * cells,
            bytes_accessed=4 * fields * levels * cells,
            transcendentals=0,
        ),
        name="top_level",
    )(mixing[0:1], state)


def serve_kernel(per_owner, far_ref, asked_ref, own_ref, other_ref, out_ref, blocks_ref):
    far = far_ref[0]
    blocks_ref[far] = own_ref[...]
    blocks_ref[1 - far] = other_ref[...]

    def body(peer, carry):
        for shard in range(2):
            for slot in range(per_owner):
                spot = shard * per_owner + slot
                out_ref[peer, :, spot * LANES : (spot + 1) * LANES] = blocks_ref[
                    shard, :, window(asked_ref[peer, spot])
                ]
        return carry

    lax.fori_loop(0, out_ref.shape[0], body, 0)


def split_high(values):
    high = values.astype(jnp.bfloat16).astype(jnp.float32)
    return jnp.concatenate([high, values - high], axis=0)


def middle_kernel(
    per_owner,
    place_ref,
    corner_ref,
    arrived_ref,
    column_ref,
    ocean_weight_ref,
    atmos_weight_ref,
    mask_ref,
    base_ref,
    state_ref,
    forcing_ref,
    send_ref,
):
    intersections, cells = column_ref.shape
    windows = cells // LANES
    fields = base_ref.shape[0]
    near = arrived_ref.shape[0]
    spots = 2 * per_owner
    send_ref[...] = jnp.zeros(send_ref.shape, jnp.float32)
    column_ids = lax.broadcasted_iota(jnp.int32, (LANES, LANES), 0)
    share_rows = lax.broadcasted_iota(jnp.int32, (2 * intersections, LANES), 0)
    first_half = share_rows % intersections < 2
    field_ids = lax.broadcasted_iota(jnp.int32, (fields, LANES), 0)
    corner = corner_ref[0, 0]

    def body(step, carry):
        here = window(step)
        lanes = column_ref[:, here] & (LANES - 1)
        ocean_weight = ocean_weight_ref[:, here]
        total = jnp.zeros((fields, LANES), jnp.float32)
        weight = jnp.zeros((1, LANES), jnp.float32)
        where = []
        for k in range(intersections):
            place = place_ref[k, step]
            owner = place // per_owner
            peer, spot = owner % near, owner // near * per_owner + place % per_owner
            where.append((peer, spot))
            picked = jnp.take_along_axis(
                arrived_ref[peer, :, window(spot)],
                jnp.broadcast_to(lanes[k : k + 1], (fields, LANES)),
                axis=1,
                mode="promise_in_bounds",
            )
            total = total + ocean_weight[k : k + 1] * picked
            weight = weight + ocean_weight[k : k + 1]
        forcing = total / weight
        forcing_ref[:, here] = forcing
        mask = mask_ref[:, here]
        surface = jnp.where(mask == 1, base_ref[:, here] + corner * forcing, state_ref[0, :, here])
        share = atmos_weight_ref[:, here] * mask.astype(jnp.float32)
        hot = [
            jnp.where(column_ids == lanes[k : k + 1], 1.0, 0.0).astype(jnp.bfloat16)
            for k in range(intersections)
        ]
        hot = jnp.concatenate(
            [
                jnp.concatenate([hot[0], hot[2]], axis=1),
                jnp.concatenate([hot[1], hot[3]], axis=1),
            ],
            axis=0,
        )
        parts = [split_high(share[k : k + 1] * surface) for k in range(intersections)]
        share_parts = split_high(share)
        blank = jnp.zeros((2 * fields, LANES), jnp.float32)
        left = [parts[0], parts[1], blank, blank, jnp.where(first_half, share_parts, 0.0)]
        right = [blank, blank, parts[2], parts[3], jnp.where(first_half, 0.0, share_parts)]
        rows = jnp.concatenate(
            [jnp.concatenate(left, axis=0), jnp.concatenate(right, axis=0)], axis=1
        ).astype(jnp.bfloat16)
        spread = lax.dot_general(
            rows, hot, (((1,), (1,)), ((), ())), preferred_element_type=jnp.float32
        )
        top = 2 * fields * intersections
        for k in range(intersections):
            peer, spot = where[k]
            side = slice((k % 2) * LANES, (k % 2 + 1) * LANES)
            at = 2 * fields * k
            send_ref[peer, :, window(spot)] = (
                spread[at : at + fields, side] + spread[at + fields : at + 2 * fields, side]
            )
            shared = (
                spread[top + k : top + k + 1, side]
                + spread[top + intersections + k : top + intersections + k + 1, side]
            )
            send_ref[peer, :, window(spots + spot // fields)] += jnp.where(
                field_ids == spot % fields, shared, 0.0
            )
        return carry

    lax.fori_loop(0, windows, body, 0, unroll=2)


def ocean_kernel(mix_ref, forcing_ref, mask_ref, x_ref, out_ref, high_ref, low_ref):
    levels, fields, block = x_ref.shape
    rows = levels * fields

    @pl.when(pl.program_id(0) == 0)
    def _():
        level = lax.broadcasted_iota(jnp.int32, (rows, levels), 0) // fields
        pick = (level == lax.broadcasted_iota(jnp.int32, (rows, levels), 1)).astype(jnp.float32)
        tall = jnp.dot(pick, mix_ref[...], precision=lax.Precision.HIGHEST)
        wide = lax.dot_general(
            tall, pick, (((1,), (1,)), ((), ())), precision=lax.Precision.HIGHEST
        )
        down = lax.broadcasted_iota(jnp.int32, (rows, rows), 0) % fields
        across = lax.broadcasted_iota(jnp.int32, (rows, rows), 1) % fields
        wide = jnp.where(down == across, wide, 0.0)
        high = wide.astype(jnp.bfloat16)
        high_ref[...] = high
        low_ref[...] = (wide - high.astype(jnp.float32)).astype(jnp.bfloat16)

    flat = x_ref[...].reshape(rows, block)
    push = jnp.concatenate(
        [forcing_ref[...], jnp.zeros((rows - fields, block), jnp.float32)], axis=0
    )
    loaded = flat + push
    high = loaded.astype(jnp.bfloat16)
    low = (loaded - high.astype(jnp.float32)).astype(jnp.bfloat16)
    mixed = (
        jnp.dot(high_ref[...], high, preferred_element_type=jnp.float32)
        + jnp.dot(high_ref[...], low, preferred_element_type=jnp.float32)
        + jnp.dot(low_ref[...], high, preferred_element_type=jnp.float32)
    )
    out_ref[...] = jnp.where(mask_ref[...] == 1, mixed, flat).reshape(levels, fields, block)


def diffuse_ocean(state, mixing, forcing, mask):
    levels, fields, cells = state.shape
    block = min(1024, cells)
    rows = levels * fields
    return pl.pallas_call(
        ocean_kernel,
        grid=(cells // block,),
        in_specs=[
            pl.BlockSpec(mixing.shape, lambda i: (0, 0)),
            pl.BlockSpec((fields, block), lambda i: (0, i)),
            pl.BlockSpec((1, block), lambda i: (0, i)),
            pl.BlockSpec((levels, fields, block), lambda i: (0, 0, i)),
        ],
        out_specs=pl.BlockSpec((levels, fields, block), lambda i: (0, 0, i)),
        out_shape=jax.ShapeDtypeStruct(state.shape, jnp.float32),
        scratch_shapes=[pltpu.VMEM((rows, rows), jnp.bfloat16)] * 2,
        compiler_params=params,
        cost_estimate=pl.CostEstimate(
            flops=6 * rows * rows * cells,
            bytes_accessed=8 * rows * cells,
            transcendentals=0,
        ),
        name="diffuse_ocean",
    )(mixing, forcing, mask, state)


def collect_kernel(per_owner, far_ref, asked_ref, back_ref, keep_ref, send_ref, *sums):
    near, fields, _ = back_ref.shape
    columns = sums[0].shape[1]
    quarter = columns // fields
    chains = len(sums) // 4
    spots = 2 * per_owner
    for ref in sums:
        ref[...] = jnp.zeros(ref.shape, jnp.float32)

    def body(step, carry):
        for spot in range(spots):
            shard = spot // per_owner
            for chain in range(chains):
                peer = step * chains + chain
                at = window(asked_ref[peer, spot])
                tile = spots + spot // fields
                row = spot % fields
                values, shares = sums[4 * chain + shard], sums[4 * chain + 2 + shard]
                values[:, at] += back_ref[peer, :, spot * LANES : (spot + 1) * LANES]
                shares[:, at] += back_ref[
                    peer, row : row + 1, tile * LANES : (tile + 1) * LANES
                ]
        return carry

    lax.fori_loop(0, near // chains, body, 0)
    far = far_ref[0]
    total = []
    for kind in range(4):
        value = sums[kind][...]
        for chain in range(1, chains):
            value = value + sums[4 * chain + kind][...]
        total.append(value)
    for ref, first in ((keep_ref, 0), (send_ref, 1)):
        ref[:, :columns] = jnp.where(far == first, total[0], total[1])
        shares = jnp.where(far == first, total[2], total[3])
        for row in range(fields):
            ref[row : row + 1, columns : columns + quarter] = shares[
                :, row * quarter : (row + 1) * quarter
            ]


def final_kernel(keep_ref, other_ref, land_weight_ref, land_ref, out_ref):
    fields, columns = out_ref.shape
    quarter = columns // fields
    both = keep_ref[:, :columns] + other_ref[:, :columns]
    shares = keep_ref[:, columns:] + other_ref[:, columns:]
    land_weight = land_weight_ref[...]
    total = both + land_weight * land_ref[...]
    for row in range(fields):
        part = slice(row * quarter, (row + 1) * quarter)
        out_ref[:, part] = total[:, part] / (shares[row : row + 1] + land_weight[:, part])


def per_device(
    atmos_profiles,
    atmos_mixing,
    drag_factor,
    surface_before,
    downward_fluxes,
    land_weight,
    land_surface,
    ocean_state,
    ocean_mixing,
    sea_mask,
    exchange_slot,
    parent_column,
    ocean_weight,
    atmos_weight,
):
    near = lax.axis_size("near") * lax.axis_size("sub")
    devices = 2 * near
    fields, _, columns = atmos_profiles.shape
    intersections, cells = exchange_slot.shape
    capacity = 2 * intersections * cells // devices
    per_owner = capacity // LANES
    spots = 2 * per_owner
    mask = sea_mask.reshape(1, cells)
    state = ocean_state.transpose(1, 0, 2)
    far = lax.axis_index("far").astype(jnp.int32).reshape(1)

    def to_near(values):
        return lax.all_to_all(values, ("near", "sub"), split_axis=0, concat_axis=0, tiled=True)

    def to_far(values):
        return lax.ppermute(values, "far", ((0, 1), (1, 0)))

    place = exchange_slot[:, ::LANES] // LANES
    tile_window = parent_column[:, ::LANES] // LANES
    peer_ids = jnp.arange(near, dtype=jnp.int32)[:, None]
    spot_ids = jnp.arange(spots, dtype=jnp.int32)[None, :]
    place_ids = (spot_ids // per_owner * near + peer_ids) * per_owner + spot_ids % per_owner
    wanted = jnp.sum(
        jnp.where(
            place.reshape(1, 1, -1) == place_ids[:, :, None], tile_window.reshape(1, 1, -1), 0
        ),
        axis=2,
    )
    asked = to_near(wanted)

    bottom = atmos_profiles[:, -1, :].astype(jnp.float32)
    forcing_rows, tendency = pl.pallas_call(
        flux_kernel,
        in_specs=[vmem] * 4,
        out_specs=[vmem] * 2,
        out_shape=[jax.ShapeDtypeStruct((fields, columns), jnp.float32)] * 2,
        compiler_params=params,
        name="surface_rates",
    )(bottom, drag_factor.reshape(1, columns), surface_before, downward_fluxes)
    other_rows = to_far(forcing_rows)
    served = pl.pallas_call(
        functools.partial(serve_kernel, per_owner),
        in_specs=[smem, smem, vmem, vmem],
        out_specs=vmem,
        out_shape=jax.ShapeDtypeStruct((near, fields, spots * LANES), jnp.float32),
        scratch_shapes=[pltpu.VMEM((2, fields, columns), jnp.float32)],
        compiler_params=params,
        name="serve_windows",
    )(far, asked, forcing_rows, other_rows)
    arrived = to_near(served)
    base = top_level(state, ocean_mixing)
    atmos_updated = diffuse_atmos(atmos_profiles, atmos_mixing, tendency)

    def whole(*shape):
        return pl.BlockSpec(shape, lambda i: (0,) * len(shape))

    lanes_out = (spots + spots // fields) * LANES
    forcing, send = pl.pallas_call(
        functools.partial(middle_kernel, per_owner),
        grid=(1,),
        in_specs=[
            smem,
            smem,
            whole(near, fields, spots * LANES),
            whole(intersections, cells),
            whole(intersections, cells),
            whole(intersections, cells),
            whole(1, cells),
            whole(fields, cells),
            whole(1, fields, cells),
        ],
        out_specs=[whole(fields, cells), whole(near, fields, lanes_out)],
        out_shape=[
            jax.ShapeDtypeStruct((fields, cells), jnp.float32),
            jax.ShapeDtypeStruct((near, fields, lanes_out), jnp.float32),
        ],
        compiler_params=params,
        name="forcing_and_windows",
    )(
        place,
        ocean_mixing[0:1, 0:1],
        arrived,
        parent_column,
        ocean_weight,
        atmos_weight,
        mask,
        base,
        state,
    )
    back = to_near(send)
    ocean_updated = diffuse_ocean(state, ocean_mixing, forcing, mask).transpose(1, 0, 2)

    chains = 2
    packed = (fields, columns + columns // fields)
    keep, away = pl.pallas_call(
        functools.partial(collect_kernel, per_owner),
        in_specs=[smem, smem, vmem],
        out_specs=[vmem] * 2,
        out_shape=[jax.ShapeDtypeStruct(packed, jnp.float32)] * 2,
        scratch_shapes=(
            [pltpu.VMEM((fields, columns), jnp.float32)] * 2
            + [pltpu.VMEM((1, columns), jnp.float32)] * 2
        )
        * chains,
        compiler_params=params,
        name="collect_windows",
    )(far, asked, back)
    surface_state = pl.pallas_call(
        final_kernel,
        in_specs=[vmem] * 4,
        out_specs=vmem,
        out_shape=jax.ShapeDtypeStruct((fields, columns), jnp.float32),
        compiler_params=params,
        name="surface_state",
    )(keep, to_far(away), land_weight.reshape(1, columns), land_surface)
    return (atmos_updated, ocean_updated, surface_state)


def solution(mesh):
    comp, sub = mesh.devices.shape
    halves = jax.sharding.Mesh(mesh.devices.reshape(2, comp // 2, sub), AXES)
    split = P(None, AXES)
    return jax.shard_map(
        per_device,
        mesh=halves,
        in_specs=(
            P(None, None, AXES),
            P(),
            P(AXES),
            split,
            split,
            P(AXES),
            split,
            P(None, None, AXES),
            P(),
            P(AXES),
            split,
            split,
            split,
            split,
        ),
        out_specs=(P(None, None, AXES), P(None, None, AXES), split),
        check_vma=False,
    )
```

```python
import functools

import jax
import jax.numpy as jnp
from jax import lax
from jax.experimental import pallas as pl
from jax.experimental.pallas import tpu as pltpu
from jax.sharding import PartitionSpec as P

couple_rate = 0.5
LANES = 128
params = pltpu.CompilerParams(vmem_limit_bytes=24 * 1024 * 1024)
stream_params = pltpu.CompilerParams(vmem_limit_bytes=56 * 1024 * 1024)
vmem = pl.BlockSpec(memory_space=pltpu.VMEM)
smem = pl.BlockSpec(memory_space=pltpu.SMEM)
AXES = ("far", "near", "sub")


def window(index):
    return pl.ds(pl.multiple_of(index * LANES, LANES), LANES)


def request_kernel(per_owner, slot_ref, column_ref, place_ref, wanted_ref):
    intersections, cells = slot_ref.shape
    near, spots = wanted_ref.shape
    windows = cells // LANES
    lane = lax.broadcasted_iota(jnp.int32, (intersections, windows), 1)

    def heads(ref):
        found = jnp.zeros((intersections, windows), jnp.int32)
        for step in range(windows):
            head = ref[:, step * LANES : step * LANES + 1]
            found = jnp.where(lane == step, head, found)
        return found // LANES

    place = heads(slot_ref)
    column_window = heads(column_ref)
    owner = place // per_owner
    peer = owner % near
    spot = owner // near * per_owner + place % per_owner
    place_ref[...] = peer * spots + spot
    peer_ids = lax.broadcasted_iota(jnp.int32, (near, windows), 0)
    spot_ids = lax.broadcasted_iota(jnp.int32, (spots, windows), 0)
    wanted = jnp.zeros((near, spots), jnp.float32)
    for k in range(intersections):
        row = slice(k, k + 1)
        peer_hot = jnp.where(peer_ids == peer[row], 1.0, 0.0)
        spot_hot = jnp.where(
            spot_ids == spot[row], column_window[row].astype(jnp.float32), 0.0
        )
        wanted = wanted + lax.dot_general(
            peer_hot.astype(jnp.bfloat16),
            spot_hot.astype(jnp.bfloat16),
            (((1,), (1,)), ((), ())),
            preferred_element_type=jnp.float32,
        )
    wanted_ref[...] = wanted.astype(jnp.int32)


def flux_kernel(last, x_ref, drag_ref, before_ref, down_ref, forcing_ref, tend_ref):
    def row(ref, index):
        return ref[index : index + 1, :]

    bottom = [x_ref[member].astype(jnp.float32)[last : last + 1, :] for member in range(4)]
    east = bottom[2] - row(before_ref, 2)
    north = bottom[3] - row(before_ref, 3)
    transfer = drag_ref[...] * jnp.sqrt(1.0 + east * east + north * north)
    sensible = transfer * (row(before_ref, 0) - bottom[0])
    latent = transfer * (row(before_ref, 1) - bottom[1])
    east_stress = couple_rate * (transfer * east)
    north_stress = couple_rate * (transfer * north)
    forcing_ref[0:1, :] = couple_rate * (
        row(down_ref, 0) + row(down_ref, 1) - sensible - latent
    )
    forcing_ref[1:2, :] = couple_rate * (latent - row(down_ref, 2) - row(down_ref, 3))
    forcing_ref[2:3, :] = east_stress
    forcing_ref[3:4, :] = north_stress
    tend_ref[0:1, :] = couple_rate * sensible
    tend_ref[1:2, :] = couple_rate * latent
    tend_ref[2:3, :] = -east_stress
    tend_ref[3:4, :] = -north_stress


def surface_rates(profiles, drag_factor, surface_before, downward):
    fields, levels, columns = profiles.shape
    block = min(4096, columns)
    tall = 16
    at = (levels - 1) // tall
    rows = pl.BlockSpec((fields, block), lambda i: (0, i))
    return pl.pallas_call(
        functools.partial(flux_kernel, levels - 1 - at * tall),
        grid=(columns // block,),
        in_specs=[
            pl.BlockSpec((fields, tall, block), lambda i: (0, at, i)),
            pl.BlockSpec((1, block), lambda i: (0, i)),
            rows,
            rows,
        ],
        out_specs=[rows, rows],
        out_shape=[jax.ShapeDtypeStruct((fields, columns), jnp.float32)] * 2,
        compiler_params=stream_params,
        name="surface_rates",
    )(profiles, drag_factor.reshape(1, columns), surface_before, downward)


def atmos_kernel(mix_ref, tend_ref, x_ref, out_ref):
    mix = mix_ref[...]
    lowest = mix[:, mix.shape[1] - 1 :].astype(jnp.float32)
    for member in range(x_ref.shape[0]):
        mixed = jnp.dot(mix, x_ref[member], preferred_element_type=jnp.float32)
        out_ref[member] = (mixed + lowest * tend_ref[member : member + 1, :]).astype(jnp.bfloat16)


def diffuse_atmos(profiles, mixing, tendency):
    fields, levels, columns = profiles.shape
    block = min(1024, columns)
    return pl.pallas_call(
        atmos_kernel,
        grid=(columns // block,),
        in_specs=[
            pl.BlockSpec((levels, levels), lambda i: (0, 0)),
            pl.BlockSpec((fields, block), lambda i: (0, i)),
            pl.BlockSpec((fields, levels, block), lambda i: (0, 0, i)),
        ],
        out_specs=pl.BlockSpec((fields, levels, block), lambda i: (0, 0, i)),
        out_shape=jax.ShapeDtypeStruct(profiles.shape, jnp.bfloat16),
        compiler_params=stream_params,
        cost_estimate=pl.CostEstimate(
            flops=2 * fields * levels * levels * columns,
            bytes_accessed=4 * fields * levels * columns,
            transcendentals=0,
        ),
        name="diffuse_atmos",
    )(mixing, tendency, profiles)


def top_kernel(mix_ref, x_ref, out_ref):
    levels = x_ref.shape[0]
    total = mix_ref[0, 0] * x_ref[0]
    for level in range(1, levels):
        total = total + mix_ref[0, level] * x_ref[level]
    out_ref[...] = total


def top_level(state, mixing):
    levels, fields, cells = state.shape
    block = min(1024, cells)
    return pl.pallas_call(
        top_kernel,
        grid=(cells // block,),
        in_specs=[smem, pl.BlockSpec((levels, fields, block), lambda i: (0, 0, i))],
        out_specs=pl.BlockSpec((fields, block), lambda i: (0, i)),
        out_shape=jax.ShapeDtypeStruct((fields, cells), jnp.float32),
        compiler_params=stream_params,
        cost_estimate=pl.CostEstimate(
            flops=2 * fields * levels * cells,
            bytes_accessed=4 * fields * levels * cells,
            transcendentals=0,
        ),
        name="top_level",
    )(mixing[0:1], state)


def serve_kernel(per_owner, far_ref, asked_ref, own_ref, other_ref, out_ref, blocks_ref):
    far = far_ref[0]
    blocks_ref[far] = own_ref[...]
    blocks_ref[1 - far] = other_ref[...]

    def body(peer, carry):
        for shard in range(2):
            for slot in range(per_owner):
                spot = shard * per_owner + slot
                out_ref[peer, :, spot * LANES : (spot + 1) * LANES] = blocks_ref[
                    shard, :, window(asked_ref[peer, spot])
                ]
        return carry

    lax.fori_loop(0, out_ref.shape[0], body, 0)


def split_high(values):
    high = values.astype(jnp.bfloat16).astype(jnp.float32)
    return jnp.concatenate([high, values - high], axis=0)


GROUP = 8


def middle_kernel(
    place_ref,
    corner_ref,
    arrived_ref,
    column_ref,
    ocean_weight_ref,
    atmos_weight_ref,
    mask_ref,
    base_ref,
    state_ref,
    forcing_ref,
    send_ref,
    lanes_ref,
    *share_refs,
):
    intersections, cells = column_ref.shape
    windows = cells // LANES
    fields = base_ref.shape[0]
    spots = arrived_ref.shape[2] // LANES
    send_ref[...] = jnp.zeros(send_ref.shape, jnp.float32)
    for ref in share_refs:
        ref[...] = jnp.zeros(ref.shape, jnp.float32)
    corner = corner_ref[0, 0]
    group_tiles = GROUP * intersections
    steps = LANES // intersections
    for first in range(0, windows, steps):
        tall = jnp.concatenate(
            [
                column_ref[:, (first + step) * LANES : (first + step + 1) * LANES] & (LANES - 1)
                for step in range(steps)
            ],
            axis=0,
        )
        turned = tall.astype(jnp.float32).T.astype(jnp.bfloat16)
        for part in range(steps // GROUP):
            lanes_ref[first // GROUP + part, :, :group_tiles] = turned[
                :, part * group_tiles : (part + 1) * group_tiles
            ]
    column_ids = lax.broadcasted_iota(jnp.int32, (LANES, LANES), 1)
    column_ids = column_ids.astype(jnp.float32).astype(jnp.bfloat16)
    one, zero = jnp.bfloat16(1.0), jnp.bfloat16(0.0)
    field_ids = lax.broadcasted_iota(jnp.int32, (fields, LANES), 0)
    share_rows = lax.broadcasted_iota(jnp.int32, (2 * intersections, LANES), 0)
    first_half = share_rows % intersections < 2
    blank = jnp.zeros((2 * fields, LANES), jnp.float32)
    top = 2 * fields * intersections

    def body(group, carry):
        turned = lanes_ref[group]
        for inner in range(GROUP):
            step = group * GROUP + inner
            here = window(step)
            lanes = column_ref[:, here] & (LANES - 1)
            ocean_weight = ocean_weight_ref[:, here]
            total = jnp.zeros((fields, LANES), jnp.float32)
            weight = jnp.zeros((1, LANES), jnp.float32)
            where = []
            for k in range(intersections):
                place = place_ref[k, step]
                peer, spot = place // spots, place % spots
                where.append((peer, spot))
                picked = jnp.take_along_axis(
                    arrived_ref[peer, :, window(spot)],
                    jnp.broadcast_to(lanes[k : k + 1], (fields, LANES)),
                    axis=1,
                    mode="promise_in_bounds",
                )
                total = total + ocean_weight[k : k + 1] * picked
                weight = weight + ocean_weight[k : k + 1]
            forcing = total / weight
            forcing_ref[:, here] = forcing
            mask = mask_ref[:, here]
            surface = jnp.where(
                mask == 1, base_ref[:, here] + corner * forcing, state_ref[0, :, here]
            )
            share = atmos_weight_ref[:, here] * mask.astype(jnp.float32)
            hot = []
            for k in range(intersections):
                tile = inner * intersections + k
                lane_of = jnp.broadcast_to(turned[:, tile : tile + 1], (LANES, LANES))
                hot.append(jnp.where(lane_of == column_ids, one, zero))
            hot = jnp.concatenate(
                [
                    jnp.concatenate([hot[0], hot[1]], axis=1),
                    jnp.concatenate([hot[2], hot[3]], axis=1),
                ],
                axis=0,
            )
            parts = [split_high(share[k : k + 1] * surface) for k in range(intersections)]
            share_parts = split_high(share)
            left = [parts[0], parts[1], blank, blank, jnp.where(first_half, share_parts, 0.0)]
            right = [blank, blank, parts[2], parts[3], jnp.where(first_half, 0.0, share_parts)]
            rows = jnp.concatenate(
                [jnp.concatenate(left, axis=0), jnp.concatenate(right, axis=0)], axis=1
            ).astype(jnp.bfloat16)
            spread = jnp.dot(rows, hot, preferred_element_type=jnp.float32)
            for k in range(intersections):
                peer, spot = where[k]
                side = slice((k % 2) * LANES, (k % 2 + 1) * LANES)
                at = 2 * fields * k
                send_ref[peer, :, window(spot)] = (
                    spread[at : at + fields, side] + spread[at + fields : at + 2 * fields, side]
                )
                shared = (
                    spread[top + k : top + k + 1, side]
                    + spread[top + intersections + k : top + intersections + k + 1, side]
                )
                share_refs[k][peer, :, window(spot // fields)] += jnp.where(
                    field_ids == spot % fields, shared, 0.0
                )
        return carry

    lax.fori_loop(0, windows // GROUP, body, 0)
    shares = share_refs[0][...]
    for ref in share_refs[1:]:
        shares = shares + ref[...]
    send_ref[:, :, spots * LANES :] = shares


def ocean_kernel(mix_ref, forcing_ref, mask_ref, x_ref, out_ref, high_ref, low_ref):
    levels, fields, block = x_ref.shape
    rows = levels * fields

    @pl.when(pl.program_id(0) == 0)
    def _():
        level = lax.broadcasted_iota(jnp.int32, (rows, levels), 0) // fields
        pick = (level == lax.broadcasted_iota(jnp.int32, (rows, levels), 1)).astype(jnp.float32)
        tall = jnp.dot(pick, mix_ref[...], precision=lax.Precision.HIGHEST)
        wide = lax.dot_general(
            tall, pick, (((1,), (1,)), ((), ())), precision=lax.Precision.HIGHEST
        )
        down = lax.broadcasted_iota(jnp.int32, (rows, rows), 0) % fields
        across = lax.broadcasted_iota(jnp.int32, (rows, rows), 1) % fields
        wide = jnp.where(down == across, wide, 0.0)
        high = wide.astype(jnp.bfloat16)
        high_ref[...] = high
        low_ref[...] = (wide - high.astype(jnp.float32)).astype(jnp.bfloat16)

    flat = x_ref[...].reshape(rows, block)
    push = jnp.concatenate(
        [forcing_ref[...], jnp.zeros((rows - fields, block), jnp.float32)], axis=0
    )
    loaded = flat + push
    high = loaded.astype(jnp.bfloat16)
    low = (loaded - high.astype(jnp.float32)).astype(jnp.bfloat16)
    mixed = (
        jnp.dot(high_ref[...], high, preferred_element_type=jnp.float32)
        + jnp.dot(high_ref[...], low, preferred_element_type=jnp.float32)
        + jnp.dot(low_ref[...], high, preferred_element_type=jnp.float32)
    )
    out_ref[...] = jnp.where(mask_ref[...] == 1, mixed, flat).reshape(levels, fields, block)


def diffuse_ocean(state, mixing, forcing, mask):
    levels, fields, cells = state.shape
    block = min(1024, cells)
    rows = levels * fields
    return pl.pallas_call(
        ocean_kernel,
        grid=(cells // block,),
        in_specs=[
            pl.BlockSpec(mixing.shape, lambda i: (0, 0)),
            pl.BlockSpec((fields, block), lambda i: (0, i)),
            pl.BlockSpec((1, block), lambda i: (0, i)),
            pl.BlockSpec((levels, fields, block), lambda i: (0, 0, i)),
        ],
        out_specs=pl.BlockSpec((levels, fields, block), lambda i: (0, 0, i)),
        out_shape=jax.ShapeDtypeStruct(state.shape, jnp.float32),
        scratch_shapes=[pltpu.VMEM((rows, rows), jnp.bfloat16)] * 2,
        compiler_params=stream_params,
        cost_estimate=pl.CostEstimate(
            flops=6 * rows * rows * cells,
            bytes_accessed=8 * rows * cells,
            transcendentals=0,
        ),
        name="diffuse_ocean",
    )(mixing, forcing, mask, state)


def collect_kernel(per_owner, far_ref, asked_ref, back_ref, keep_ref, send_ref, *sums):
    near, fields, _ = back_ref.shape
    columns = sums[0].shape[1]
    quarter = columns // fields
    chains = len(sums) // 4
    spots = 2 * per_owner
    for ref in sums:
        ref[...] = jnp.zeros(ref.shape, jnp.float32)

    def body(step, carry):
        for spot in range(spots):
            shard = spot // per_owner
            for chain in range(chains):
                peer = step * chains + chain
                at = window(asked_ref[peer, spot])
                tile = spots + spot // fields
                row = spot % fields
                values, shares = sums[4 * chain + shard], sums[4 * chain + 2 + shard]
                values[:, at] += back_ref[peer, :, spot * LANES : (spot + 1) * LANES]
                shares[:, at] += back_ref[
                    peer, row : row + 1, tile * LANES : (tile + 1) * LANES
                ]
        return carry

    lax.fori_loop(0, near // chains, body, 0)
    far = far_ref[0]
    total = []
    for kind in range(4):
        value = sums[kind][...]
        for chain in range(1, chains):
            value = value + sums[4 * chain + kind][...]
        total.append(value)
    for ref, first in ((keep_ref, 0), (send_ref, 1)):
        ref[:, :columns] = jnp.where(far == first, total[0], total[1])
        shares = jnp.where(far == first, total[2], total[3])
        for row in range(fields):
            ref[row : row + 1, columns : columns + quarter] = shares[
                :, row * quarter : (row + 1) * quarter
            ]


def final_kernel(keep_ref, other_ref, land_weight_ref, land_ref, out_ref):
    fields, columns = out_ref.shape
    quarter = columns // fields
    both = keep_ref[:, :columns] + other_ref[:, :columns]
    shares = keep_ref[:, columns:] + other_ref[:, columns:]
    land_weight = land_weight_ref[...]
    total = both + land_weight * land_ref[...]
    for row in range(fields):
        part = slice(row * quarter, (row + 1) * quarter)
        out_ref[:, part] = total[:, part] / (shares[row : row + 1] + land_weight[:, part])


def per_device(
    atmos_profiles,
    atmos_mixing,
    drag_factor,
    surface_before,
    downward_fluxes,
    land_weight,
    land_surface,
    ocean_state,
    ocean_mixing,
    sea_mask,
    exchange_slot,
    parent_column,
    ocean_weight,
    atmos_weight,
):
    near = lax.axis_size("near") * lax.axis_size("sub")
    devices = 2 * near
    fields, _, columns = atmos_profiles.shape
    intersections, cells = exchange_slot.shape
    capacity = 2 * intersections * cells // devices
    per_owner = capacity // LANES
    spots = 2 * per_owner
    mask = sea_mask.reshape(1, cells)
    state = ocean_state.transpose(1, 0, 2)
    far = lax.axis_index("far").astype(jnp.int32).reshape(1)

    def to_near(values):
        return lax.all_to_all(values, ("near", "sub"), split_axis=0, concat_axis=0, tiled=True)

    def to_far(values):
        return lax.ppermute(values, "far", ((0, 1), (1, 0)))

    place, wanted = pl.pallas_call(
        functools.partial(request_kernel, per_owner),
        in_specs=[vmem] * 2,
        out_specs=[vmem] * 2,
        out_shape=[
            jax.ShapeDtypeStruct((intersections, cells // LANES), jnp.int32),
            jax.ShapeDtypeStruct((near, spots), jnp.int32),
        ],
        compiler_params=params,
        name="requests",
    )(exchange_slot, parent_column)
    asked = to_near(wanted)
    forcing_rows, tendency = surface_rates(
        atmos_profiles, drag_factor, surface_before, downward_fluxes
    )
    other_rows = to_far(forcing_rows)
    served = pl.pallas_call(
        functools.partial(serve_kernel, per_owner),
        in_specs=[smem, smem, vmem, vmem],
        out_specs=vmem,
        out_shape=jax.ShapeDtypeStruct((near, fields, spots * LANES), jnp.float32),
        scratch_shapes=[pltpu.VMEM((2, fields, columns), jnp.float32)],
        compiler_params=params,
        name="serve_windows",
    )(far, asked, forcing_rows, other_rows)
    arrived = to_near(served)
    base = top_level(state, ocean_mixing)
    atmos_updated = diffuse_atmos(atmos_profiles, atmos_mixing, tendency)
    arrived, atmos_updated, base = lax.optimization_barrier((arrived, atmos_updated, base))

    def whole(*shape):
        return pl.BlockSpec(shape, lambda i: (0,) * len(shape))

    lanes_out = (spots + spots // fields) * LANES
    forcing, send = pl.pallas_call(
        middle_kernel,
        grid=(1,),
        in_specs=[
            smem,
            smem,
            whole(near, fields, spots * LANES),
            whole(intersections, cells),
            whole(intersections, cells),
            whole(intersections, cells),
            whole(1, cells),
            whole(fields, cells),
            whole(1, fields, cells),
        ],
        out_specs=[whole(fields, cells), whole(near, fields, lanes_out)],
        out_shape=[
            jax.ShapeDtypeStruct((fields, cells), jnp.float32),
            jax.ShapeDtypeStruct((near, fields, lanes_out), jnp.float32),
        ],
        scratch_shapes=[pltpu.VMEM((cells // LANES // GROUP, LANES, LANES), jnp.bfloat16)]
        + [pltpu.VMEM((near, fields, spots // fields * LANES), jnp.float32)] * intersections,
        compiler_params=params,
        name="forcing_and_windows",
    )(
        place,
        ocean_mixing[0:1, 0:1],
        arrived,
        parent_column,
        ocean_weight,
        atmos_weight,
        mask,
        base,
        state,
    )
    back = to_near(send)
    ocean_updated = diffuse_ocean(state, ocean_mixing, forcing, mask).transpose(1, 0, 2)
    back, ocean_updated = lax.optimization_barrier((back, ocean_updated))

    chains = 2
    packed = (fields, columns + columns // fields)
    keep, away = pl.pallas_call(
        functools.partial(collect_kernel, per_owner),
        in_specs=[smem, smem, vmem],
        out_specs=[vmem] * 2,
        out_shape=[jax.ShapeDtypeStruct(packed, jnp.float32)] * 2,
        scratch_shapes=(
            [pltpu.VMEM((fields, columns), jnp.float32)] * 2
            + [pltpu.VMEM((1, columns), jnp.float32)] * 2
        )
        * chains,
        compiler_params=params,
        name="collect_windows",
    )(far, asked, back)
    surface_state = pl.pallas_call(
        final_kernel,
        in_specs=[vmem] * 4,
        out_specs=vmem,
        out_shape=jax.ShapeDtypeStruct((fields, columns), jnp.float32),
        compiler_params=params,
        name="surface_state",
    )(keep, to_far(away), land_weight.reshape(1, columns), land_surface)
    return (atmos_updated, ocean_updated, surface_state)


def solution(mesh):
    comp, sub = mesh.devices.shape
    halves = jax.sharding.Mesh(mesh.devices.reshape(2, comp // 2, sub), AXES)
    split = P(None, AXES)
    return jax.shard_map(
        per_device,
        mesh=halves,
        in_specs=(
            P(None, None, AXES),
            P(),
            P(AXES),
            split,
            split,
            P(AXES),
            split,
            P(None, None, AXES),
            P(),
            P(AXES),
            split,
            split,
            split,
            split,
        ),
        out_specs=(P(None, None, AXES), P(None, None, AXES), split),
        check_vma=False,
    )
```

```python
import functools

import jax
import jax.numpy as jnp
from jax import lax
from jax.experimental import pallas as pl
from jax.experimental.pallas import tpu as pltpu
from jax.sharding import PartitionSpec as P

couple_rate = 0.5
LANES = 128
params = pltpu.CompilerParams(vmem_limit_bytes=24 * 1024 * 1024)
stream_params = pltpu.CompilerParams(vmem_limit_bytes=56 * 1024 * 1024)
vmem = pl.BlockSpec(memory_space=pltpu.VMEM)
smem = pl.BlockSpec(memory_space=pltpu.SMEM)
AXES = ("far", "near", "sub")


def window(index):
    return pl.ds(pl.multiple_of(index * LANES, LANES), LANES)


def request_kernel(per_owner, slot_ref, column_ref, place_ref, spot_ref, wanted_ref):
    intersections, cells = slot_ref.shape
    near, spots = wanted_ref.shape
    windows = cells // LANES
    lane = lax.broadcasted_iota(jnp.int32, (intersections, windows), 1)

    def heads(ref):
        found = jnp.zeros((intersections, windows), jnp.int32)
        for step in range(windows):
            head = ref[:, step * LANES : step * LANES + 1]
            found = jnp.where(lane == step, head, found)
        return found // LANES

    place = heads(slot_ref)
    column_window = heads(column_ref)
    owner = place // per_owner
    peer = owner % near
    spot = owner // near * per_owner + place % per_owner
    place_ref[...] = place
    spot_ref[...] = peer * spots + spot
    peer_ids = lax.broadcasted_iota(jnp.int32, (near, windows), 0)
    spot_ids = lax.broadcasted_iota(jnp.int32, (spots, windows), 0)
    wanted = jnp.zeros((near, spots), jnp.float32)
    for k in range(intersections):
        row = slice(k, k + 1)
        peer_hot = jnp.where(peer_ids == peer[row], 1.0, 0.0)
        spot_hot = jnp.where(
            spot_ids == spot[row], column_window[row].astype(jnp.float32), 0.0
        )
        wanted = wanted + lax.dot_general(
            peer_hot.astype(jnp.bfloat16),
            spot_hot.astype(jnp.bfloat16),
            (((1,), (1,)), ((), ())),
            preferred_element_type=jnp.float32,
        )
    wanted_ref[...] = wanted.astype(jnp.int32)


def flux_kernel(last, x_ref, drag_ref, before_ref, down_ref, forcing_ref, tend_ref):
    def row(ref, index):
        return ref[index : index + 1, :]

    bottom = [x_ref[member].astype(jnp.float32)[last : last + 1, :] for member in range(4)]
    east = bottom[2] - row(before_ref, 2)
    north = bottom[3] - row(before_ref, 3)
    transfer = drag_ref[...] * jnp.sqrt(1.0 + east * east + north * north)
    sensible = transfer * (row(before_ref, 0) - bottom[0])
    latent = transfer * (row(before_ref, 1) - bottom[1])
    east_stress = couple_rate * (transfer * east)
    north_stress = couple_rate * (transfer * north)
    forcing_ref[0:1, :] = couple_rate * (
        row(down_ref, 0) + row(down_ref, 1) - sensible - latent
    )
    forcing_ref[1:2, :] = couple_rate * (latent - row(down_ref, 2) - row(down_ref, 3))
    forcing_ref[2:3, :] = east_stress
    forcing_ref[3:4, :] = north_stress
    tend_ref[0:1, :] = couple_rate * sensible
    tend_ref[1:2, :] = couple_rate * latent
    tend_ref[2:3, :] = -east_stress
    tend_ref[3:4, :] = -north_stress


def surface_rates(profiles, drag_factor, surface_before, downward):
    fields, levels, columns = profiles.shape
    block = min(4096, columns)
    tall = 16
    at = (levels - 1) // tall
    rows = pl.BlockSpec((fields, block), lambda i: (0, i))
    return pl.pallas_call(
        functools.partial(flux_kernel, levels - 1 - at * tall),
        grid=(columns // block,),
        in_specs=[
            pl.BlockSpec((fields, tall, block), lambda i: (0, at, i)),
            pl.BlockSpec((1, block), lambda i: (0, i)),
            rows,
            rows,
        ],
        out_specs=[rows, rows],
        out_shape=[jax.ShapeDtypeStruct((fields, columns), jnp.float32)] * 2,
        compiler_params=stream_params,
        name="surface_rates",
    )(profiles, drag_factor.reshape(1, columns), surface_before, downward)


def atmos_kernel(mix_ref, tend_ref, *refs):
    mix = mix_ref[...]
    lowest = mix[:, mix.shape[1] - 1 :].astype(jnp.float32)
    out_ref = refs[-1]
    for member, x_ref in enumerate(refs[:-1]):
        mixed = jnp.dot(mix, x_ref[0], preferred_element_type=jnp.float32)
        out_ref[member] = (mixed + lowest * tend_ref[member : member + 1, :]).astype(jnp.bfloat16)


def diffuse_atmos(profiles, mixing, tendency):
    fields, levels, columns = profiles.shape
    block = min(2048, columns)

    def field(member):
        return pl.BlockSpec((1, levels, block), lambda i: (member, 0, i))

    return pl.pallas_call(
        atmos_kernel,
        grid=(columns // block,),
        in_specs=[
            pl.BlockSpec((levels, levels), lambda i: (0, 0)),
            pl.BlockSpec((fields, block), lambda i: (0, i)),
        ]
        + [field(member) for member in range(fields)],
        out_specs=pl.BlockSpec((fields, levels, block), lambda i: (0, 0, i)),
        out_shape=jax.ShapeDtypeStruct(profiles.shape, jnp.bfloat16),
        compiler_params=stream_params,
        cost_estimate=pl.CostEstimate(
            flops=2 * fields * levels * levels * columns,
            bytes_accessed=4 * fields * levels * columns,
            transcendentals=0,
        ),
        name="diffuse_atmos",
    )(mixing, tendency, *[profiles] * fields)


def level_specs(levels, fields, block):
    count = 4 if levels % 4 == 0 else 1

    def part(number):
        return pl.BlockSpec((levels // count, fields, block), lambda i: (number, 0, i))

    return [part(number) for number in range(count)]


def top_kernel(mix_ref, *refs):
    state_refs, base_ref, first_ref = refs[:-2], refs[-2], refs[-1]
    total = None
    level = 0
    for ref in state_refs:
        for inner in range(ref.shape[0]):
            term = mix_ref[0, level] * ref[inner]
            total = term if total is None else total + term
            level += 1
    base_ref[...] = total
    first_ref[...] = state_refs[0][0]


def top_level(state, mixing):
    levels, fields, cells = state.shape
    block = min(2048, cells)
    specs = level_specs(levels, fields, block)
    return pl.pallas_call(
        top_kernel,
        grid=(cells // block,),
        in_specs=[smem] + specs,
        out_specs=[pl.BlockSpec((fields, block), lambda i: (0, i))] * 2,
        out_shape=[jax.ShapeDtypeStruct((fields, cells), jnp.float32)] * 2,
        compiler_params=stream_params,
        cost_estimate=pl.CostEstimate(
            flops=2 * fields * levels * cells,
            bytes_accessed=4 * fields * levels * cells,
            transcendentals=0,
        ),
        name="top_level",
    )(mixing, *[state] * len(specs))


def serve_kernel(per_owner, far_ref, asked_ref, own_ref, other_ref, out_ref, blocks_ref):
    far = far_ref[0]
    blocks_ref[far] = own_ref[...]
    blocks_ref[1 - far] = other_ref[...]

    def body(peer, carry):
        for shard in range(2):
            for slot in range(per_owner):
                spot = shard * per_owner + slot
                out_ref[peer, spot] = blocks_ref[shard, :, window(asked_ref[peer, spot])]
        return carry

    lax.fori_loop(0, out_ref.shape[0], body, 0)


def split_high(values):
    high = values.astype(jnp.bfloat16).astype(jnp.float32)
    return jnp.concatenate([high, values - high], axis=0)


GROUP = 8


def middle_kernel(
    far_ref,
    place_ref,
    spot_ref,
    mix_ref,
    arrived_ref,
    column_ref,
    ocean_weight_ref,
    atmos_weight_ref,
    mask_ref,
    base_ref,
    state_ref,
    forcing_ref,
    away_ref,
    home_ref,
    lanes_ref,
    value_ref,
    *share_refs,
):
    intersections, cells = column_ref.shape
    windows = cells // LANES
    fields = base_ref.shape[0]
    near, packed = away_ref.shape[:2]
    per_owner = packed * fields // (fields + 1)
    for ref in (value_ref, *share_refs):
        ref[...] = jnp.zeros(ref.shape, jnp.float32)
    corner = mix_ref[0, 0]
    group_tiles = GROUP * intersections
    steps = LANES // intersections
    for first in range(0, windows, steps):
        tall = jnp.concatenate(
            [
                column_ref[:, (first + step) * LANES : (first + step + 1) * LANES] & (LANES - 1)
                for step in range(steps)
            ],
            axis=0,
        )
        turned = tall.astype(jnp.float32).T.astype(jnp.bfloat16)
        for part in range(steps // GROUP):
            lanes_ref[first // GROUP + part, :, :group_tiles] = turned[
                :, part * group_tiles : (part + 1) * group_tiles
            ]
    column_ids = lax.broadcasted_iota(jnp.int32, (LANES, LANES), 1)
    column_ids = column_ids.astype(jnp.float32).astype(jnp.bfloat16)
    one, zero = jnp.bfloat16(1.0), jnp.bfloat16(0.0)
    field_ids = lax.broadcasted_iota(jnp.int32, (fields, LANES), 0)
    share_rows = lax.broadcasted_iota(jnp.int32, (2 * intersections, LANES), 0)
    first_half = share_rows % intersections < 2
    blank = jnp.zeros((2 * fields, LANES), jnp.float32)
    top = 2 * fields * intersections

    def body(group, carry):
        turned = lanes_ref[group]
        for inner in range(GROUP):
            step = group * GROUP + inner
            here = window(step)
            lanes = column_ref[:, here] & (LANES - 1)
            ocean_weight = ocean_weight_ref[:, here]
            total = jnp.zeros((fields, LANES), jnp.float32)
            weight = jnp.zeros((1, LANES), jnp.float32)
            where = []
            for k in range(intersections):
                where.append(place_ref[k, step])
                picked = jnp.take_along_axis(
                    arrived_ref[spot_ref[k, step]],
                    jnp.broadcast_to(lanes[k : k + 1], (fields, LANES)),
                    axis=1,
                    mode="promise_in_bounds",
                )
                total = total + ocean_weight[k : k + 1] * picked
                weight = weight + ocean_weight[k : k + 1]
            forcing = total / weight
            forcing_ref[:, here] = forcing
            mask = mask_ref[:, here]
            surface = jnp.where(
                mask == 1, base_ref[:, here] + corner * forcing, state_ref[:, here]
            )
            share = atmos_weight_ref[:, here] * mask.astype(jnp.float32)
            hot = []
            for k in range(intersections):
                tile = inner * intersections + k
                lane_of = jnp.broadcast_to(turned[:, tile : tile + 1], (LANES, LANES))
                hot.append(jnp.where(lane_of == column_ids, one, zero))
            hot = jnp.concatenate(
                [
                    jnp.concatenate([hot[0], hot[1]], axis=1),
                    jnp.concatenate([hot[2], hot[3]], axis=1),
                ],
                axis=0,
            )
            parts = [split_high(share[k : k + 1] * surface) for k in range(intersections)]
            share_parts = split_high(share)
            left = [parts[0], parts[1], blank, blank, jnp.where(first_half, share_parts, 0.0)]
            right = [blank, blank, parts[2], parts[3], jnp.where(first_half, 0.0, share_parts)]
            rows = jnp.concatenate(
                [jnp.concatenate(left, axis=0), jnp.concatenate(right, axis=0)], axis=1
            ).astype(jnp.bfloat16)
            spread = jnp.dot(rows, hot, preferred_element_type=jnp.float32)
            for k in range(intersections):
                place = where[k]
                side = slice((k % 2) * LANES, (k % 2 + 1) * LANES)
                at = 2 * fields * k
                value_ref[place] = (
                    spread[at : at + fields, side] + spread[at + fields : at + 2 * fields, side]
                )
                shared = (
                    spread[top + k : top + k + 1, side]
                    + spread[top + intersections + k : top + intersections + k + 1, side]
                )
                share_refs[k][lax.div(place, fields)] += jnp.where(
                    field_ids == lax.rem(place, fields), shared, 0.0
                )
        return carry

    lax.fori_loop(0, windows // GROUP, body, 0)
    far = far_ref[0]
    rows = per_owner // fields
    for ref, shard in ((away_ref, 1 - far), (home_ref, far)):
        values = value_ref[pl.ds(shard * near * per_owner, near * per_owner)]
        ref[:, :per_owner] = values.reshape(near, per_owner, fields, LANES)
        at = pl.ds(shard * near * rows, near * rows)
        shares = share_refs[0][at]
        for share_ref in share_refs[1:]:
            shares = shares + share_ref[at]
        ref[:, per_owner:] = shares.reshape(near, rows, fields, LANES)


def ocean_kernel(mix_ref, forcing_ref, mask_ref, *refs):
    x_refs, (out_ref, high_ref, low_ref) = refs[:-3], refs[-3:]
    levels, fields, block = out_ref.shape
    rows = levels * fields

    @pl.when(pl.program_id(0) == 0)
    def _():
        level = lax.broadcasted_iota(jnp.int32, (rows, levels), 0) // fields
        pick = (level == lax.broadcasted_iota(jnp.int32, (rows, levels), 1)).astype(jnp.float32)
        tall = jnp.dot(pick, mix_ref[...], precision=lax.Precision.HIGHEST)
        wide = lax.dot_general(
            tall, pick, (((1,), (1,)), ((), ())), precision=lax.Precision.HIGHEST
        )
        down = lax.broadcasted_iota(jnp.int32, (rows, rows), 0) % fields
        across = lax.broadcasted_iota(jnp.int32, (rows, rows), 1) % fields
        wide = jnp.where(down == across, wide, 0.0)
        high = wide.astype(jnp.bfloat16)
        high_ref[...] = high
        low_ref[...] = (wide - high.astype(jnp.float32)).astype(jnp.bfloat16)

    flat = jnp.concatenate(
        [ref[...].reshape(rows // len(x_refs), block) for ref in x_refs], axis=0
    )
    push = jnp.concatenate(
        [forcing_ref[...], jnp.zeros((rows - fields, block), jnp.float32)], axis=0
    )
    loaded = flat + push
    high = loaded.astype(jnp.bfloat16)
    low = (loaded - high.astype(jnp.float32)).astype(jnp.bfloat16)
    mixed = (
        jnp.dot(high_ref[...], high, preferred_element_type=jnp.float32)
        + jnp.dot(high_ref[...], low, preferred_element_type=jnp.float32)
        + jnp.dot(low_ref[...], high, preferred_element_type=jnp.float32)
    )
    out_ref[...] = jnp.where(mask_ref[...] == 1, mixed, flat).reshape(levels, fields, block)


def diffuse_ocean(state, mixing, forcing, mask):
    levels, fields, cells = state.shape
    block = min(1024, cells)
    rows = levels * fields
    specs = level_specs(levels, fields, block)
    return pl.pallas_call(
        ocean_kernel,
        grid=(cells // block,),
        in_specs=[
            pl.BlockSpec(mixing.shape, lambda i: (0, 0)),
            pl.BlockSpec((fields, block), lambda i: (0, i)),
            pl.BlockSpec((1, block), lambda i: (0, i)),
        ]
        + specs,
        out_specs=pl.BlockSpec((levels, fields, block), lambda i: (0, 0, i)),
        out_shape=jax.ShapeDtypeStruct(state.shape, jnp.float32),
        scratch_shapes=[pltpu.VMEM((rows, rows), jnp.bfloat16)] * 2,
        compiler_params=stream_params,
        cost_estimate=pl.CostEstimate(
            flops=6 * rows * rows * cells,
            bytes_accessed=8 * rows * cells,
            transcendentals=0,
        ),
        name="diffuse_ocean",
    )(mixing, forcing, mask, *[state] * len(specs))


def collect_kernel(per_owner, home, far_ref, asked_ref, back_ref, out_ref, *sums):
    near, packed, fields, _ = back_ref.shape
    columns = sums[0].shape[1]
    quarter = columns // fields
    chains = len(sums) // 2
    far = far_ref[0]
    first = (far if home else 1 - far) * per_owner
    for ref in sums:
        ref[...] = jnp.zeros(ref.shape, jnp.float32)

    def body(step, carry):
        for slot in range(per_owner):
            for chain in range(chains):
                peer = step * chains + chain
                at = window(asked_ref[peer, first + slot])
                tile, row = per_owner + slot // fields, slot % fields
                sums[chain][:, at] += back_ref[peer, slot]
                sums[chains + chain][:, at] += back_ref[peer, tile, row : row + 1]
        return carry

    lax.fori_loop(0, near // chains, body, 0)
    values, shares = sums[0][...], sums[chains][...]
    for chain in range(1, chains):
        values = values + sums[chain][...]
        shares = shares + sums[chains + chain][...]
    out_ref[:, :columns] = values
    for row in range(fields):
        out_ref[row : row + 1, columns:] = shares[:, row * quarter : (row + 1) * quarter]


def collect(asked, far, back, per_owner, columns, home):
    fields = back.shape[2]
    chains = 4
    return pl.pallas_call(
        functools.partial(collect_kernel, per_owner, home),
        in_specs=[smem, smem, vmem],
        out_specs=vmem,
        out_shape=jax.ShapeDtypeStruct((fields, columns + columns // fields), jnp.float32),
        scratch_shapes=[pltpu.VMEM((fields, columns), jnp.float32)] * chains
        + [pltpu.VMEM((1, columns), jnp.float32)] * chains,
        compiler_params=params,
        name="collect_home" if home else "collect_away",
    )(far, asked, back)


def final_kernel(keep_ref, other_ref, land_weight_ref, land_ref, out_ref):
    fields, columns = out_ref.shape
    quarter = columns // fields
    both = keep_ref[:, :columns] + other_ref[:, :columns]
    shares = keep_ref[:, columns:] + other_ref[:, columns:]
    land_weight = land_weight_ref[...]
    total = both + land_weight * land_ref[...]
    for row in range(fields):
        part = slice(row * quarter, (row + 1) * quarter)
        out_ref[:, part] = total[:, part] / (shares[row : row + 1] + land_weight[:, part])


def per_device(
    atmos_profiles,
    atmos_mixing,
    drag_factor,
    surface_before,
    downward_fluxes,
    land_weight,
    land_surface,
    ocean_state,
    ocean_mixing,
    sea_mask,
    exchange_slot,
    parent_column,
    ocean_weight,
    atmos_weight,
):
    near = lax.axis_size("near") * lax.axis_size("sub")
    devices = 2 * near
    fields, _, columns = atmos_profiles.shape
    intersections, cells = exchange_slot.shape
    capacity = 2 * intersections * cells // devices
    per_owner = capacity // LANES
    spots = 2 * per_owner
    mask = sea_mask.reshape(1, cells)
    state = ocean_state.transpose(1, 0, 2)
    far = lax.axis_index("far").astype(jnp.int32).reshape(1)

    def to_near(values):
        return lax.all_to_all(values, ("near", "sub"), split_axis=0, concat_axis=0, tiled=True)

    def to_far(values):
        return lax.ppermute(values, "far", ((0, 1), (1, 0)))

    forcing_rows, tendency = surface_rates(
        atmos_profiles, drag_factor, surface_before, downward_fluxes
    )
    exchange_slot, forcing_rows = lax.optimization_barrier((exchange_slot, forcing_rows))
    place, spot, wanted = pl.pallas_call(
        functools.partial(request_kernel, per_owner),
        in_specs=[vmem] * 2,
        out_specs=[vmem] * 3,
        out_shape=[
            jax.ShapeDtypeStruct((intersections, cells // LANES), jnp.int32),
            jax.ShapeDtypeStruct((intersections, cells // LANES), jnp.int32),
            jax.ShapeDtypeStruct((near, spots), jnp.int32),
        ],
        compiler_params=stream_params,
        name="requests",
    )(exchange_slot, parent_column)
    forcing_rows, wanted = lax.optimization_barrier((forcing_rows, wanted))
    asked = to_near(wanted)
    other_rows = to_far(forcing_rows)
    served = pl.pallas_call(
        functools.partial(serve_kernel, per_owner),
        in_specs=[smem, smem, vmem, vmem],
        out_specs=vmem,
        out_shape=jax.ShapeDtypeStruct((near, spots, fields, LANES), jnp.float32),
        scratch_shapes=[pltpu.VMEM((2, fields, columns), jnp.float32)],
        compiler_params=params,
        name="serve_windows",
    )(far, asked, forcing_rows, other_rows)
    arrived = to_near(served)
    base, first_level = top_level(state, ocean_mixing)
    atmos_updated = diffuse_atmos(atmos_profiles, atmos_mixing, tendency)
    arrived, atmos_updated, base = lax.optimization_barrier((arrived, atmos_updated, base))

    def whole(*shape):
        return pl.BlockSpec(shape, lambda i: (0,) * len(shape))

    rows = per_owner // fields
    sent = (near, per_owner + rows, fields, LANES)
    forcing, away, home = pl.pallas_call(
        middle_kernel,
        grid=(1,),
        in_specs=[
            smem,
            smem,
            smem,
            smem,
            whole(near * spots, fields, LANES),
            whole(intersections, cells),
            whole(intersections, cells),
            whole(intersections, cells),
            whole(1, cells),
            whole(fields, cells),
            whole(fields, cells),
        ],
        out_specs=[whole(fields, cells), whole(*sent), whole(*sent)],
        out_shape=[
            jax.ShapeDtypeStruct((fields, cells), jnp.float32),
            jax.ShapeDtypeStruct(sent, jnp.float32),
            jax.ShapeDtypeStruct(sent, jnp.float32),
        ],
        scratch_shapes=[
            pltpu.VMEM((cells // LANES // GROUP, LANES, LANES), jnp.bfloat16),
            pltpu.VMEM((near * spots, fields, LANES), jnp.float32),
        ]
        + [pltpu.VMEM((2 * near * rows, fields, LANES), jnp.float32)] * intersections,
        compiler_params=params,
        name="forcing_and_windows",
    )(
        far,
        place,
        spot,
        ocean_mixing,
        arrived.reshape(near * spots, fields, LANES),
        parent_column,
        ocean_weight,
        atmos_weight,
        mask,
        base,
        first_level,
    )
    back_away = to_near(away)
    back_home = to_near(home)
    sums_away = collect(asked, far, back_away, per_owner, columns, False)
    other_sums = to_far(sums_away)
    ocean_updated = diffuse_ocean(state, ocean_mixing, forcing, mask).transpose(1, 0, 2)
    back_home, ocean_updated = lax.optimization_barrier((back_home, ocean_updated))
    sums_home = collect(asked, far, back_home, per_owner, columns, True)
    surface_state = pl.pallas_call(
        final_kernel,
        in_specs=[vmem] * 4,
        out_specs=vmem,
        out_shape=jax.ShapeDtypeStruct((fields, columns), jnp.float32),
        compiler_params=params,
        name="surface_state",
    )(sums_home, other_sums, land_weight.reshape(1, columns), land_surface)
    return (atmos_updated, ocean_updated, surface_state)


def solution(mesh):
    comp, sub = mesh.devices.shape
    halves = jax.sharding.Mesh(mesh.devices.reshape(2, comp // 2, sub), AXES)
    split = P(None, AXES)
    return jax.shard_map(
        per_device,
        mesh=halves,
        in_specs=(
            P(None, None, AXES),
            P(),
            P(AXES),
            split,
            split,
            P(AXES),
            split,
            P(None, None, AXES),
            P(),
            P(AXES),
            split,
            split,
            split,
            split,
        ),
        out_specs=(P(None, None, AXES), P(None, None, AXES), split),
        check_vma=False,
    )
```

```python
import functools

import jax
import jax.numpy as jnp
from jax import lax
from jax.experimental import pallas as pl
from jax.experimental.pallas import tpu as pltpu
from jax.sharding import PartitionSpec as P

couple_rate = 0.5
LANES = 128
params = pltpu.CompilerParams(vmem_limit_bytes=24 * 1024 * 1024)
stream_params = pltpu.CompilerParams(vmem_limit_bytes=52 * 1024 * 1024)
first_params = pltpu.CompilerParams(vmem_limit_bytes=56 * 1024 * 1024)
vmem = pl.BlockSpec(memory_space=pltpu.VMEM)
smem = pl.BlockSpec(memory_space=pltpu.SMEM)
AXES = ("far", "near", "sub")


def window(index):
    return pl.ds(pl.multiple_of(index * LANES, LANES), LANES)


def make_requests(per_owner, slot_ref, column_ref, place_ref, spot_ref, wanted_ref):
    intersections, cells = slot_ref.shape
    near, spots = wanted_ref.shape
    windows = cells // LANES
    lane = lax.broadcasted_iota(jnp.int32, (intersections, windows), 1)

    def heads(ref):
        found = jnp.zeros((intersections, windows), jnp.int32)
        for step in range(windows):
            head = ref[:, step * LANES : step * LANES + 1]
            found = jnp.where(lane == step, head, found)
        return found // LANES

    place = heads(slot_ref)
    column_window = heads(column_ref)
    owner = place // per_owner
    peer = owner % near
    spot = owner // near * per_owner + place % per_owner
    place_ref[...] = place
    spot_ref[...] = peer * spots + spot
    peer_ids = lax.broadcasted_iota(jnp.int32, (near, windows), 0)
    spot_ids = lax.broadcasted_iota(jnp.int32, (spots, windows), 0)
    wanted = jnp.zeros((near, spots), jnp.float32)
    for k in range(intersections):
        row = slice(k, k + 1)
        peer_hot = jnp.where(peer_ids == peer[row], 1.0, 0.0)
        spot_hot = jnp.where(
            spot_ids == spot[row], column_window[row].astype(jnp.float32), 0.0
        )
        wanted = wanted + lax.dot_general(
            peer_hot.astype(jnp.bfloat16),
            spot_hot.astype(jnp.bfloat16),
            (((1,), (1,)), ((), ())),
            preferred_element_type=jnp.float32,
        )
    wanted_ref[...] = wanted.astype(jnp.int32)


def start_kernel(
    last,
    per_owner,
    slot_ref,
    column_ref,
    x_ref,
    drag_ref,
    before_ref,
    down_ref,
    place_ref,
    spot_ref,
    wanted_ref,
    forcing_ref,
    tend_ref,
):
    @pl.when(pl.program_id(0) == 0)
    def _():
        make_requests(per_owner, slot_ref, column_ref, place_ref, spot_ref, wanted_ref)

    def row(ref, index):
        return ref[index : index + 1, :]

    bottom = [x_ref[member].astype(jnp.float32)[last : last + 1, :] for member in range(4)]
    east = bottom[2] - row(before_ref, 2)
    north = bottom[3] - row(before_ref, 3)
    transfer = drag_ref[...] * jnp.sqrt(1.0 + east * east + north * north)
    sensible = transfer * (row(before_ref, 0) - bottom[0])
    latent = transfer * (row(before_ref, 1) - bottom[1])
    east_stress = couple_rate * (transfer * east)
    north_stress = couple_rate * (transfer * north)
    forcing_ref[0:1, :] = couple_rate * (
        row(down_ref, 0) + row(down_ref, 1) - sensible - latent
    )
    forcing_ref[1:2, :] = couple_rate * (latent - row(down_ref, 2) - row(down_ref, 3))
    forcing_ref[2:3, :] = east_stress
    forcing_ref[3:4, :] = north_stress
    tend_ref[0:1, :] = couple_rate * sensible
    tend_ref[1:2, :] = couple_rate * latent
    tend_ref[2:3, :] = -east_stress
    tend_ref[3:4, :] = -north_stress


def start(near, per_owner, slots, parents, profiles, drag_factor, surface_before, downward):
    fields, levels, columns = profiles.shape
    intersections, cells = slots.shape
    block = min(4096, columns)
    tall = 16
    at = (levels - 1) // tall
    rows = pl.BlockSpec((fields, block), lambda i: (0, i))
    tiles = (intersections, cells // LANES)
    asked = (near, 2 * per_owner)

    def whole(shape):
        return pl.BlockSpec(shape, lambda i: (0, 0))

    return pl.pallas_call(
        functools.partial(start_kernel, levels - 1 - at * tall, per_owner),
        grid=(columns // block,),
        in_specs=[
            whole(slots.shape),
            whole(slots.shape),
            pl.BlockSpec((fields, tall, block), lambda i: (0, at, i)),
            pl.BlockSpec((1, block), lambda i: (0, i)),
            rows,
            rows,
        ],
        out_specs=[whole(tiles), whole(tiles), whole(asked), rows, rows],
        out_shape=[
            jax.ShapeDtypeStruct(tiles, jnp.int32),
            jax.ShapeDtypeStruct(tiles, jnp.int32),
            jax.ShapeDtypeStruct(asked, jnp.int32),
            jax.ShapeDtypeStruct((fields, columns), jnp.float32),
            jax.ShapeDtypeStruct((fields, columns), jnp.float32),
        ],
        compiler_params=first_params,
        name="requests_and_rates",
    )(slots, parents, profiles, drag_factor.reshape(1, columns), surface_before, downward)


def atmos_kernel(mix_ref, tend_ref, *refs):
    mix = mix_ref[...]
    lowest = mix[:, mix.shape[1] - 1 :].astype(jnp.float32)
    out_ref = refs[-1]
    for member, x_ref in enumerate(refs[:-1]):
        mixed = jnp.dot(mix, x_ref[0], preferred_element_type=jnp.float32)
        out_ref[member] = (mixed + lowest * tend_ref[member : member + 1, :]).astype(jnp.bfloat16)


def diffuse_atmos(profiles, mixing, tendency):
    fields, levels, columns = profiles.shape
    block = min(2048, columns)

    def field(member):
        return pl.BlockSpec((1, levels, block), lambda i: (member, 0, i))

    return pl.pallas_call(
        atmos_kernel,
        grid=(columns // block,),
        in_specs=[
            pl.BlockSpec((levels, levels), lambda i: (0, 0)),
            pl.BlockSpec((fields, block), lambda i: (0, i)),
        ]
        + [field(member) for member in range(fields)],
        out_specs=pl.BlockSpec((fields, levels, block), lambda i: (0, 0, i)),
        out_shape=jax.ShapeDtypeStruct(profiles.shape, jnp.bfloat16),
        compiler_params=stream_params,
        cost_estimate=pl.CostEstimate(
            flops=2 * fields * levels * levels * columns,
            bytes_accessed=4 * fields * levels * columns,
            transcendentals=0,
        ),
        name="diffuse_atmos",
    )(mixing, tendency, *[profiles] * fields)


def level_specs(levels, fields, block):
    count = 4 if levels % 4 == 0 else 1

    def part(number):
        return pl.BlockSpec((levels // count, fields, block), lambda i: (number, 0, i))

    return [part(number) for number in range(count)]


def top_kernel(mix_ref, *refs):
    state_refs, base_ref, first_ref = refs[:-2], refs[-2], refs[-1]
    total = None
    level = 0
    for ref in state_refs:
        for inner in range(ref.shape[0]):
            term = mix_ref[0, level] * ref[inner]
            total = term if total is None else total + term
            level += 1
    base_ref[...] = total
    first_ref[...] = state_refs[0][0]


def top_level(state, mixing):
    levels, fields, cells = state.shape
    block = min(2048, cells)
    specs = level_specs(levels, fields, block)
    return pl.pallas_call(
        top_kernel,
        grid=(cells // block,),
        in_specs=[smem] + specs,
        out_specs=[pl.BlockSpec((fields, block), lambda i: (0, i))] * 2,
        out_shape=[jax.ShapeDtypeStruct((fields, cells), jnp.float32)] * 2,
        compiler_params=stream_params,
        cost_estimate=pl.CostEstimate(
            flops=2 * fields * levels * cells,
            bytes_accessed=4 * fields * levels * cells,
            transcendentals=0,
        ),
        name="top_level",
    )(mixing, *[state] * len(specs))


def serve_kernel(per_owner, far_ref, asked_ref, own_ref, other_ref, out_ref, blocks_ref):
    far = far_ref[0]
    blocks_ref[far] = own_ref[...]
    blocks_ref[1 - far] = other_ref[...]

    def body(peer, carry):
        for shard in range(2):
            for slot in range(per_owner):
                spot = shard * per_owner + slot
                out_ref[peer, spot] = blocks_ref[shard, :, window(asked_ref[peer, spot])]
        return carry

    lax.fori_loop(0, out_ref.shape[0], body, 0)


def split_high(values):
    high = values.astype(jnp.bfloat16).astype(jnp.float32)
    return jnp.concatenate([high, values - high], axis=0)


GROUP = 8


def middle_kernel(
    far_ref,
    place_ref,
    spot_ref,
    mix_ref,
    arrived_ref,
    column_ref,
    ocean_weight_ref,
    atmos_weight_ref,
    mask_ref,
    base_ref,
    state_ref,
    forcing_ref,
    away_ref,
    home_ref,
    lanes_ref,
    value_ref,
    *share_refs,
):
    intersections, cells = column_ref.shape
    windows = cells // LANES
    fields = base_ref.shape[0]
    near, packed = away_ref.shape[:2]
    per_owner = packed * fields // (fields + 1)
    for ref in (value_ref, *share_refs):
        ref[...] = jnp.zeros(ref.shape, jnp.float32)
    corner = mix_ref[0, 0]
    group_tiles = GROUP * intersections
    steps = LANES // intersections
    for first in range(0, windows, steps):
        tall = jnp.concatenate(
            [
                column_ref[:, (first + step) * LANES : (first + step + 1) * LANES] & (LANES - 1)
                for step in range(steps)
            ],
            axis=0,
        )
        turned = tall.astype(jnp.float32).T.astype(jnp.bfloat16)
        for part in range(steps // GROUP):
            lanes_ref[first // GROUP + part, :, :group_tiles] = turned[
                :, part * group_tiles : (part + 1) * group_tiles
            ]
    column_ids = lax.broadcasted_iota(jnp.int32, (LANES, LANES), 1)
    column_ids = column_ids.astype(jnp.float32).astype(jnp.bfloat16)
    one, zero = jnp.bfloat16(1.0), jnp.bfloat16(0.0)
    field_ids = lax.broadcasted_iota(jnp.int32, (fields, LANES), 0)
    share_rows = lax.broadcasted_iota(jnp.int32, (2 * intersections, LANES), 0)
    first_half = share_rows % intersections < 2
    blank = jnp.zeros((2 * fields, LANES), jnp.float32)
    top = 2 * fields * intersections

    def body(group, carry):
        turned = lanes_ref[group]
        for inner in range(GROUP):
            step = group * GROUP + inner
            here = window(step)
            lanes = column_ref[:, here] & (LANES - 1)
            ocean_weight = ocean_weight_ref[:, here]
            total = jnp.zeros((fields, LANES), jnp.float32)
            weight = jnp.zeros((1, LANES), jnp.float32)
            where = []
            for k in range(intersections):
                where.append(place_ref[k, step])
                picked = jnp.take_along_axis(
                    arrived_ref[spot_ref[k, step]],
                    jnp.broadcast_to(lanes[k : k + 1], (fields, LANES)),
                    axis=1,
                    mode="promise_in_bounds",
                )
                total = total + ocean_weight[k : k + 1] * picked
                weight = weight + ocean_weight[k : k + 1]
            forcing = total / weight
            forcing_ref[:, here] = forcing
            mask = mask_ref[:, here]
            surface = jnp.where(
                mask == 1, base_ref[:, here] + corner * forcing, state_ref[:, here]
            )
            share = atmos_weight_ref[:, here] * mask.astype(jnp.float32)
            hot = []
            for k in range(intersections):
                tile = inner * intersections + k
                lane_of = jnp.broadcast_to(turned[:, tile : tile + 1], (LANES, LANES))
                hot.append(jnp.where(lane_of == column_ids, one, zero))
            hot = jnp.concatenate(
                [
                    jnp.concatenate([hot[0], hot[1]], axis=1),
                    jnp.concatenate([hot[2], hot[3]], axis=1),
                ],
                axis=0,
            )
            parts = [split_high(share[k : k + 1] * surface) for k in range(intersections)]
            share_parts = split_high(share)
            left = [parts[0], parts[1], blank, blank, jnp.where(first_half, share_parts, 0.0)]
            right = [blank, blank, parts[2], parts[3], jnp.where(first_half, 0.0, share_parts)]
            rows = jnp.concatenate(
                [jnp.concatenate(left, axis=0), jnp.concatenate(right, axis=0)], axis=1
            ).astype(jnp.bfloat16)
            spread = jnp.dot(rows, hot, preferred_element_type=jnp.float32)
            for k in range(intersections):
                place = where[k]
                side = slice((k % 2) * LANES, (k % 2 + 1) * LANES)
                at = 2 * fields * k
                value_ref[place] = (
                    spread[at : at + fields, side] + spread[at + fields : at + 2 * fields, side]
                )
                shared = (
                    spread[top + k : top + k + 1, side]
                    + spread[top + intersections + k : top + intersections + k + 1, side]
                )
                share_refs[k][lax.div(place, fields)] += jnp.where(
                    field_ids == lax.rem(place, fields), shared, 0.0
                )
        return carry

    lax.fori_loop(0, windows // GROUP, body, 0)
    far = far_ref[0]
    rows = per_owner // fields
    for ref, shard in ((away_ref, 1 - far), (home_ref, far)):
        values = value_ref[pl.ds(shard * near * per_owner, near * per_owner)]
        ref[:, :per_owner] = values.reshape(near, per_owner, fields, LANES)
        at = pl.ds(shard * near * rows, near * rows)
        shares = share_refs[0][at]
        for share_ref in share_refs[1:]:
            shares = shares + share_ref[at]
        ref[:, per_owner:] = shares.reshape(near, rows, fields, LANES)


def ocean_kernel(mix_ref, forcing_ref, mask_ref, *refs):
    x_refs, (out_ref, high_ref, low_ref) = refs[:-3], refs[-3:]
    levels, fields, block = out_ref.shape
    rows = levels * fields

    @pl.when(pl.program_id(0) == 0)
    def _():
        level = lax.broadcasted_iota(jnp.int32, (rows, levels), 0) // fields
        pick = (level == lax.broadcasted_iota(jnp.int32, (rows, levels), 1)).astype(jnp.float32)
        tall = jnp.dot(pick, mix_ref[...], precision=lax.Precision.HIGHEST)
        wide = lax.dot_general(
            tall, pick, (((1,), (1,)), ((), ())), precision=lax.Precision.HIGHEST
        )
        down = lax.broadcasted_iota(jnp.int32, (rows, rows), 0) % fields
        across = lax.broadcasted_iota(jnp.int32, (rows, rows), 1) % fields
        wide = jnp.where(down == across, wide, 0.0)
        high = wide.astype(jnp.bfloat16)
        high_ref[...] = high
        low_ref[...] = (wide - high.astype(jnp.float32)).astype(jnp.bfloat16)

    flat = jnp.concatenate(
        [ref[...].reshape(rows // len(x_refs), block) for ref in x_refs], axis=0
    )
    push = jnp.concatenate(
        [forcing_ref[...], jnp.zeros((rows - fields, block), jnp.float32)], axis=0
    )
    loaded = flat + push
    high = loaded.astype(jnp.bfloat16)
    low = (loaded - high.astype(jnp.float32)).astype(jnp.bfloat16)
    mixed = (
        jnp.dot(high_ref[...], high, preferred_element_type=jnp.float32)
        + jnp.dot(high_ref[...], low, preferred_element_type=jnp.float32)
        + jnp.dot(low_ref[...], high, preferred_element_type=jnp.float32)
    )
    out_ref[...] = jnp.where(mask_ref[...] == 1, mixed, flat).reshape(levels, fields, block)


def diffuse_ocean(state, mixing, forcing, mask):
    levels, fields, cells = state.shape
    block = min(1024, cells)
    rows = levels * fields
    specs = level_specs(levels, fields, block)
    return pl.pallas_call(
        ocean_kernel,
        grid=(cells // block,),
        in_specs=[
            pl.BlockSpec(mixing.shape, lambda i: (0, 0)),
            pl.BlockSpec((fields, block), lambda i: (0, i)),
            pl.BlockSpec((1, block), lambda i: (0, i)),
        ]
        + specs,
        out_specs=pl.BlockSpec((levels, fields, block), lambda i: (0, 0, i)),
        out_shape=jax.ShapeDtypeStruct(state.shape, jnp.float32),
        scratch_shapes=[pltpu.VMEM((rows, rows), jnp.bfloat16)] * 2,
        compiler_params=stream_params,
        cost_estimate=pl.CostEstimate(
            flops=6 * rows * rows * cells,
            bytes_accessed=8 * rows * cells,
            transcendentals=0,
        ),
        name="diffuse_ocean",
    )(mixing, forcing, mask, *[state] * len(specs))


def collect_kernel(per_owner, home, far_ref, asked_ref, back_ref, out_ref, *sums):
    near, packed, fields, _ = back_ref.shape
    columns = sums[0].shape[1]
    quarter = columns // fields
    chains = len(sums) // 2
    far = far_ref[0]
    first = (far if home else 1 - far) * per_owner
    for ref in sums:
        ref[...] = jnp.zeros(ref.shape, jnp.float32)

    def body(step, carry):
        for slot in range(per_owner):
            for chain in range(chains):
                peer = step * chains + chain
                at = window(asked_ref[peer, first + slot])
                tile, row = per_owner + slot // fields, slot % fields
                sums[chain][:, at] += back_ref[peer, slot]
                sums[chains + chain][:, at] += back_ref[peer, tile, row : row + 1]
        return carry

    lax.fori_loop(0, near // chains, body, 0)
    values, shares = sums[0][...], sums[chains][...]
    for chain in range(1, chains):
        values = values + sums[chain][...]
        shares = shares + sums[chains + chain][...]
    out_ref[:, :columns] = values
    for row in range(fields):
        out_ref[row : row + 1, columns:] = shares[:, row * quarter : (row + 1) * quarter]


def collect(asked, far, back, per_owner, columns, home):
    fields = back.shape[2]
    chains = 4
    return pl.pallas_call(
        functools.partial(collect_kernel, per_owner, home),
        in_specs=[smem, smem, vmem],
        out_specs=vmem,
        out_shape=jax.ShapeDtypeStruct((fields, columns + columns // fields), jnp.float32),
        scratch_shapes=[pltpu.VMEM((fields, columns), jnp.float32)] * chains
        + [pltpu.VMEM((1, columns), jnp.float32)] * chains,
        compiler_params=params,
        name="collect_home" if home else "collect_away",
    )(far, asked, back)


def final_kernel(keep_ref, other_ref, land_weight_ref, land_ref, out_ref):
    fields, columns = out_ref.shape
    quarter = columns // fields
    both = keep_ref[:, :columns] + other_ref[:, :columns]
    shares = keep_ref[:, columns:] + other_ref[:, columns:]
    land_weight = land_weight_ref[...]
    total = both + land_weight * land_ref[...]
    for row in range(fields):
        part = slice(row * quarter, (row + 1) * quarter)
        out_ref[:, part] = total[:, part] / (shares[row : row + 1] + land_weight[:, part])


def per_device(
    atmos_profiles,
    atmos_mixing,
    drag_factor,
    surface_before,
    downward_fluxes,
    land_weight,
    land_surface,
    ocean_state,
    ocean_mixing,
    sea_mask,
    exchange_slot,
    parent_column,
    ocean_weight,
    atmos_weight,
):
    near = lax.axis_size("near") * lax.axis_size("sub")
    devices = 2 * near
    fields, _, columns = atmos_profiles.shape
    intersections, cells = exchange_slot.shape
    capacity = 2 * intersections * cells // devices
    per_owner = capacity // LANES
    spots = 2 * per_owner
    mask = sea_mask.reshape(1, cells)
    state = ocean_state.transpose(1, 0, 2)
    far = lax.axis_index("far").astype(jnp.int32).reshape(1)

    def to_near(values):
        return lax.all_to_all(values, ("near", "sub"), split_axis=0, concat_axis=0, tiled=True)

    def to_far(values):
        return lax.ppermute(values, "far", ((0, 1), (1, 0)))

    place, spot, wanted, forcing_rows, tendency = start(
        near,
        per_owner,
        exchange_slot,
        parent_column,
        atmos_profiles,
        drag_factor,
        surface_before,
        downward_fluxes,
    )
    asked = to_near(wanted)
    other_rows = to_far(forcing_rows)
    served = pl.pallas_call(
        functools.partial(serve_kernel, per_owner),
        in_specs=[smem, smem, vmem, vmem],
        out_specs=vmem,
        out_shape=jax.ShapeDtypeStruct((near, spots, fields, LANES), jnp.float32),
        scratch_shapes=[pltpu.VMEM((2, fields, columns), jnp.float32)],
        compiler_params=params,
        name="serve_windows",
    )(far, asked, forcing_rows, other_rows)
    arrived = to_near(served)
    base, first_level = top_level(state, ocean_mixing)
    arrived, base = lax.optimization_barrier((arrived, base))

    rows = per_owner // fields
    sent = (near, per_owner + rows, fields, LANES)
    forcing, away, home = pl.pallas_call(
        middle_kernel,
        in_specs=[smem] * 4 + [vmem] * 7,
        out_specs=[vmem] * 3,
        out_shape=[
            jax.ShapeDtypeStruct((fields, cells), jnp.float32),
            jax.ShapeDtypeStruct(sent, jnp.float32),
            jax.ShapeDtypeStruct(sent, jnp.float32),
        ],
        scratch_shapes=[
            pltpu.VMEM((cells // LANES // GROUP, LANES, LANES), jnp.bfloat16),
            pltpu.VMEM((near * spots, fields, LANES), jnp.float32),
        ]
        + [pltpu.VMEM((2 * near * rows, fields, LANES), jnp.float32)] * intersections,
        compiler_params=params,
        name="forcing_and_windows",
    )(
        far,
        place,
        spot,
        ocean_mixing,
        arrived.reshape(near * spots, fields, LANES),
        parent_column,
        ocean_weight,
        atmos_weight,
        mask,
        base,
        first_level,
    )
    tendency, forcing = lax.optimization_barrier((tendency, forcing))
    atmos_updated = diffuse_atmos(atmos_profiles, atmos_mixing, tendency)
    back_away, atmos_updated, home = lax.optimization_barrier(
        (to_near(away), atmos_updated, home)
    )
    back_home = to_near(home)
    sums_away = collect(asked, far, back_away, per_owner, columns, False)
    other_sums = to_far(sums_away)
    ocean_updated = diffuse_ocean(state, ocean_mixing, forcing, mask).transpose(1, 0, 2)
    back_home, ocean_updated = lax.optimization_barrier((back_home, ocean_updated))
    sums_home = collect(asked, far, back_home, per_owner, columns, True)
    surface_state = pl.pallas_call(
        final_kernel,
        in_specs=[vmem] * 4,
        out_specs=vmem,
        out_shape=jax.ShapeDtypeStruct((fields, columns), jnp.float32),
        compiler_params=params,
        name="surface_state",
    )(sums_home, other_sums, land_weight.reshape(1, columns), land_surface)
    return (atmos_updated, ocean_updated, surface_state)


def solution(mesh):
    comp, sub = mesh.devices.shape
    halves = jax.sharding.Mesh(mesh.devices.reshape(2, comp // 2, sub), AXES)
    split = P(None, AXES)
    return jax.shard_map(
        per_device,
        mesh=halves,
        in_specs=(
            P(None, None, AXES),
            P(),
            P(AXES),
            split,
            split,
            P(AXES),
            split,
            P(None, None, AXES),
            P(),
            P(AXES),
            split,
            split,
            split,
            split,
        ),
        out_specs=(P(None, None, AXES), P(None, None, AXES), split),
        check_vma=False,
    )
```

```python
import functools

import jax
import jax.numpy as jnp
from jax import lax
from jax.experimental import pallas as pl
from jax.experimental.pallas import tpu as pltpu
from jax.sharding import PartitionSpec as P

couple_rate = 0.5
LANES = 128
params = pltpu.CompilerParams(vmem_limit_bytes=24 * 1024 * 1024)
stream_params = pltpu.CompilerParams(vmem_limit_bytes=52 * 1024 * 1024)
first_params = pltpu.CompilerParams(vmem_limit_bytes=56 * 1024 * 1024)
vmem = pl.BlockSpec(memory_space=pltpu.VMEM)
smem = pl.BlockSpec(memory_space=pltpu.SMEM)
AXES = ("far", "near", "sub")


def window(index):
    return pl.ds(pl.multiple_of(index * LANES, LANES), LANES)


def make_requests(per_owner, slot_ref, column_ref, place_ref, spot_ref, wanted_ref):
    intersections, cells = slot_ref.shape
    near, spots = wanted_ref.shape
    windows = cells // LANES
    lane = lax.broadcasted_iota(jnp.int32, (intersections, windows), 1)

    def heads(ref):
        found = jnp.zeros((intersections, windows), jnp.int32)
        for step in range(windows):
            head = ref[:, step * LANES : step * LANES + 1]
            found = jnp.where(lane == step, head, found)
        return found // LANES

    place = heads(slot_ref)
    column_window = heads(column_ref)
    owner = place // per_owner
    peer = owner % near
    spot = owner // near * per_owner + place % per_owner
    place_ref[...] = place
    spot_ref[...] = peer * spots + spot
    peer_ids = lax.broadcasted_iota(jnp.int32, (near, windows), 0)
    spot_ids = lax.broadcasted_iota(jnp.int32, (spots, windows), 0)
    wanted = jnp.zeros((near, spots), jnp.float32)
    for k in range(intersections):
        row = slice(k, k + 1)
        peer_hot = jnp.where(peer_ids == peer[row], 1.0, 0.0)
        spot_hot = jnp.where(
            spot_ids == spot[row], column_window[row].astype(jnp.float32), 0.0
        )
        wanted = wanted + lax.dot_general(
            peer_hot.astype(jnp.bfloat16),
            spot_hot.astype(jnp.bfloat16),
            (((1,), (1,)), ((), ())),
            preferred_element_type=jnp.float32,
        )
    wanted_ref[...] = wanted.astype(jnp.int32)


def start_kernel(
    last,
    per_owner,
    slot_ref,
    column_ref,
    x_ref,
    drag_ref,
    before_ref,
    down_ref,
    place_ref,
    spot_ref,
    wanted_ref,
    forcing_ref,
    tend_ref,
):
    @pl.when(pl.program_id(0) == 0)
    def _():
        make_requests(per_owner, slot_ref, column_ref, place_ref, spot_ref, wanted_ref)

    def row(ref, index):
        return ref[index : index + 1, :]

    bottom = [x_ref[member].astype(jnp.float32)[last : last + 1, :] for member in range(4)]
    east = bottom[2] - row(before_ref, 2)
    north = bottom[3] - row(before_ref, 3)
    transfer = drag_ref[...] * jnp.sqrt(1.0 + east * east + north * north)
    sensible = transfer * (row(before_ref, 0) - bottom[0])
    latent = transfer * (row(before_ref, 1) - bottom[1])
    east_stress = couple_rate * (transfer * east)
    north_stress = couple_rate * (transfer * north)
    forcing_ref[0:1, :] = couple_rate * (
        row(down_ref, 0) + row(down_ref, 1) - sensible - latent
    )
    forcing_ref[1:2, :] = couple_rate * (latent - row(down_ref, 2) - row(down_ref, 3))
    forcing_ref[2:3, :] = east_stress
    forcing_ref[3:4, :] = north_stress
    tend_ref[0:1, :] = couple_rate * sensible
    tend_ref[1:2, :] = couple_rate * latent
    tend_ref[2:3, :] = -east_stress
    tend_ref[3:4, :] = -north_stress


def start(near, per_owner, slots, parents, profiles, drag_factor, surface_before, downward):
    fields, levels, columns = profiles.shape
    intersections, cells = slots.shape
    block = min(4096, columns)
    tall = 16
    at = (levels - 1) // tall
    rows = pl.BlockSpec((fields, block), lambda i: (0, i))
    tiles = (intersections, cells // LANES)
    asked = (near, 2 * per_owner)

    def whole(shape):
        return pl.BlockSpec(shape, lambda i: (0, 0))

    return pl.pallas_call(
        functools.partial(start_kernel, levels - 1 - at * tall, per_owner),
        grid=(columns // block,),
        in_specs=[
            whole(slots.shape),
            whole(slots.shape),
            pl.BlockSpec((fields, tall, block), lambda i: (0, at, i)),
            pl.BlockSpec((1, block), lambda i: (0, i)),
            rows,
            rows,
        ],
        out_specs=[whole(tiles), whole(tiles), whole(asked), rows, rows],
        out_shape=[
            jax.ShapeDtypeStruct(tiles, jnp.int32),
            jax.ShapeDtypeStruct(tiles, jnp.int32),
            jax.ShapeDtypeStruct(asked, jnp.int32),
            jax.ShapeDtypeStruct((fields, columns), jnp.float32),
            jax.ShapeDtypeStruct((fields, columns), jnp.float32),
        ],
        compiler_params=first_params,
        name="requests_and_rates",
    )(slots, parents, profiles, drag_factor.reshape(1, columns), surface_before, downward)


def atmos_kernel(mix_ref, tend_ref, *refs):
    mix = mix_ref[...]
    lowest = mix[:, mix.shape[1] - 1 :].astype(jnp.float32)
    out_ref = refs[-1]
    for member, x_ref in enumerate(refs[:-1]):
        mixed = jnp.dot(mix, x_ref[0], preferred_element_type=jnp.float32)
        out_ref[member] = (mixed + lowest * tend_ref[member : member + 1, :]).astype(jnp.bfloat16)


def diffuse_atmos(profiles, mixing, tendency):
    fields, levels, columns = profiles.shape
    block = min(2048, columns)

    def field(member):
        return pl.BlockSpec((1, levels, block), lambda i: (member, 0, i))

    return pl.pallas_call(
        atmos_kernel,
        grid=(columns // block,),
        in_specs=[
            pl.BlockSpec((levels, levels), lambda i: (0, 0)),
            pl.BlockSpec((fields, block), lambda i: (0, i)),
        ]
        + [field(member) for member in range(fields)],
        out_specs=pl.BlockSpec((fields, levels, block), lambda i: (0, 0, i)),
        out_shape=jax.ShapeDtypeStruct(profiles.shape, jnp.bfloat16),
        compiler_params=stream_params,
        cost_estimate=pl.CostEstimate(
            flops=2 * fields * levels * levels * columns,
            bytes_accessed=4 * fields * levels * columns,
            transcendentals=0,
        ),
        name="diffuse_atmos",
    )(mixing, tendency, *[profiles] * fields)


def level_specs(levels, fields, block):
    count = 4 if levels % 4 == 0 else 1

    def part(number):
        return pl.BlockSpec((levels // count, fields, block), lambda i: (number, 0, i))

    return [part(number) for number in range(count)]


def top_kernel(mix_ref, *refs):
    state_refs, base_ref, first_ref = refs[:-2], refs[-2], refs[-1]
    total = None
    level = 0
    for ref in state_refs:
        for inner in range(ref.shape[0]):
            term = mix_ref[0, level] * ref[inner]
            total = term if total is None else total + term
            level += 1
    base_ref[...] = total
    first_ref[...] = state_refs[0][0]


def top_level(state, mixing):
    levels, fields, cells = state.shape
    block = min(2048, cells)
    specs = level_specs(levels, fields, block)
    return pl.pallas_call(
        top_kernel,
        grid=(cells // block,),
        in_specs=[smem] + specs,
        out_specs=[pl.BlockSpec((fields, block), lambda i: (0, i))] * 2,
        out_shape=[jax.ShapeDtypeStruct((fields, cells), jnp.float32)] * 2,
        compiler_params=stream_params,
        cost_estimate=pl.CostEstimate(
            flops=2 * fields * levels * cells,
            bytes_accessed=4 * fields * levels * cells,
            transcendentals=0,
        ),
        name="top_level",
    )(mixing, *[state] * len(specs))


def serve_kernel(
    per_owner, far_ref, asked_ref, own_ref, other_ref, out_ref, blocks_ref, arrived_sem
):
    copies = [
        pltpu.make_async_copy(ref, blocks_ref.at[index], arrived_sem.at[index])
        for index, ref in enumerate((own_ref, other_ref))
    ]
    for copy in copies:
        copy.start()
    for copy in copies:
        copy.wait()
    far = far_ref[0]

    def body(peer, carry):
        for shard in range(2):
            for slot in range(per_owner):
                spot = shard * per_owner + slot
                out_ref[peer, spot] = blocks_ref[
                    shard ^ far, :, window(asked_ref[peer, spot])
                ]
        return carry

    lax.fori_loop(0, out_ref.shape[0], body, 0)


def split_high(values):
    high = values.astype(jnp.bfloat16).astype(jnp.float32)
    return jnp.concatenate([high, values - high], axis=0)


GROUP = 8


def hot_kernel(
    place_ref,
    column_ref,
    atmos_weight_ref,
    mask_ref,
    hot_ref,
    share_ref,
    lanes_ref,
    *sums,
):
    intersections, cells = column_ref.shape
    windows = cells // LANES
    fields = share_ref.shape[1]
    for ref in sums:
        ref[...] = jnp.zeros(ref.shape, jnp.float32)
    group_tiles = GROUP * intersections
    steps = LANES // intersections
    for first in range(0, windows, steps):
        tall = jnp.concatenate(
            [
                column_ref[:, (first + step) * LANES : (first + step + 1) * LANES] & (LANES - 1)
                for step in range(steps)
            ],
            axis=0,
        )
        turned = tall.astype(jnp.float32).T.astype(jnp.bfloat16)
        for part in range(steps // GROUP):
            lanes_ref[first // GROUP + part, :, :group_tiles] = turned[
                :, part * group_tiles : (part + 1) * group_tiles
            ]
    column_ids = lax.broadcasted_iota(jnp.int32, (LANES, LANES), 1)
    column_ids = column_ids.astype(jnp.float32).astype(jnp.bfloat16)
    one, zero = jnp.bfloat16(1.0), jnp.bfloat16(0.0)
    field_ids = lax.broadcasted_iota(jnp.int32, (fields, LANES), 0)
    share_rows = lax.broadcasted_iota(jnp.int32, (2 * intersections, LANES), 0)
    first_half = share_rows % intersections < 2

    def body(group, carry):
        turned = lanes_ref[group]
        for inner in range(GROUP):
            step = group * GROUP + inner
            here = window(step)
            share = atmos_weight_ref[:, here] * mask_ref[:, here].astype(jnp.float32)
            hot = []
            for k in range(intersections):
                tile = inner * intersections + k
                lane_of = jnp.broadcast_to(turned[:, tile : tile + 1], (LANES, LANES))
                hot.append(jnp.where(lane_of == column_ids, one, zero))
            hot = jnp.concatenate(
                [
                    jnp.concatenate([hot[0], hot[1]], axis=1),
                    jnp.concatenate([hot[2], hot[3]], axis=1),
                ],
                axis=0,
            )
            hot_ref[step] = hot
            parts = split_high(share)
            rows = jnp.concatenate(
                [jnp.where(first_half, parts, 0.0), jnp.where(first_half, 0.0, parts)], axis=1
            ).astype(jnp.bfloat16)
            spread = jnp.dot(rows, hot, preferred_element_type=jnp.float32)
            for k in range(intersections):
                side = slice((k % 2) * LANES, (k % 2 + 1) * LANES)
                low = intersections + k
                shared = spread[k : k + 1, side] + spread[low : low + 1, side]
                place = place_ref[k, step]
                sums[k][lax.div(place, fields)] += jnp.where(
                    field_ids == lax.rem(place, fields), shared, 0.0
                )
        return carry

    lax.fori_loop(0, windows // GROUP, body, 0)
    total = sums[0][...]
    for ref in sums[1:]:
        total = total + ref[...]
    share_ref[...] = total


def middle_kernel(
    far_ref,
    place_ref,
    spot_ref,
    mix_ref,
    arrived_ref,
    column_ref,
    ocean_weight_ref,
    atmos_weight_ref,
    mask_ref,
    base_ref,
    state_ref,
    hot_ref,
    share_ref,
    forcing_ref,
    away_ref,
    home_ref,
    value_ref,
):
    intersections, cells = column_ref.shape
    windows = cells // LANES
    fields = base_ref.shape[0]
    near, packed = away_ref.shape[:2]
    per_owner = packed * fields // (fields + 1)
    value_ref[...] = jnp.zeros(value_ref.shape, jnp.float32)
    corner = mix_ref[0, 0]
    blank = jnp.zeros((2 * fields, LANES), jnp.float32)

    def body(group, carry):
        for inner in range(GROUP):
            step = group * GROUP + inner
            here = window(step)
            lanes = column_ref[:, here] & (LANES - 1)
            ocean_weight = ocean_weight_ref[:, here]
            total = jnp.zeros((fields, LANES), jnp.float32)
            weight = jnp.zeros((1, LANES), jnp.float32)
            for k in range(intersections):
                picked = jnp.take_along_axis(
                    arrived_ref[spot_ref[k, step]],
                    jnp.broadcast_to(lanes[k : k + 1], (fields, LANES)),
                    axis=1,
                    mode="promise_in_bounds",
                )
                total = total + ocean_weight[k : k + 1] * picked
                weight = weight + ocean_weight[k : k + 1]
            forcing = total / weight
            forcing_ref[:, here] = forcing
            mask = mask_ref[:, here]
            surface = jnp.where(
                mask == 1, base_ref[:, here] + corner * forcing, state_ref[:, here]
            )
            share = atmos_weight_ref[:, here] * mask.astype(jnp.float32)
            parts = [split_high(share[k : k + 1] * surface) for k in range(intersections)]
            left = [parts[0], parts[1], blank, blank]
            right = [blank, blank, parts[2], parts[3]]
            rows = jnp.concatenate(
                [jnp.concatenate(left, axis=0), jnp.concatenate(right, axis=0)], axis=1
            ).astype(jnp.bfloat16)
            spread = jnp.dot(rows, hot_ref[step], preferred_element_type=jnp.float32)
            for k in range(intersections):
                side = slice((k % 2) * LANES, (k % 2 + 1) * LANES)
                at = 2 * fields * k
                value_ref[place_ref[k, step]] = (
                    spread[at : at + fields, side] + spread[at + fields : at + 2 * fields, side]
                )
        return carry

    lax.fori_loop(0, windows // GROUP, body, 0)
    far = far_ref[0]
    rows = per_owner // fields
    for ref, shard in ((away_ref, 1 - far), (home_ref, far)):
        values = value_ref[pl.ds(shard * near * per_owner, near * per_owner)]
        ref[:, :per_owner] = values.reshape(near, per_owner, fields, LANES)
        shares = share_ref[pl.ds(shard * near * rows, near * rows)]
        ref[:, per_owner:] = shares.reshape(near, rows, fields, LANES)


def ocean_kernel(mix_ref, forcing_ref, mask_ref, *refs):
    x_refs, (out_ref, high_ref, low_ref) = refs[:-3], refs[-3:]
    levels, fields, block = out_ref.shape
    rows = levels * fields

    @pl.when(pl.program_id(0) == 0)
    def _():
        level = lax.broadcasted_iota(jnp.int32, (rows, levels), 0) // fields
        pick = (level == lax.broadcasted_iota(jnp.int32, (rows, levels), 1)).astype(jnp.float32)
        tall = jnp.dot(pick, mix_ref[...], precision=lax.Precision.HIGHEST)
        wide = lax.dot_general(
            tall, pick, (((1,), (1,)), ((), ())), precision=lax.Precision.HIGHEST
        )
        down = lax.broadcasted_iota(jnp.int32, (rows, rows), 0) % fields
        across = lax.broadcasted_iota(jnp.int32, (rows, rows), 1) % fields
        wide = jnp.where(down == across, wide, 0.0)
        high = wide.astype(jnp.bfloat16)
        high_ref[...] = high
        low_ref[...] = (wide - high.astype(jnp.float32)).astype(jnp.bfloat16)

    flat = jnp.concatenate(
        [ref[...].reshape(rows // len(x_refs), block) for ref in x_refs], axis=0
    )
    push = jnp.concatenate(
        [forcing_ref[...], jnp.zeros((rows - fields, block), jnp.float32)], axis=0
    )
    loaded = flat + push
    high = loaded.astype(jnp.bfloat16)
    low = (loaded - high.astype(jnp.float32)).astype(jnp.bfloat16)
    mixed = (
        jnp.dot(high_ref[...], high, preferred_element_type=jnp.float32)
        + jnp.dot(high_ref[...], low, preferred_element_type=jnp.float32)
        + jnp.dot(low_ref[...], high, preferred_element_type=jnp.float32)
    )
    out_ref[...] = jnp.where(mask_ref[...] == 1, mixed, flat).reshape(levels, fields, block)


def diffuse_ocean(state, mixing, forcing, mask):
    levels, fields, cells = state.shape
    block = min(1024, cells)
    rows = levels * fields
    specs = level_specs(levels, fields, block)
    return pl.pallas_call(
        ocean_kernel,
        grid=(cells // block,),
        in_specs=[
            pl.BlockSpec(mixing.shape, lambda i: (0, 0)),
            pl.BlockSpec((fields, block), lambda i: (0, i)),
            pl.BlockSpec((1, block), lambda i: (0, i)),
        ]
        + specs,
        out_specs=pl.BlockSpec((levels, fields, block), lambda i: (0, 0, i)),
        out_shape=jax.ShapeDtypeStruct(state.shape, jnp.float32),
        scratch_shapes=[pltpu.VMEM((rows, rows), jnp.bfloat16)] * 2,
        compiler_params=stream_params,
        cost_estimate=pl.CostEstimate(
            flops=6 * rows * rows * cells,
            bytes_accessed=8 * rows * cells,
            transcendentals=0,
        ),
        name="diffuse_ocean",
    )(mixing, forcing, mask, *[state] * len(specs))


def collect_kernel(per_owner, home, far_ref, asked_ref, back_ref, out_ref, *sums):
    near, packed, fields, _ = back_ref.shape
    columns = sums[0].shape[1]
    quarter = columns // fields
    chains = len(sums) // 2
    far = far_ref[0]
    first = (far if home else 1 - far) * per_owner
    for ref in sums:
        ref[...] = jnp.zeros(ref.shape, jnp.float32)

    def body(step, carry):
        for slot in range(per_owner):
            for chain in range(chains):
                peer = step * chains + chain
                at = window(asked_ref[peer, first + slot])
                tile, row = per_owner + slot // fields, slot % fields
                sums[chain][:, at] += back_ref[peer, slot]
                sums[chains + chain][:, at] += back_ref[peer, tile, row : row + 1]
        return carry

    lax.fori_loop(0, near // chains, body, 0)
    values, shares = sums[0][...], sums[chains][...]
    for chain in range(1, chains):
        values = values + sums[chain][...]
        shares = shares + sums[chains + chain][...]
    out_ref[:, :columns] = values
    for row in range(fields):
        out_ref[row : row + 1, columns:] = shares[:, row * quarter : (row + 1) * quarter]


def collect(asked, far, back, per_owner, columns, home):
    fields = back.shape[2]
    chains = 4
    return pl.pallas_call(
        functools.partial(collect_kernel, per_owner, home),
        in_specs=[smem, smem, vmem],
        out_specs=vmem,
        out_shape=jax.ShapeDtypeStruct((fields, columns + columns // fields), jnp.float32),
        scratch_shapes=[pltpu.VMEM((fields, columns), jnp.float32)] * chains
        + [pltpu.VMEM((1, columns), jnp.float32)] * chains,
        compiler_params=params,
        name="collect_home" if home else "collect_away",
    )(far, asked, back)


def final_kernel(keep_ref, other_ref, land_weight_ref, land_ref, out_ref):
    fields, columns = out_ref.shape
    quarter = columns // fields
    both = keep_ref[:, :columns] + other_ref[:, :columns]
    shares = keep_ref[:, columns:] + other_ref[:, columns:]
    land_weight = land_weight_ref[...]
    total = both + land_weight * land_ref[...]
    for row in range(fields):
        part = slice(row * quarter, (row + 1) * quarter)
        out_ref[:, part] = total[:, part] / (shares[row : row + 1] + land_weight[:, part])


def per_device(
    atmos_profiles,
    atmos_mixing,
    drag_factor,
    surface_before,
    downward_fluxes,
    land_weight,
    land_surface,
    ocean_state,
    ocean_mixing,
    sea_mask,
    exchange_slot,
    parent_column,
    ocean_weight,
    atmos_weight,
):
    near = lax.axis_size("near") * lax.axis_size("sub")
    devices = 2 * near
    fields, _, columns = atmos_profiles.shape
    intersections, cells = exchange_slot.shape
    capacity = 2 * intersections * cells // devices
    per_owner = capacity // LANES
    spots = 2 * per_owner
    mask = sea_mask.reshape(1, cells)
    state = ocean_state.transpose(1, 0, 2)
    far = lax.axis_index("far").astype(jnp.int32).reshape(1)

    def to_near(values):
        return lax.all_to_all(values, ("near", "sub"), split_axis=0, concat_axis=0, tiled=True)

    def to_far(values):
        return lax.ppermute(values, "far", ((0, 1), (1, 0)))

    place, spot, wanted, forcing_rows, tendency = start(
        near,
        per_owner,
        exchange_slot,
        parent_column,
        atmos_profiles,
        drag_factor,
        surface_before,
        downward_fluxes,
    )
    asked = to_near(wanted)
    other_rows = to_far(forcing_rows)
    base, first_level = top_level(state, ocean_mixing)
    asked, base, first_level = lax.optimization_barrier((asked, base, first_level))
    served = pl.pallas_call(
        functools.partial(serve_kernel, per_owner),
        in_specs=[smem, smem] + [pl.BlockSpec(memory_space=pl.ANY)] * 2,
        out_specs=vmem,
        out_shape=jax.ShapeDtypeStruct((near, spots, fields, LANES), jnp.float32),
        scratch_shapes=[
            pltpu.VMEM((2, fields, columns), jnp.float32),
            pltpu.SemaphoreType.DMA((2,)),
        ],
        compiler_params=params,
        name="serve_windows",
    )(far, asked, forcing_rows, other_rows)
    served, columns_asked = lax.optimization_barrier((served, parent_column))
    arrived = to_near(served)
    rows = per_owner // fields
    windows = cells // LANES
    hot, shares = pl.pallas_call(
        hot_kernel,
        in_specs=[smem] + [vmem] * 3,
        out_specs=[vmem] * 2,
        out_shape=[
            jax.ShapeDtypeStruct((windows, 2 * LANES, 2 * LANES), jnp.bfloat16),
            jax.ShapeDtypeStruct((2 * near * rows, fields, LANES), jnp.float32),
        ],
        scratch_shapes=[pltpu.VMEM((windows // GROUP, LANES, LANES), jnp.bfloat16)]
        + [pltpu.VMEM((2 * near * rows, fields, LANES), jnp.float32)] * intersections,
        compiler_params=params,
        name="one_hot_and_shares",
    )(place, columns_asked, atmos_weight, mask)
    arrived, hot, shares = lax.optimization_barrier((arrived, hot, shares))
    sent = (near, per_owner + rows, fields, LANES)
    forcing, away, home = pl.pallas_call(
        middle_kernel,
        in_specs=[smem] * 4 + [vmem] * 9,
        out_specs=[vmem] * 3,
        out_shape=[
            jax.ShapeDtypeStruct((fields, cells), jnp.float32),
            jax.ShapeDtypeStruct(sent, jnp.float32),
            jax.ShapeDtypeStruct(sent, jnp.float32),
        ],
        scratch_shapes=[pltpu.VMEM((near * spots, fields, LANES), jnp.float32)],
        compiler_params=params,
        name="forcing_and_windows",
    )(
        far,
        place,
        spot,
        ocean_mixing,
        arrived.reshape(near * spots, fields, LANES),
        parent_column,
        ocean_weight,
        atmos_weight,
        mask,
        base,
        first_level,
        hot,
        shares,
    )
    tendency, forcing = lax.optimization_barrier((tendency, forcing))
    atmos_updated = diffuse_atmos(atmos_profiles, atmos_mixing, tendency)
    back_away, atmos_updated, home = lax.optimization_barrier(
        (to_near(away), atmos_updated, home)
    )
    back_home = to_near(home)
    sums_away = collect(asked, far, back_away, per_owner, columns, False)
    other_sums = to_far(sums_away)
    ocean_updated = diffuse_ocean(state, ocean_mixing, forcing, mask).transpose(1, 0, 2)
    back_home, ocean_updated = lax.optimization_barrier((back_home, ocean_updated))
    sums_home = collect(asked, far, back_home, per_owner, columns, True)
    surface_state = pl.pallas_call(
        final_kernel,
        in_specs=[vmem] * 4,
        out_specs=vmem,
        out_shape=jax.ShapeDtypeStruct((fields, columns), jnp.float32),
        compiler_params=params,
        name="surface_state",
    )(sums_home, other_sums, land_weight.reshape(1, columns), land_surface)
    return (atmos_updated, ocean_updated, surface_state)


def solution(mesh):
    comp, sub = mesh.devices.shape
    halves = jax.sharding.Mesh(mesh.devices.reshape(2, comp // 2, sub), AXES)
    split = P(None, AXES)
    return jax.shard_map(
        per_device,
        mesh=halves,
        in_specs=(
            P(None, None, AXES),
            P(),
            P(AXES),
            split,
            split,
            P(AXES),
            split,
            P(None, None, AXES),
            P(),
            P(AXES),
            split,
            split,
            split,
            split,
        ),
        out_specs=(P(None, None, AXES), P(None, None, AXES), split),
        check_vma=False,
    )
```

```python
import functools

import jax
import jax.numpy as jnp
from jax import lax
from jax.experimental import pallas as pl
from jax.experimental.pallas import tpu as pltpu
from jax.sharding import PartitionSpec as P

couple_rate = 0.5
LANES = 128
params = pltpu.CompilerParams(vmem_limit_bytes=24 * 1024 * 1024)
stream_params = pltpu.CompilerParams(vmem_limit_bytes=52 * 1024 * 1024)
middle_params = pltpu.CompilerParams(vmem_limit_bytes=48 * 1024 * 1024)
first_params = pltpu.CompilerParams(vmem_limit_bytes=56 * 1024 * 1024)
vmem = pl.BlockSpec(memory_space=pltpu.VMEM)
smem = pl.BlockSpec(memory_space=pltpu.SMEM)
hbm = pl.BlockSpec(memory_space=pl.ANY)
AXES = ("far", "near", "sub")


def window(index):
    return pl.ds(pl.multiple_of(index * LANES, LANES), LANES)


def make_requests(per_owner, slot_ref, column_ref, place_ref, spot_ref, wanted_ref):
    intersections, cells = slot_ref.shape
    near, spots = wanted_ref.shape
    windows = cells // LANES
    lane = lax.broadcasted_iota(jnp.int32, (intersections, windows), 1)

    def heads(ref):
        found = jnp.zeros((intersections, windows), jnp.int32)
        for step in range(windows):
            head = ref[:, step * LANES : step * LANES + 1]
            found = jnp.where(lane == step, head, found)
        return found // LANES

    place = heads(slot_ref)
    column_window = heads(column_ref)
    owner = place // per_owner
    peer = owner % near
    spot = owner // near * per_owner + place % per_owner
    place_ref[...] = place
    spot_ref[...] = peer * spots + spot
    peer_ids = lax.broadcasted_iota(jnp.int32, (near, windows), 0)
    spot_ids = lax.broadcasted_iota(jnp.int32, (spots, windows), 0)
    wanted = jnp.zeros((near, spots), jnp.float32)
    for k in range(intersections):
        row = slice(k, k + 1)
        peer_hot = jnp.where(peer_ids == peer[row], 1.0, 0.0)
        spot_hot = jnp.where(
            spot_ids == spot[row], column_window[row].astype(jnp.float32), 0.0
        )
        wanted = wanted + lax.dot_general(
            peer_hot.astype(jnp.bfloat16),
            spot_hot.astype(jnp.bfloat16),
            (((1,), (1,)), ((), ())),
            preferred_element_type=jnp.float32,
        )
    wanted_ref[...] = wanted.astype(jnp.int32)


def start_kernel(
    last,
    per_owner,
    slot_ref,
    column_ref,
    x_ref,
    drag_ref,
    before_ref,
    down_ref,
    place_ref,
    spot_ref,
    wanted_ref,
    forcing_ref,
    tend_ref,
):
    @pl.when(pl.program_id(0) == 0)
    def _():
        make_requests(per_owner, slot_ref, column_ref, place_ref, spot_ref, wanted_ref)

    def row(ref, index):
        return ref[index : index + 1, :]

    bottom = [x_ref[member].astype(jnp.float32)[last : last + 1, :] for member in range(4)]
    east = bottom[2] - row(before_ref, 2)
    north = bottom[3] - row(before_ref, 3)
    transfer = drag_ref[...] * jnp.sqrt(1.0 + east * east + north * north)
    sensible = transfer * (row(before_ref, 0) - bottom[0])
    latent = transfer * (row(before_ref, 1) - bottom[1])
    east_stress = couple_rate * (transfer * east)
    north_stress = couple_rate * (transfer * north)
    forcing_ref[0:1, :] = couple_rate * (
        row(down_ref, 0) + row(down_ref, 1) - sensible - latent
    )
    forcing_ref[1:2, :] = couple_rate * (latent - row(down_ref, 2) - row(down_ref, 3))
    forcing_ref[2:3, :] = east_stress
    forcing_ref[3:4, :] = north_stress
    tend_ref[0:1, :] = couple_rate * sensible
    tend_ref[1:2, :] = couple_rate * latent
    tend_ref[2:3, :] = -east_stress
    tend_ref[3:4, :] = -north_stress


def start(near, per_owner, slots, parents, profiles, drag_factor, surface_before, downward):
    fields, levels, columns = profiles.shape
    intersections, cells = slots.shape
    block = min(4096, columns)
    tall = 16
    at = (levels - 1) // tall
    rows = pl.BlockSpec((fields, block), lambda i: (0, i))
    tiles = (intersections, cells // LANES)
    asked = (near, 2 * per_owner)

    def whole(shape):
        return pl.BlockSpec(shape, lambda i: (0, 0))

    return pl.pallas_call(
        functools.partial(start_kernel, levels - 1 - at * tall, per_owner),
        grid=(columns // block,),
        in_specs=[
            whole(slots.shape),
            whole(slots.shape),
            pl.BlockSpec((fields, tall, block), lambda i: (0, at, i)),
            pl.BlockSpec((1, block), lambda i: (0, i)),
            rows,
            rows,
        ],
        out_specs=[whole(tiles), whole(tiles), whole(asked), rows, rows],
        out_shape=[
            jax.ShapeDtypeStruct(tiles, jnp.int32),
            jax.ShapeDtypeStruct(tiles, jnp.int32),
            jax.ShapeDtypeStruct(asked, jnp.int32),
            jax.ShapeDtypeStruct((fields, columns), jnp.float32),
            jax.ShapeDtypeStruct((fields, columns), jnp.float32),
        ],
        compiler_params=first_params,
        name="requests_and_rates",
    )(slots, parents, profiles, drag_factor.reshape(1, columns), surface_before, downward)


def atmos_kernel(mix_ref, tend_ref, *refs):
    mix = mix_ref[...]
    lowest = mix[:, mix.shape[1] - 1 :].astype(jnp.float32)
    out_ref = refs[-1]
    for member, x_ref in enumerate(refs[:-1]):
        mixed = jnp.dot(mix, x_ref[0], preferred_element_type=jnp.float32)
        out_ref[member] = (mixed + lowest * tend_ref[member : member + 1, :]).astype(jnp.bfloat16)


def diffuse_atmos(profiles, mixing, tendency):
    fields, levels, columns = profiles.shape
    block = min(2048, columns)

    def field(member):
        return pl.BlockSpec((1, levels, block), lambda i: (member, 0, i))

    return pl.pallas_call(
        atmos_kernel,
        grid=(columns // block,),
        in_specs=[
            pl.BlockSpec((levels, levels), lambda i: (0, 0)),
            pl.BlockSpec((fields, block), lambda i: (0, i)),
        ]
        + [field(member) for member in range(fields)],
        out_specs=pl.BlockSpec((fields, levels, block), lambda i: (0, 0, i)),
        out_shape=jax.ShapeDtypeStruct(profiles.shape, jnp.bfloat16),
        compiler_params=stream_params,
        cost_estimate=pl.CostEstimate(
            flops=2 * fields * levels * levels * columns,
            bytes_accessed=4 * fields * levels * columns,
            transcendentals=0,
        ),
        name="diffuse_atmos",
    )(mixing, tendency, *[profiles] * fields)


def level_specs(levels, fields, block):
    count = 4 if levels % 4 == 0 else 1

    def part(number):
        return pl.BlockSpec((levels // count, fields, block), lambda i: (number, 0, i))

    return [part(number) for number in range(count)]


def top_kernel(mix_ref, *refs):
    state_refs, base_ref, first_ref = refs[:-2], refs[-2], refs[-1]
    total = None
    level = 0
    for ref in state_refs:
        for inner in range(ref.shape[0]):
            term = mix_ref[0, level] * ref[inner]
            total = term if total is None else total + term
            level += 1
    base_ref[...] = total
    first_ref[...] = state_refs[0][0]


def top_level(state, mixing):
    levels, fields, cells = state.shape
    block = min(2048, cells)
    specs = level_specs(levels, fields, block)
    return pl.pallas_call(
        top_kernel,
        grid=(cells // block,),
        in_specs=[smem] + specs,
        out_specs=[pl.BlockSpec((fields, block), lambda i: (0, i))] * 2,
        out_shape=[jax.ShapeDtypeStruct((fields, cells), jnp.float32)] * 2,
        compiler_params=stream_params,
        cost_estimate=pl.CostEstimate(
            flops=2 * fields * levels * cells,
            bytes_accessed=4 * fields * levels * cells,
            transcendentals=0,
        ),
        name="top_level",
    )(mixing, *[state] * len(specs))


def serve_kernel(
    per_owner, far_ref, asked_ref, own_ref, other_ref, out_ref, blocks_ref, arrived_sem
):
    @pl.when(pl.program_id(0) == 0)
    def _():
        copies = [
            pltpu.make_async_copy(ref, blocks_ref.at[index], arrived_sem.at[index])
            for index, ref in enumerate((own_ref, other_ref))
        ]
        for copy in copies:
            copy.start()
        for copy in copies:
            copy.wait()

    far = far_ref[0]
    peers = out_ref.shape[0]
    first = pl.program_id(0) * peers

    def body(peer, carry):
        for shard in range(2):
            for slot in range(per_owner):
                spot = shard * per_owner + slot
                out_ref[peer, spot] = blocks_ref[
                    shard ^ far, :, window(asked_ref[first + peer, spot])
                ]
        return carry

    lax.fori_loop(0, peers, body, 0)


def split_high(values):
    high = values.astype(jnp.bfloat16).astype(jnp.float32)
    return jnp.concatenate([high, values - high], axis=0)


GROUP = 8


def hot_kernel(
    place_ref,
    column_ref,
    atmos_weight_ref,
    mask_ref,
    hot_ref,
    share_ref,
    lanes_ref,
    *sums,
):
    intersections, cells = column_ref.shape
    windows = cells // LANES
    fields = share_ref.shape[1]
    group_tiles = GROUP * intersections
    steps = LANES // intersections
    group = pl.program_id(0)
    @pl.when(group == 0)
    def _():
        for ref in sums:
            ref[...] = jnp.zeros(ref.shape, jnp.float32)
        for first in range(0, windows, steps):
            tall = jnp.concatenate(
                [
                    column_ref[:, (first + step) * LANES : (first + step + 1) * LANES] & (LANES - 1)
                    for step in range(steps)
                ],
                axis=0,
            )
            turned = tall.astype(jnp.float32).T.astype(jnp.bfloat16)
            for part in range(steps // GROUP):
                lanes_ref[first // GROUP + part, :, :group_tiles] = turned[
                    :, part * group_tiles : (part + 1) * group_tiles
                ]

    column_ids = lax.broadcasted_iota(jnp.int32, (LANES, LANES), 1)
    column_ids = column_ids.astype(jnp.float32).astype(jnp.bfloat16)
    one, zero = jnp.bfloat16(1.0), jnp.bfloat16(0.0)
    field_ids = lax.broadcasted_iota(jnp.int32, (fields, LANES), 0)
    share_rows = lax.broadcasted_iota(jnp.int32, (2 * intersections, LANES), 0)
    first_half = share_rows % intersections < 2

    turned = lanes_ref[group]
    for inner in range(GROUP):
        step = group * GROUP + inner
        here = window(step)
        share = atmos_weight_ref[:, here] * mask_ref[:, here].astype(jnp.float32)
        hot = []
        for k in range(intersections):
            tile = inner * intersections + k
            lane_of = jnp.broadcast_to(turned[:, tile : tile + 1], (LANES, LANES))
            hot.append(jnp.where(lane_of == column_ids, one, zero))
        hot = jnp.concatenate(
            [
                jnp.concatenate([hot[0], hot[1]], axis=1),
                jnp.concatenate([hot[2], hot[3]], axis=1),
            ],
            axis=0,
        )
        hot_ref[inner] = hot
        parts = split_high(share)
        rows = jnp.concatenate(
            [jnp.where(first_half, parts, 0.0), jnp.where(first_half, 0.0, parts)], axis=1
        ).astype(jnp.bfloat16)
        spread = jnp.dot(rows, hot, preferred_element_type=jnp.float32)
        for k in range(intersections):
            side = slice((k % 2) * LANES, (k % 2 + 1) * LANES)
            low = intersections + k
            shared = spread[k : k + 1, side] + spread[low : low + 1, side]
            place = place_ref[k, step]
            sums[k][lax.div(place, fields)] += jnp.where(
                field_ids == lax.rem(place, fields), shared, 0.0
            )

    @pl.when(group == pl.num_programs(0) - 1)
    def _():
        total = sums[0][...]
        for ref in sums[1:]:
            total = total + ref[...]
        share_ref[...] = total


def middle_kernel(
    far_ref,
    place_ref,
    spot_ref,
    mix_ref,
    arrived_ref,
    column_ref,
    ocean_weight_ref,
    atmos_weight_ref,
    mask_ref,
    base_ref,
    state_ref,
    hot_ref,
    share_ref,
    forcing_ref,
    away_ref,
    home_ref,
    value_ref,
    held_ref,
    held_sem,
    sent_sem,
):
    intersections, cells = column_ref.shape
    windows = cells // LANES
    fields = base_ref.shape[0]
    near, packed = away_ref.shape[:2]
    per_owner = packed * fields // (fields + 1)
    rows = per_owner // fields

    def fetch(group):
        part = pl.ds(group * GROUP, GROUP)
        return pltpu.make_async_copy(hot_ref.at[part], held_ref.at[part], held_sem.at[group])

    for group in range(windows // GROUP):
        fetch(group).start()
    value_ref[...] = jnp.zeros(value_ref.shape, jnp.float32)
    corner = mix_ref[0, 0]
    blank = jnp.zeros((2 * fields, LANES), jnp.float32)

    def body(group, carry):
        fetch(group).wait()
        for inner in range(GROUP):
            step = group * GROUP + inner
            here = window(step)
            lanes = column_ref[:, here] & (LANES - 1)
            ocean_weight = ocean_weight_ref[:, here]
            total = jnp.zeros((fields, LANES), jnp.float32)
            weight = jnp.zeros((1, LANES), jnp.float32)
            for k in range(intersections):
                picked = jnp.take_along_axis(
                    arrived_ref[spot_ref[k, step]],
                    jnp.broadcast_to(lanes[k : k + 1], (fields, LANES)),
                    axis=1,
                    mode="promise_in_bounds",
                )
                total = total + ocean_weight[k : k + 1] * picked
                weight = weight + ocean_weight[k : k + 1]
            forcing = total / weight
            forcing_ref[:, here] = forcing
            mask = mask_ref[:, here]
            surface = jnp.where(
                mask == 1, base_ref[:, here] + corner * forcing, state_ref[:, here]
            )
            share = atmos_weight_ref[:, here] * mask.astype(jnp.float32)
            parts = [split_high(share[k : k + 1] * surface) for k in range(intersections)]
            left = [parts[0], parts[1], blank, blank]
            right = [blank, blank, parts[2], parts[3]]
            parts = jnp.concatenate(
                [jnp.concatenate(left, axis=0), jnp.concatenate(right, axis=0)], axis=1
            ).astype(jnp.bfloat16)
            spread = jnp.dot(parts, held_ref[step], preferred_element_type=jnp.float32)
            for k in range(intersections):
                side = slice((k % 2) * LANES, (k % 2 + 1) * LANES)
                at = 2 * fields * k
                value_ref[place_ref[k, step]] = (
                    spread[at : at + fields, side] + spread[at + fields : at + 2 * fields, side]
                )
        return carry

    lax.fori_loop(0, windows // GROUP, body, 0)
    far = far_ref[0]
    shards = value_ref.reshape(2, near, per_owner, fields, LANES)
    copies = []
    for index, (ref, shard) in enumerate(((away_ref, 1 - far), (home_ref, far))):
        copies.append(
            pltpu.make_async_copy(
                shards.at[shard], ref.at[:, pl.ds(0, per_owner)], sent_sem.at[2 * index]
            )
        )
        copies.append(
            pltpu.make_async_copy(
                share_ref.at[shard],
                ref.at[:, pl.ds(per_owner, rows)],
                sent_sem.at[2 * index + 1],
            )
        )
    for copy in copies:
        copy.start()
    for copy in copies:
        copy.wait()


def ocean_kernel(mix_ref, forcing_ref, mask_ref, *refs):
    x_refs, (out_ref, high_ref, low_ref) = refs[:-3], refs[-3:]
    levels, fields, block = out_ref.shape
    rows = levels * fields

    @pl.when(pl.program_id(0) == 0)
    def _():
        level = lax.broadcasted_iota(jnp.int32, (rows, levels), 0) // fields
        pick = (level == lax.broadcasted_iota(jnp.int32, (rows, levels), 1)).astype(jnp.float32)
        tall = jnp.dot(pick, mix_ref[...], precision=lax.Precision.HIGHEST)
        wide = lax.dot_general(
            tall, pick, (((1,), (1,)), ((), ())), precision=lax.Precision.HIGHEST
        )
        down = lax.broadcasted_iota(jnp.int32, (rows, rows), 0) % fields
        across = lax.broadcasted_iota(jnp.int32, (rows, rows), 1) % fields
        wide = jnp.where(down == across, wide, 0.0)
        high = wide.astype(jnp.bfloat16)
        high_ref[...] = high
        low_ref[...] = (wide - high.astype(jnp.float32)).astype(jnp.bfloat16)

    flat = jnp.concatenate(
        [ref[...].reshape(rows // len(x_refs), block) for ref in x_refs], axis=0
    )
    push = jnp.concatenate(
        [forcing_ref[...], jnp.zeros((rows - fields, block), jnp.float32)], axis=0
    )
    loaded = flat + push
    high = loaded.astype(jnp.bfloat16)
    low = (loaded - high.astype(jnp.float32)).astype(jnp.bfloat16)
    mixed = (
        jnp.dot(high_ref[...], high, preferred_element_type=jnp.float32)
        + jnp.dot(high_ref[...], low, preferred_element_type=jnp.float32)
        + jnp.dot(low_ref[...], high, preferred_element_type=jnp.float32)
    )
    out_ref[...] = jnp.where(mask_ref[...] == 1, mixed, flat).reshape(levels, fields, block)


def diffuse_ocean(state, mixing, forcing, mask):
    levels, fields, cells = state.shape
    block = min(1024, cells)
    rows = levels * fields
    specs = level_specs(levels, fields, block)
    return pl.pallas_call(
        ocean_kernel,
        grid=(cells // block,),
        in_specs=[
            pl.BlockSpec(mixing.shape, lambda i: (0, 0)),
            pl.BlockSpec((fields, block), lambda i: (0, i)),
            pl.BlockSpec((1, block), lambda i: (0, i)),
        ]
        + specs,
        out_specs=pl.BlockSpec((levels, fields, block), lambda i: (0, 0, i)),
        out_shape=jax.ShapeDtypeStruct(state.shape, jnp.float32),
        scratch_shapes=[pltpu.VMEM((rows, rows), jnp.bfloat16)] * 2,
        compiler_params=stream_params,
        cost_estimate=pl.CostEstimate(
            flops=6 * rows * rows * cells,
            bytes_accessed=8 * rows * cells,
            transcendentals=0,
        ),
        name="diffuse_ocean",
    )(mixing, forcing, mask, *[state] * len(specs))


def collect_kernel(per_owner, far_ref, asked_ref, back_ref, *refs):
    near, _, fields, _ = back_ref.shape
    chains = 4
    sums = refs[-2 * chains :]
    rest = refs[: -2 * chains]
    home = len(rest) > 1
    columns = sums[0].shape[1]
    quarter = columns // fields
    far = far_ref[0]
    first = (far if home else 1 - far) * per_owner
    for ref in sums:
        ref[...] = jnp.zeros(ref.shape, jnp.float32)

    def body(step, carry):
        for slot in range(per_owner):
            for chain in range(chains):
                peer = step * chains + chain
                at = window(asked_ref[peer, first + slot])
                tile, row = per_owner + slot // fields, slot % fields
                sums[chain][:, at] += back_ref[peer, slot]
                sums[chains + chain][:, at] += back_ref[peer, tile, row : row + 1]
        return carry

    lax.fori_loop(0, near // chains, body, 0)
    values, shares = sums[0][...], sums[chains][...]
    for chain in range(1, chains):
        values = values + sums[chain][...]
        shares = shares + sums[chains + chain][...]
    out_ref = rest[-1]
    if home:
        other_ref, land_weight_ref, land_ref = rest[:3]
        land_weight = land_weight_ref[...]
        total = values + other_ref[:, :columns] + land_weight * land_ref[...]
        weight = shares + land_weight
        for row in range(fields):
            part = slice(row * quarter, (row + 1) * quarter)
            other_shares = other_ref[row : row + 1, columns:]
            out_ref[:, part] = total[:, part] / (weight[:, part] + other_shares)
    else:
        out_ref[:, :columns] = values
        for row in range(fields):
            out_ref[row : row + 1, columns:] = shares[:, row * quarter : (row + 1) * quarter]


def collect(asked, far, back, per_owner, columns, rest):
    fields = back.shape[2]
    chains = 4
    width = columns if rest else columns + columns // fields
    return pl.pallas_call(
        functools.partial(collect_kernel, per_owner),
        in_specs=[smem, smem, vmem] + [vmem] * len(rest),
        out_specs=vmem,
        out_shape=jax.ShapeDtypeStruct((fields, width), jnp.float32),
        scratch_shapes=[pltpu.VMEM((fields, columns), jnp.float32)] * chains
        + [pltpu.VMEM((1, columns), jnp.float32)] * chains,
        compiler_params=params,
        name="surface_state" if rest else "collect_away",
    )(far, asked, back, *rest)


def per_device(
    atmos_profiles,
    atmos_mixing,
    drag_factor,
    surface_before,
    downward_fluxes,
    land_weight,
    land_surface,
    ocean_state,
    ocean_mixing,
    sea_mask,
    exchange_slot,
    parent_column,
    ocean_weight,
    atmos_weight,
):
    near = lax.axis_size("near") * lax.axis_size("sub")
    devices = 2 * near
    fields, _, columns = atmos_profiles.shape
    intersections, cells = exchange_slot.shape
    capacity = 2 * intersections * cells // devices
    per_owner = capacity // LANES
    spots = 2 * per_owner
    mask = sea_mask.reshape(1, cells)
    state = ocean_state.transpose(1, 0, 2)
    far = lax.axis_index("far").astype(jnp.int32).reshape(1)

    def to_near(values):
        return lax.all_to_all(values, ("near", "sub"), split_axis=0, concat_axis=0, tiled=True)

    def to_far(values):
        return lax.ppermute(values, "far", ((0, 1), (1, 0)))

    place, spot, wanted, forcing_rows, tendency = start(
        near,
        per_owner,
        exchange_slot,
        parent_column,
        atmos_profiles,
        drag_factor,
        surface_before,
        downward_fluxes,
    )
    asked = to_near(wanted)
    other_rows = to_far(forcing_rows)
    base, first_level = top_level(state, ocean_mixing)
    asked, base, first_level = lax.optimization_barrier((asked, base, first_level))
    served = pl.pallas_call(
        functools.partial(serve_kernel, per_owner),
        grid=(4,),
        in_specs=[smem, smem, hbm, hbm],
        out_specs=pl.BlockSpec((near // 4, spots, fields, LANES), lambda i: (i, 0, 0, 0)),
        out_shape=jax.ShapeDtypeStruct((near, spots, fields, LANES), jnp.float32),
        scratch_shapes=[
            pltpu.VMEM((2, fields, columns), jnp.float32),
            pltpu.SemaphoreType.DMA((2,)),
        ],
        compiler_params=params,
        name="serve_windows",
    )(far, asked, forcing_rows, other_rows)
    served, columns_asked = lax.optimization_barrier((served, parent_column))
    arrived = to_near(served)
    rows = per_owner // fields
    windows = cells // LANES
    hot, shares = pl.pallas_call(
        hot_kernel,
        grid=(windows // GROUP,),
        in_specs=[smem] + [vmem] * 3,
        out_specs=[
            pl.BlockSpec((GROUP, 2 * LANES, 2 * LANES), lambda i: (i, 0, 0)),
            pl.BlockSpec((2 * near * rows, fields, LANES), lambda i: (0, 0, 0)),
        ],
        out_shape=[
            jax.ShapeDtypeStruct((windows, 2 * LANES, 2 * LANES), jnp.bfloat16),
            jax.ShapeDtypeStruct((2 * near * rows, fields, LANES), jnp.float32),
        ],
        scratch_shapes=[pltpu.VMEM((windows // GROUP, LANES, LANES), jnp.bfloat16)]
        + [pltpu.VMEM((2 * near * rows, fields, LANES), jnp.float32)] * intersections,
        compiler_params=middle_params,
        name="one_hot_and_shares",
    )(place, columns_asked, atmos_weight, mask)
    arrived, hot, shares = lax.optimization_barrier((arrived, hot, shares))
    sent = (near, per_owner + rows, fields, LANES)
    forcing, away, home = pl.pallas_call(
        middle_kernel,
        in_specs=[smem] * 4 + [vmem] * 7 + [hbm, vmem],
        out_specs=[vmem, hbm, hbm],
        out_shape=[
            jax.ShapeDtypeStruct((fields, cells), jnp.float32),
            jax.ShapeDtypeStruct(sent, jnp.float32),
            jax.ShapeDtypeStruct(sent, jnp.float32),
        ],
        scratch_shapes=[
            pltpu.VMEM((near * spots, fields, LANES), jnp.float32),
            pltpu.VMEM((windows, 2 * LANES, 2 * LANES), jnp.bfloat16),
            pltpu.SemaphoreType.DMA((windows // GROUP,)),
            pltpu.SemaphoreType.DMA((4,)),
        ],
        compiler_params=middle_params,
        name="forcing_and_windows",
    )(
        far,
        place,
        spot,
        ocean_mixing,
        arrived.reshape(near * spots, fields, LANES),
        parent_column,
        ocean_weight,
        atmos_weight,
        mask,
        base,
        first_level,
        hot,
        shares.reshape(2, near, rows, fields, LANES),
    )
    tendency, forcing = lax.optimization_barrier((tendency, forcing))
    atmos_updated = diffuse_atmos(atmos_profiles, atmos_mixing, tendency)
    back_away, atmos_updated, home = lax.optimization_barrier(
        (to_near(away), atmos_updated, home)
    )
    back_home = to_near(home)
    sums_away = collect(asked, far, back_away, per_owner, columns, ())
    other_sums = to_far(sums_away)
    ocean_updated = diffuse_ocean(state, ocean_mixing, forcing, mask).transpose(1, 0, 2)
    back_home, ocean_updated = lax.optimization_barrier((back_home, ocean_updated))
    surface_state = collect(
        asked,
        far,
        back_home,
        per_owner,
        columns,
        (other_sums, land_weight.reshape(1, columns), land_surface),
    )
    return (atmos_updated, ocean_updated, surface_state)


def solution(mesh):
    comp, sub = mesh.devices.shape
    halves = jax.sharding.Mesh(mesh.devices.reshape(2, comp // 2, sub), AXES)
    split = P(None, AXES)
    return jax.shard_map(
        per_device,
        mesh=halves,
        in_specs=(
            P(None, None, AXES),
            P(),
            P(AXES),
            split,
            split,
            P(AXES),
            split,
            P(None, None, AXES),
            P(),
            P(AXES),
            split,
            split,
            split,
            split,
        ),
        out_specs=(P(None, None, AXES), P(None, None, AXES), split),
        check_vma=False,
    )
```

```python
import functools

import jax
import jax.numpy as jnp
from jax import lax
from jax.experimental import pallas as pl
from jax.experimental.pallas import tpu as pltpu
from jax.sharding import PartitionSpec as P

couple_rate = 0.5
LANES = 128
params = pltpu.CompilerParams(vmem_limit_bytes=24 * 1024 * 1024)
stream_params = pltpu.CompilerParams(vmem_limit_bytes=52 * 1024 * 1024)
middle_params = pltpu.CompilerParams(vmem_limit_bytes=48 * 1024 * 1024)
first_params = pltpu.CompilerParams(vmem_limit_bytes=56 * 1024 * 1024)
vmem = pl.BlockSpec(memory_space=pltpu.VMEM)
smem = pl.BlockSpec(memory_space=pltpu.SMEM)
hbm = pl.BlockSpec(memory_space=pl.ANY)
AXES = ("far", "near", "sub")


def window(index):
    return pl.ds(pl.multiple_of(index * LANES, LANES), LANES)


def make_requests(per_owner, slot_ref, column_ref, place_ref, spot_ref, wanted_ref):
    intersections, cells = slot_ref.shape
    near, spots = wanted_ref.shape
    windows = cells // LANES
    lane = lax.broadcasted_iota(jnp.int32, (intersections, windows), 1)

    def heads(ref):
        found = jnp.zeros((intersections, windows), jnp.int32)
        for step in range(windows):
            head = ref[:, step * LANES : step * LANES + 1]
            found = jnp.where(lane == step, head, found)
        return found // LANES

    place = heads(slot_ref)
    column_window = heads(column_ref)
    owner = place // per_owner
    peer = owner % near
    spot = owner // near * per_owner + place % per_owner
    place_ref[...] = place
    spot_ref[...] = peer * spots + spot
    peer_ids = lax.broadcasted_iota(jnp.int32, (near, windows), 0)
    spot_ids = lax.broadcasted_iota(jnp.int32, (spots, windows), 0)
    wanted = jnp.zeros((near, spots), jnp.float32)
    for k in range(intersections):
        row = slice(k, k + 1)
        peer_hot = jnp.where(peer_ids == peer[row], 1.0, 0.0)
        spot_hot = jnp.where(
            spot_ids == spot[row], column_window[row].astype(jnp.float32), 0.0
        )
        wanted = wanted + lax.dot_general(
            peer_hot.astype(jnp.bfloat16),
            spot_hot.astype(jnp.bfloat16),
            (((1,), (1,)), ((), ())),
            preferred_element_type=jnp.float32,
        )
    wanted_ref[...] = wanted.astype(jnp.int32)


def start_kernel(
    last,
    per_owner,
    slot_ref,
    column_ref,
    x_ref,
    drag_ref,
    before_ref,
    down_ref,
    place_ref,
    spot_ref,
    wanted_ref,
    forcing_ref,
    tend_ref,
):
    @pl.when(pl.program_id(0) == 0)
    def _():
        make_requests(per_owner, slot_ref, column_ref, place_ref, spot_ref, wanted_ref)

    def row(ref, index):
        return ref[index : index + 1, :]

    bottom = [x_ref[member].astype(jnp.float32)[last : last + 1, :] for member in range(4)]
    east = bottom[2] - row(before_ref, 2)
    north = bottom[3] - row(before_ref, 3)
    transfer = drag_ref[...] * jnp.sqrt(1.0 + east * east + north * north)
    sensible = transfer * (row(before_ref, 0) - bottom[0])
    latent = transfer * (row(before_ref, 1) - bottom[1])
    east_stress = couple_rate * (transfer * east)
    north_stress = couple_rate * (transfer * north)
    forcing_ref[0:1, :] = couple_rate * (
        row(down_ref, 0) + row(down_ref, 1) - sensible - latent
    )
    forcing_ref[1:2, :] = couple_rate * (latent - row(down_ref, 2) - row(down_ref, 3))
    forcing_ref[2:3, :] = east_stress
    forcing_ref[3:4, :] = north_stress
    tend_ref[0:1, :] = couple_rate * sensible
    tend_ref[1:2, :] = couple_rate * latent
    tend_ref[2:3, :] = -east_stress
    tend_ref[3:4, :] = -north_stress


def start(near, per_owner, slots, parents, profiles, drag_factor, surface_before, downward):
    fields, levels, columns = profiles.shape
    intersections, cells = slots.shape
    block = min(4096, columns)
    tall = 16
    at = (levels - 1) // tall
    rows = pl.BlockSpec((fields, block), lambda i: (0, i))
    tiles = (intersections, cells // LANES)
    asked = (near, 2 * per_owner)

    def whole(shape):
        return pl.BlockSpec(shape, lambda i: (0, 0))

    return pl.pallas_call(
        functools.partial(start_kernel, levels - 1 - at * tall, per_owner),
        grid=(columns // block,),
        in_specs=[
            whole(slots.shape),
            whole(slots.shape),
            pl.BlockSpec((fields, tall, block), lambda i: (0, at, i)),
            pl.BlockSpec((1, block), lambda i: (0, i)),
            rows,
            rows,
        ],
        out_specs=[whole(tiles), whole(tiles), whole(asked), rows, rows],
        out_shape=[
            jax.ShapeDtypeStruct(tiles, jnp.int32),
            jax.ShapeDtypeStruct(tiles, jnp.int32),
            jax.ShapeDtypeStruct(asked, jnp.int32),
            jax.ShapeDtypeStruct((fields, columns), jnp.float32),
            jax.ShapeDtypeStruct((fields, columns), jnp.float32),
        ],
        compiler_params=first_params,
        name="requests_and_rates",
    )(slots, parents, profiles, drag_factor.reshape(1, columns), surface_before, downward)


def atmos_kernel(mix_ref, tend_ref, *refs):
    mix = mix_ref[...]
    lowest = mix[:, mix.shape[1] - 1 :].astype(jnp.float32)
    out_ref = refs[-1]
    for member, x_ref in enumerate(refs[:-1]):
        mixed = jnp.dot(mix, x_ref[0], preferred_element_type=jnp.float32)
        out_ref[member] = (mixed + lowest * tend_ref[member : member + 1, :]).astype(jnp.bfloat16)


def diffuse_atmos(profiles, mixing, tendency):
    fields, levels, columns = profiles.shape
    block = min(2048, columns)

    def field(member):
        return pl.BlockSpec((1, levels, block), lambda i: (member, 0, i))

    return pl.pallas_call(
        atmos_kernel,
        grid=(columns // block,),
        in_specs=[
            pl.BlockSpec((levels, levels), lambda i: (0, 0)),
            pl.BlockSpec((fields, block), lambda i: (0, i)),
        ]
        + [field(member) for member in range(fields)],
        out_specs=pl.BlockSpec((fields, levels, block), lambda i: (0, 0, i)),
        out_shape=jax.ShapeDtypeStruct(profiles.shape, jnp.bfloat16),
        compiler_params=stream_params,
        cost_estimate=pl.CostEstimate(
            flops=2 * fields * levels * levels * columns,
            bytes_accessed=4 * fields * levels * columns,
            transcendentals=0,
        ),
        name="diffuse_atmos",
    )(mixing, tendency, *[profiles] * fields)


def level_specs(levels, fields, block):
    count = 4 if levels % 4 == 0 else 1

    def part(number):
        return pl.BlockSpec((levels // count, fields, block), lambda i: (number, 0, i))

    return [part(number) for number in range(count)]


def top_kernel(mix_ref, *refs):
    state_refs, base_ref, first_ref = refs[:-2], refs[-2], refs[-1]
    total = None
    level = 0
    for ref in state_refs:
        for inner in range(ref.shape[0]):
            term = mix_ref[0, level] * ref[inner]
            total = term if total is None else total + term
            level += 1
    base_ref[...] = total
    first_ref[...] = state_refs[0][0]


def top_level(state, mixing):
    levels, fields, cells = state.shape
    block = min(2048, cells)
    specs = level_specs(levels, fields, block)
    return pl.pallas_call(
        top_kernel,
        grid=(cells // block,),
        in_specs=[smem] + specs,
        out_specs=[pl.BlockSpec((fields, block), lambda i: (0, i))] * 2,
        out_shape=[jax.ShapeDtypeStruct((fields, cells), jnp.float32)] * 2,
        compiler_params=stream_params,
        cost_estimate=pl.CostEstimate(
            flops=2 * fields * levels * cells,
            bytes_accessed=4 * fields * levels * cells,
            transcendentals=0,
        ),
        name="top_level",
    )(mixing, *[state] * len(specs))


def serve_kernel(
    per_owner,
    far_ref,
    asked_ref,
    own_ref,
    other_ref,
    out_ref,
    blocks_ref,
    filled_ref,
    arrived_sem,
    sent_sem,
):
    copies = [
        pltpu.make_async_copy(ref, blocks_ref.at[index], arrived_sem.at[index])
        for index, ref in enumerate((own_ref, other_ref))
    ]
    for copy in copies:
        copy.start()
    for copy in copies:
        copy.wait()
    far = far_ref[0]

    def body(peer, carry):
        for shard in range(2):
            for slot in range(per_owner):
                spot = shard * per_owner + slot
                filled_ref[peer, spot] = blocks_ref[
                    shard ^ far, :, window(asked_ref[peer, spot])
                ]
        return carry

    sends = []
    parts = sent_sem.shape[0]
    peers = filled_ref.shape[0] // parts
    for part in range(parts):
        lax.fori_loop(part * peers, (part + 1) * peers, body, 0)
        at = pl.ds(part * peers, peers)
        send = pltpu.make_async_copy(filled_ref.at[at], out_ref.at[at], sent_sem.at[part])
        send.start()
        sends.append(send)
    for send in sends:
        send.wait()


def split_high(values):
    high = values.astype(jnp.bfloat16).astype(jnp.float32)
    return jnp.concatenate([high, values - high], axis=0)


GROUP = 8


def hot_kernel(
    place_ref,
    column_ref,
    atmos_weight_ref,
    mask_ref,
    hot_ref,
    share_ref,
    lanes_ref,
    *sums,
):
    intersections, cells = column_ref.shape
    windows = cells // LANES
    fields = share_ref.shape[1]
    group_tiles = GROUP * intersections
    steps = LANES // intersections
    group = pl.program_id(0)
    @pl.when(group == 0)
    def _():
        for ref in sums:
            ref[...] = jnp.zeros(ref.shape, jnp.float32)
        for first in range(0, windows, steps):
            tall = jnp.concatenate(
                [
                    column_ref[:, (first + step) * LANES : (first + step + 1) * LANES] & (LANES - 1)
                    for step in range(steps)
                ],
                axis=0,
            )
            turned = tall.astype(jnp.float32).T.astype(jnp.bfloat16)
            for part in range(steps // GROUP):
                lanes_ref[first // GROUP + part, :, :group_tiles] = turned[
                    :, part * group_tiles : (part + 1) * group_tiles
                ]

    column_ids = lax.broadcasted_iota(jnp.int32, (LANES, LANES), 1)
    column_ids = column_ids.astype(jnp.float32).astype(jnp.bfloat16)
    one, zero = jnp.bfloat16(1.0), jnp.bfloat16(0.0)
    field_ids = lax.broadcasted_iota(jnp.int32, (fields, LANES), 0)
    share_rows = lax.broadcasted_iota(jnp.int32, (2 * intersections, LANES), 0)
    first_half = share_rows % intersections < 2

    turned = lanes_ref[group]
    for inner in range(GROUP):
        step = group * GROUP + inner
        here = window(step)
        share = atmos_weight_ref[:, here] * mask_ref[:, here].astype(jnp.float32)
        hot = []
        for k in range(intersections):
            tile = inner * intersections + k
            lane_of = jnp.broadcast_to(turned[:, tile : tile + 1], (LANES, LANES))
            hot.append(jnp.where(lane_of == column_ids, one, zero))
        hot = jnp.concatenate(
            [
                jnp.concatenate([hot[0], hot[1]], axis=1),
                jnp.concatenate([hot[2], hot[3]], axis=1),
            ],
            axis=0,
        )
        hot_ref[inner] = hot
        parts = split_high(share)
        rows = jnp.concatenate(
            [jnp.where(first_half, parts, 0.0), jnp.where(first_half, 0.0, parts)], axis=1
        ).astype(jnp.bfloat16)
        spread = jnp.dot(rows, hot, preferred_element_type=jnp.float32)
        for k in range(intersections):
            side = slice((k % 2) * LANES, (k % 2 + 1) * LANES)
            low = intersections + k
            shared = spread[k : k + 1, side] + spread[low : low + 1, side]
            place = place_ref[k, step]
            sums[k][lax.div(place, fields)] += jnp.where(
                field_ids == lax.rem(place, fields), shared, 0.0
            )

    @pl.when(group == pl.num_programs(0) - 1)
    def _():
        total = sums[0][...]
        for ref in sums[1:]:
            total = total + ref[...]
        share_ref[...] = total


def middle_kernel(
    far_ref,
    place_ref,
    spot_ref,
    mix_ref,
    arrived_ref,
    column_ref,
    ocean_weight_ref,
    atmos_weight_ref,
    mask_ref,
    base_ref,
    state_ref,
    hot_ref,
    share_ref,
    forcing_ref,
    away_ref,
    home_ref,
    value_ref,
    held_ref,
    held_sem,
    sent_sem,
):
    intersections, cells = column_ref.shape
    windows = cells // LANES
    fields = base_ref.shape[0]
    near, packed = away_ref.shape[:2]
    per_owner = packed * fields // (fields + 1)
    rows = per_owner // fields

    def fetch(group):
        part = pl.ds(group * GROUP, GROUP)
        return pltpu.make_async_copy(hot_ref.at[part], held_ref.at[part], held_sem.at[group])

    groups = windows // GROUP
    ahead = min(3, groups)
    for group in range(ahead):
        fetch(group).start()
    value_ref[...] = jnp.zeros(value_ref.shape, jnp.float32)
    corner = mix_ref[0, 0]
    blank = jnp.zeros((2 * fields, LANES), jnp.float32)

    def body(group, carry):
        fetch(group).wait()

        @pl.when(group + ahead < groups)
        def _():
            fetch(group + ahead).start()

        for inner in range(GROUP):
            step = group * GROUP + inner
            here = window(step)
            lanes = column_ref[:, here] & (LANES - 1)
            ocean_weight = ocean_weight_ref[:, here]
            total = jnp.zeros((fields, LANES), jnp.float32)
            weight = jnp.zeros((1, LANES), jnp.float32)
            for k in range(intersections):
                picked = jnp.take_along_axis(
                    arrived_ref[spot_ref[k, step]],
                    jnp.broadcast_to(lanes[k : k + 1], (fields, LANES)),
                    axis=1,
                    mode="promise_in_bounds",
                )
                total = total + ocean_weight[k : k + 1] * picked
                weight = weight + ocean_weight[k : k + 1]
            forcing = total / weight
            forcing_ref[:, here] = forcing
            mask = mask_ref[:, here]
            surface = jnp.where(
                mask == 1, base_ref[:, here] + corner * forcing, state_ref[:, here]
            )
            share = atmos_weight_ref[:, here] * mask.astype(jnp.float32)
            parts = [split_high(share[k : k + 1] * surface) for k in range(intersections)]
            left = [parts[0], parts[1], blank, blank]
            right = [blank, blank, parts[2], parts[3]]
            parts = jnp.concatenate(
                [jnp.concatenate(left, axis=0), jnp.concatenate(right, axis=0)], axis=1
            ).astype(jnp.bfloat16)
            spread = jnp.dot(parts, held_ref[step], preferred_element_type=jnp.float32)
            for k in range(intersections):
                side = slice((k % 2) * LANES, (k % 2 + 1) * LANES)
                at = 2 * fields * k
                value_ref[place_ref[k, step]] = (
                    spread[at : at + fields, side] + spread[at + fields : at + 2 * fields, side]
                )
        return carry

    lax.fori_loop(0, windows // GROUP, body, 0)
    far = far_ref[0]
    shards = value_ref.reshape(2, near, per_owner, fields, LANES)
    copies = []
    for index, (ref, shard) in enumerate(((away_ref, 1 - far), (home_ref, far))):
        copies.append(
            pltpu.make_async_copy(
                shards.at[shard], ref.at[:, pl.ds(0, per_owner)], sent_sem.at[2 * index]
            )
        )
        copies.append(
            pltpu.make_async_copy(
                share_ref.at[shard],
                ref.at[:, pl.ds(per_owner, rows)],
                sent_sem.at[2 * index + 1],
            )
        )
    for copy in copies:
        copy.start()
    for copy in copies:
        copy.wait()


def ocean_kernel(mix_ref, forcing_ref, mask_ref, *refs):
    x_refs, (out_ref, high_ref, low_ref) = refs[:-3], refs[-3:]
    levels, fields, block = out_ref.shape
    rows = levels * fields

    @pl.when(pl.program_id(0) == 0)
    def _():
        level = lax.broadcasted_iota(jnp.int32, (rows, levels), 0) // fields
        pick = (level == lax.broadcasted_iota(jnp.int32, (rows, levels), 1)).astype(jnp.float32)
        tall = jnp.dot(pick, mix_ref[...], precision=lax.Precision.HIGHEST)
        wide = lax.dot_general(
            tall, pick, (((1,), (1,)), ((), ())), precision=lax.Precision.HIGHEST
        )
        down = lax.broadcasted_iota(jnp.int32, (rows, rows), 0) % fields
        across = lax.broadcasted_iota(jnp.int32, (rows, rows), 1) % fields
        wide = jnp.where(down == across, wide, 0.0)
        high = wide.astype(jnp.bfloat16)
        high_ref[...] = high
        low_ref[...] = (wide - high.astype(jnp.float32)).astype(jnp.bfloat16)

    flat = jnp.concatenate(
        [ref[...].reshape(rows // len(x_refs), block) for ref in x_refs], axis=0
    )
    push = jnp.concatenate(
        [forcing_ref[...], jnp.zeros((rows - fields, block), jnp.float32)], axis=0
    )
    loaded = flat + push
    high = loaded.astype(jnp.bfloat16)
    low = (loaded - high.astype(jnp.float32)).astype(jnp.bfloat16)
    mixed = (
        jnp.dot(high_ref[...], high, preferred_element_type=jnp.float32)
        + jnp.dot(high_ref[...], low, preferred_element_type=jnp.float32)
        + jnp.dot(low_ref[...], high, preferred_element_type=jnp.float32)
    )
    out_ref[...] = jnp.where(mask_ref[...] == 1, mixed, flat).reshape(levels, fields, block)


def diffuse_ocean(state, mixing, forcing, mask):
    levels, fields, cells = state.shape
    block = min(1024, cells)
    rows = levels * fields
    specs = level_specs(levels, fields, block)
    return pl.pallas_call(
        ocean_kernel,
        grid=(cells // block,),
        in_specs=[
            pl.BlockSpec(mixing.shape, lambda i: (0, 0)),
            pl.BlockSpec((fields, block), lambda i: (0, i)),
            pl.BlockSpec((1, block), lambda i: (0, i)),
        ]
        + specs,
        out_specs=pl.BlockSpec((levels, fields, block), lambda i: (0, 0, i)),
        out_shape=jax.ShapeDtypeStruct(state.shape, jnp.float32),
        scratch_shapes=[pltpu.VMEM((rows, rows), jnp.bfloat16)] * 2,
        compiler_params=stream_params,
        cost_estimate=pl.CostEstimate(
            flops=6 * rows * rows * cells,
            bytes_accessed=8 * rows * cells,
            transcendentals=0,
        ),
        name="diffuse_ocean",
    )(mixing, forcing, mask, *[state] * len(specs))


def collect_kernel(per_owner, far_ref, asked_ref, back_ref, *refs):
    near, _, fields, _ = back_ref.shape
    chains = 4
    sums = refs[-2 * chains :]
    rest = refs[: -2 * chains]
    home = len(rest) > 1
    columns = sums[0].shape[1]
    quarter = columns // fields
    far = far_ref[0]
    first = (far if home else 1 - far) * per_owner
    for ref in sums:
        ref[...] = jnp.zeros(ref.shape, jnp.float32)

    def body(step, carry):
        for slot in range(per_owner):
            for chain in range(chains):
                peer = step * chains + chain
                at = window(asked_ref[peer, first + slot])
                tile, row = per_owner + slot // fields, slot % fields
                sums[chain][:, at] += back_ref[peer, slot]
                sums[chains + chain][:, at] += back_ref[peer, tile, row : row + 1]
        return carry

    lax.fori_loop(0, near // chains, body, 0)
    values, shares = sums[0][...], sums[chains][...]
    for chain in range(1, chains):
        values = values + sums[chain][...]
        shares = shares + sums[chains + chain][...]
    out_ref = rest[-1]
    if home:
        other_ref, land_weight_ref, land_ref = rest[:3]
        land_weight = land_weight_ref[...]
        total = values + other_ref[:, :columns] + land_weight * land_ref[...]
        weight = shares + land_weight
        for row in range(fields):
            part = slice(row * quarter, (row + 1) * quarter)
            other_shares = other_ref[row : row + 1, columns:]
            out_ref[:, part] = total[:, part] / (weight[:, part] + other_shares)
    else:
        out_ref[:, :columns] = values
        for row in range(fields):
            out_ref[row : row + 1, columns:] = shares[:, row * quarter : (row + 1) * quarter]


def collect(asked, far, back, per_owner, columns, rest):
    fields = back.shape[2]
    chains = 4
    width = columns if rest else columns + columns // fields
    return pl.pallas_call(
        functools.partial(collect_kernel, per_owner),
        in_specs=[smem, smem, vmem] + [vmem] * len(rest),
        out_specs=vmem,
        out_shape=jax.ShapeDtypeStruct((fields, width), jnp.float32),
        scratch_shapes=[pltpu.VMEM((fields, columns), jnp.float32)] * chains
        + [pltpu.VMEM((1, columns), jnp.float32)] * chains,
        compiler_params=params,
        name="surface_state" if rest else "collect_away",
    )(far, asked, back, *rest)


def per_device(
    atmos_profiles,
    atmos_mixing,
    drag_factor,
    surface_before,
    downward_fluxes,
    land_weight,
    land_surface,
    ocean_state,
    ocean_mixing,
    sea_mask,
    exchange_slot,
    parent_column,
    ocean_weight,
    atmos_weight,
):
    near = lax.axis_size("near") * lax.axis_size("sub")
    devices = 2 * near
    fields, _, columns = atmos_profiles.shape
    intersections, cells = exchange_slot.shape
    capacity = 2 * intersections * cells // devices
    per_owner = capacity // LANES
    spots = 2 * per_owner
    mask = sea_mask.reshape(1, cells)
    state = ocean_state.transpose(1, 0, 2)
    far = lax.axis_index("far").astype(jnp.int32).reshape(1)

    def to_near(values):
        return lax.all_to_all(values, ("near", "sub"), split_axis=0, concat_axis=0, tiled=True)

    def to_far(values):
        return lax.ppermute(values, "far", ((0, 1), (1, 0)))

    place, spot, wanted, forcing_rows, tendency = start(
        near,
        per_owner,
        exchange_slot,
        parent_column,
        atmos_profiles,
        drag_factor,
        surface_before,
        downward_fluxes,
    )
    asked = to_near(wanted)
    other_rows = to_far(forcing_rows)
    base, first_level = top_level(state, ocean_mixing)
    asked, base, first_level = lax.optimization_barrier((asked, base, first_level))
    served = pl.pallas_call(
        functools.partial(serve_kernel, per_owner),
        in_specs=[smem, smem, hbm, hbm],
        out_specs=hbm,
        out_shape=jax.ShapeDtypeStruct((near, spots, fields, LANES), jnp.float32),
        scratch_shapes=[
            pltpu.VMEM((2, fields, columns), jnp.float32),
            pltpu.VMEM((near, spots, fields, LANES), jnp.float32),
            pltpu.SemaphoreType.DMA((2,)),
            pltpu.SemaphoreType.DMA((4,)),
        ],
        compiler_params=params,
        name="serve_windows",
    )(far, asked, forcing_rows, other_rows)
    served, columns_asked = lax.optimization_barrier((served, parent_column))
    arrived = to_near(served)
    rows = per_owner // fields
    windows = cells // LANES
    hot, shares = pl.pallas_call(
        hot_kernel,
        grid=(windows // GROUP,),
        in_specs=[smem] + [vmem] * 3,
        out_specs=[
            pl.BlockSpec((GROUP, 2 * LANES, 2 * LANES), lambda i: (i, 0, 0)),
            pl.BlockSpec((2 * near * rows, fields, LANES), lambda i: (0, 0, 0)),
        ],
        out_shape=[
            jax.ShapeDtypeStruct((windows, 2 * LANES, 2 * LANES), jnp.bfloat16),
            jax.ShapeDtypeStruct((2 * near * rows, fields, LANES), jnp.float32),
        ],
        scratch_shapes=[pltpu.VMEM((windows // GROUP, LANES, LANES), jnp.bfloat16)]
        + [pltpu.VMEM((2 * near * rows, fields, LANES), jnp.float32)] * intersections,
        compiler_params=middle_params,
        name="one_hot_and_shares",
    )(place, columns_asked, atmos_weight, mask)
    arrived, hot, shares = lax.optimization_barrier((arrived, hot, shares))
    sent = (near, per_owner + rows, fields, LANES)
    forcing, away, home = pl.pallas_call(
        middle_kernel,
        in_specs=[smem] * 4 + [vmem] * 7 + [hbm, vmem],
        out_specs=[vmem, hbm, hbm],
        out_shape=[
            jax.ShapeDtypeStruct((fields, cells), jnp.float32),
            jax.ShapeDtypeStruct(sent, jnp.float32),
            jax.ShapeDtypeStruct(sent, jnp.float32),
        ],
        scratch_shapes=[
            pltpu.VMEM((near * spots, fields, LANES), jnp.float32),
            pltpu.VMEM((windows, 2 * LANES, 2 * LANES), jnp.bfloat16),
            pltpu.SemaphoreType.DMA((windows // GROUP,)),
            pltpu.SemaphoreType.DMA((4,)),
        ],
        compiler_params=middle_params,
        name="forcing_and_windows",
    )(
        far,
        place,
        spot,
        ocean_mixing,
        arrived.reshape(near * spots, fields, LANES),
        parent_column,
        ocean_weight,
        atmos_weight,
        mask,
        base,
        first_level,
        hot,
        shares.reshape(2, near, rows, fields, LANES),
    )
    tendency, forcing = lax.optimization_barrier((tendency, forcing))
    atmos_updated = diffuse_atmos(atmos_profiles, atmos_mixing, tendency)
    back_away, atmos_updated, home = lax.optimization_barrier(
        (to_near(away), atmos_updated, home)
    )
    back_home = to_near(home)
    sums_away = collect(asked, far, back_away, per_owner, columns, ())
    other_sums = to_far(sums_away)
    ocean_updated = diffuse_ocean(state, ocean_mixing, forcing, mask).transpose(1, 0, 2)
    back_home, ocean_updated = lax.optimization_barrier((back_home, ocean_updated))
    surface_state = collect(
        asked,
        far,
        back_home,
        per_owner,
        columns,
        (other_sums, land_weight.reshape(1, columns), land_surface),
    )
    return (atmos_updated, ocean_updated, surface_state)


def solution(mesh):
    comp, sub = mesh.devices.shape
    halves = jax.sharding.Mesh(mesh.devices.reshape(2, comp // 2, sub), AXES)
    split = P(None, AXES)
    return jax.shard_map(
        per_device,
        mesh=halves,
        in_specs=(
            P(None, None, AXES),
            P(),
            P(AXES),
            split,
            split,
            P(AXES),
            split,
            P(None, None, AXES),
            P(),
            P(AXES),
            split,
            split,
            split,
            split,
        ),
        out_specs=(P(None, None, AXES), P(None, None, AXES), split),
        check_vma=False,
    )
```

```python
import functools

import jax
import jax.numpy as jnp
from jax import lax
from jax.experimental import pallas as pl
from jax.experimental.pallas import tpu as pltpu
from jax.sharding import PartitionSpec as P

couple_rate = 0.5
LANES = 128
params = pltpu.CompilerParams(vmem_limit_bytes=24 * 1024 * 1024)
stream_params = pltpu.CompilerParams(vmem_limit_bytes=52 * 1024 * 1024)
middle_params = pltpu.CompilerParams(vmem_limit_bytes=48 * 1024 * 1024)
first_params = pltpu.CompilerParams(vmem_limit_bytes=56 * 1024 * 1024)
vmem = pl.BlockSpec(memory_space=pltpu.VMEM)
smem = pl.BlockSpec(memory_space=pltpu.SMEM)
hbm = pl.BlockSpec(memory_space=pl.ANY)
AXES = ("far", "near", "sub")


def window(index):
    return pl.ds(pl.multiple_of(index * LANES, LANES), LANES)


def make_requests(per_owner, slot_ref, column_ref, place_ref, spot_ref, wanted_ref):
    intersections, cells = slot_ref.shape
    near, spots = wanted_ref.shape
    windows = cells // LANES
    lane = lax.broadcasted_iota(jnp.int32, (intersections, windows), 1)

    def heads(ref):
        found = jnp.zeros((intersections, windows), jnp.int32)
        for step in range(windows):
            head = ref[:, step * LANES : step * LANES + 1]
            found = jnp.where(lane == step, head, found)
        return found // LANES

    place = heads(slot_ref)
    column_window = heads(column_ref)
    owner = place // per_owner
    peer = owner % near
    spot = owner // near * per_owner + place % per_owner
    place_ref[...] = place
    spot_ref[...] = peer * spots + spot
    peer_ids = lax.broadcasted_iota(jnp.int32, (near, windows), 0)
    spot_ids = lax.broadcasted_iota(jnp.int32, (spots, windows), 0)
    wanted = jnp.zeros((near, spots), jnp.float32)
    for k in range(intersections):
        row = slice(k, k + 1)
        peer_hot = jnp.where(peer_ids == peer[row], 1.0, 0.0)
        spot_hot = jnp.where(
            spot_ids == spot[row], column_window[row].astype(jnp.float32), 0.0
        )
        wanted = wanted + lax.dot_general(
            peer_hot.astype(jnp.bfloat16),
            spot_hot.astype(jnp.bfloat16),
            (((1,), (1,)), ((), ())),
            preferred_element_type=jnp.float32,
        )
    wanted_ref[...] = wanted.astype(jnp.int32)


def start_kernel(
    last,
    per_owner,
    slot_ref,
    column_ref,
    x_ref,
    drag_ref,
    before_ref,
    down_ref,
    place_ref,
    spot_ref,
    wanted_ref,
    forcing_ref,
    tend_ref,
):
    @pl.when(pl.program_id(0) == 0)
    def _():
        make_requests(per_owner, slot_ref, column_ref, place_ref, spot_ref, wanted_ref)

    def row(ref, index):
        return ref[index : index + 1, :]

    bottom = [x_ref[member].astype(jnp.float32)[last : last + 1, :] for member in range(4)]
    east = bottom[2] - row(before_ref, 2)
    north = bottom[3] - row(before_ref, 3)
    transfer = drag_ref[...] * jnp.sqrt(1.0 + east * east + north * north)
    sensible = transfer * (row(before_ref, 0) - bottom[0])
    latent = transfer * (row(before_ref, 1) - bottom[1])
    east_stress = couple_rate * (transfer * east)
    north_stress = couple_rate * (transfer * north)
    forcing_ref[0:1, :] = couple_rate * (
        row(down_ref, 0) + row(down_ref, 1) - sensible - latent
    )
    forcing_ref[1:2, :] = couple_rate * (latent - row(down_ref, 2) - row(down_ref, 3))
    forcing_ref[2:3, :] = east_stress
    forcing_ref[3:4, :] = north_stress
    tend_ref[0:1, :] = couple_rate * sensible
    tend_ref[1:2, :] = couple_rate * latent
    tend_ref[2:3, :] = -east_stress
    tend_ref[3:4, :] = -north_stress


def start(near, per_owner, slots, parents, profiles, drag_factor, surface_before, downward):
    fields, levels, columns = profiles.shape
    intersections, cells = slots.shape
    block = min(4096, columns)
    tall = 16
    at = (levels - 1) // tall
    rows = pl.BlockSpec((fields, block), lambda i: (0, i))
    tiles = (intersections, cells // LANES)
    asked = (near, 2 * per_owner)

    def whole(shape):
        return pl.BlockSpec(shape, lambda i: (0, 0))

    return pl.pallas_call(
        functools.partial(start_kernel, levels - 1 - at * tall, per_owner),
        grid=(columns // block,),
        in_specs=[
            whole(slots.shape),
            whole(slots.shape),
            pl.BlockSpec((fields, tall, block), lambda i: (0, at, i)),
            pl.BlockSpec((1, block), lambda i: (0, i)),
            rows,
            rows,
        ],
        out_specs=[whole(tiles), whole(tiles), whole(asked), rows, rows],
        out_shape=[
            jax.ShapeDtypeStruct(tiles, jnp.int32),
            jax.ShapeDtypeStruct(tiles, jnp.int32),
            jax.ShapeDtypeStruct(asked, jnp.int32),
            jax.ShapeDtypeStruct((fields, columns), jnp.float32),
            jax.ShapeDtypeStruct((fields, columns), jnp.float32),
        ],
        compiler_params=first_params,
        name="requests_and_rates",
    )(slots, parents, profiles, drag_factor.reshape(1, columns), surface_before, downward)


def atmos_kernel(mix_ref, tend_ref, *refs):
    mix = mix_ref[...]
    lowest = mix[:, mix.shape[1] - 1 :].astype(jnp.float32)
    out_ref = refs[-1]
    for member, x_ref in enumerate(refs[:-1]):
        mixed = jnp.dot(mix, x_ref[0], preferred_element_type=jnp.float32)
        out_ref[member] = (mixed + lowest * tend_ref[member : member + 1, :]).astype(jnp.bfloat16)


def diffuse_atmos(profiles, mixing, tendency):
    fields, levels, columns = profiles.shape
    block = min(2048, columns)

    def field(member):
        return pl.BlockSpec((1, levels, block), lambda i: (member, 0, i))

    return pl.pallas_call(
        atmos_kernel,
        grid=(columns // block,),
        in_specs=[
            pl.BlockSpec((levels, levels), lambda i: (0, 0)),
            pl.BlockSpec((fields, block), lambda i: (0, i)),
        ]
        + [field(member) for member in range(fields)],
        out_specs=pl.BlockSpec((fields, levels, block), lambda i: (0, 0, i)),
        out_shape=jax.ShapeDtypeStruct(profiles.shape, jnp.bfloat16),
        compiler_params=stream_params,
        cost_estimate=pl.CostEstimate(
            flops=2 * fields * levels * levels * columns,
            bytes_accessed=4 * fields * levels * columns,
            transcendentals=0,
        ),
        name="diffuse_atmos",
    )(mixing, tendency, *[profiles] * fields)


def level_specs(levels, fields, block):
    count = 4 if levels % 4 == 0 else 1

    def part(number):
        return pl.BlockSpec((levels // count, fields, block), lambda i: (number, 0, i))

    return [part(number) for number in range(count)]


def top_kernel(mix_ref, *refs):
    state_refs, base_ref, first_ref = refs[:-2], refs[-2], refs[-1]
    total = None
    level = 0
    for ref in state_refs:
        for inner in range(ref.shape[0]):
            term = mix_ref[0, level] * ref[inner]
            total = term if total is None else total + term
            level += 1
    base_ref[...] = total
    first_ref[...] = state_refs[0][0]


def top_level(state, mixing):
    levels, fields, cells = state.shape
    block = min(2048, cells)
    specs = level_specs(levels, fields, block)
    return pl.pallas_call(
        top_kernel,
        grid=(cells // block,),
        in_specs=[smem] + specs,
        out_specs=[pl.BlockSpec((fields, block), lambda i: (0, i))] * 2,
        out_shape=[jax.ShapeDtypeStruct((fields, cells), jnp.float32)] * 2,
        compiler_params=stream_params,
        cost_estimate=pl.CostEstimate(
            flops=2 * fields * levels * cells,
            bytes_accessed=4 * fields * levels * cells,
            transcendentals=0,
        ),
        name="top_level",
    )(mixing, *[state] * len(specs))


def serve_kernel(
    per_owner,
    far_ref,
    asked_ref,
    own_ref,
    other_ref,
    out_ref,
    blocks_ref,
    filled_ref,
    arrived_sem,
    sent_sem,
):
    copies = [
        pltpu.make_async_copy(ref, blocks_ref.at[index], arrived_sem.at[index])
        for index, ref in enumerate((own_ref, other_ref))
    ]
    for copy in copies:
        copy.start()
    for copy in copies:
        copy.wait()
    far = far_ref[0]

    def body(peer, carry):
        for shard in range(2):
            for slot in range(per_owner):
                spot = shard * per_owner + slot
                filled_ref[peer, spot] = blocks_ref[
                    shard ^ far, :, window(asked_ref[peer, spot])
                ]
        return carry

    sends = []
    parts = sent_sem.shape[0]
    peers = filled_ref.shape[0] // parts
    for part in range(parts):
        lax.fori_loop(part * peers, (part + 1) * peers, body, 0)
        at = pl.ds(part * peers, peers)
        send = pltpu.make_async_copy(filled_ref.at[at], out_ref.at[at], sent_sem.at[part])
        send.start()
        sends.append(send)
    for send in sends:
        send.wait()


def split_high(values):
    high = values.astype(jnp.bfloat16).astype(jnp.float32)
    return jnp.concatenate([high, values - high], axis=0)


GROUP = 8


def hot_kernel(
    place_ref,
    column_ref,
    atmos_weight_ref,
    mask_ref,
    hot_ref,
    share_ref,
    lanes_ref,
    *sums,
):
    intersections, cells = column_ref.shape
    windows = cells // LANES
    fields = share_ref.shape[1]
    group_tiles = GROUP * intersections
    steps = LANES // intersections
    group = pl.program_id(0)
    @pl.when(group == 0)
    def _():
        for ref in sums:
            ref[...] = jnp.zeros(ref.shape, jnp.float32)
        for first in range(0, windows, steps):
            tall = jnp.concatenate(
                [
                    column_ref[:, (first + step) * LANES : (first + step + 1) * LANES] & (LANES - 1)
                    for step in range(steps)
                ],
                axis=0,
            )
            turned = tall.astype(jnp.float32).T.astype(jnp.bfloat16)
            for part in range(steps // GROUP):
                lanes_ref[first // GROUP + part, :, :group_tiles] = turned[
                    :, part * group_tiles : (part + 1) * group_tiles
                ]

    column_ids = lax.broadcasted_iota(jnp.int32, (LANES, LANES), 1)
    column_ids = column_ids.astype(jnp.float32).astype(jnp.bfloat16)
    one, zero = jnp.bfloat16(1.0), jnp.bfloat16(0.0)
    field_ids = lax.broadcasted_iota(jnp.int32, (fields, LANES), 0)
    share_rows = lax.broadcasted_iota(jnp.int32, (2 * intersections, LANES), 0)
    first_half = share_rows % intersections < 2

    turned = lanes_ref[group]
    for inner in range(GROUP):
        step = group * GROUP + inner
        here = window(step)
        share = atmos_weight_ref[:, here] * mask_ref[:, here].astype(jnp.float32)
        hot = []
        for k in range(intersections):
            tile = inner * intersections + k
            lane_of = jnp.broadcast_to(turned[:, tile : tile + 1], (LANES, LANES))
            hot.append(jnp.where(lane_of == column_ids, one, zero))
        hot = jnp.concatenate(
            [
                jnp.concatenate([hot[0], hot[1]], axis=1),
                jnp.concatenate([hot[2], hot[3]], axis=1),
            ],
            axis=0,
        )
        hot_ref[inner] = hot
        parts = split_high(share)
        rows = jnp.concatenate(
            [jnp.where(first_half, parts, 0.0), jnp.where(first_half, 0.0, parts)], axis=1
        ).astype(jnp.bfloat16)
        spread = jnp.dot(rows, hot, preferred_element_type=jnp.float32)
        for k in range(intersections):
            side = slice((k % 2) * LANES, (k % 2 + 1) * LANES)
            low = intersections + k
            shared = spread[k : k + 1, side] + spread[low : low + 1, side]
            place = place_ref[k, step]
            sums[k][lax.div(place, fields)] += jnp.where(
                field_ids == lax.rem(place, fields), shared, 0.0
            )

    @pl.when(group == pl.num_programs(0) - 1)
    def _():
        total = sums[0][...]
        for ref in sums[1:]:
            total = total + ref[...]
        share_ref[...] = total


def middle_kernel(
    far_ref,
    place_ref,
    spot_ref,
    mix_ref,
    arrived_ref,
    column_ref,
    ocean_weight_ref,
    atmos_weight_ref,
    mask_ref,
    base_ref,
    state_ref,
    hot_ref,
    share_ref,
    forcing_ref,
    away_ref,
    home_ref,
    value_ref,
    parts_ref,
    held_ref,
    held_sem,
    sent_sem,
):
    intersections, cells = column_ref.shape
    windows = cells // LANES
    fields = base_ref.shape[0]
    near, packed = away_ref.shape[:2]
    per_owner = packed * fields // (fields + 1)
    rows = per_owner // fields

    def fetch(group):
        part = pl.ds(group * GROUP, GROUP)
        return pltpu.make_async_copy(hot_ref.at[part], held_ref.at[part], held_sem.at[group])

    groups = windows // GROUP
    for group in range(groups):
        fetch(group).start()
    value_ref[...] = jnp.zeros(value_ref.shape, jnp.float32)
    corner = mix_ref[0, 0]
    blank = jnp.zeros((2 * fields, LANES), jnp.float32)

    def body(group, carry):
        for inner in range(GROUP):
            step = group * GROUP + inner
            here = window(step)
            lanes = column_ref[:, here] & (LANES - 1)
            ocean_weight = ocean_weight_ref[:, here]
            total = jnp.zeros((fields, LANES), jnp.float32)
            weight = jnp.zeros((1, LANES), jnp.float32)
            for k in range(intersections):
                picked = jnp.take_along_axis(
                    arrived_ref[spot_ref[k, step]],
                    jnp.broadcast_to(lanes[k : k + 1], (fields, LANES)),
                    axis=1,
                    mode="promise_in_bounds",
                )
                total = total + ocean_weight[k : k + 1] * picked
                weight = weight + ocean_weight[k : k + 1]
            forcing = total / weight
            forcing_ref[:, here] = forcing
            mask = mask_ref[:, here]
            surface = jnp.where(
                mask == 1, base_ref[:, here] + corner * forcing, state_ref[:, here]
            )
            share = atmos_weight_ref[:, here] * mask.astype(jnp.float32)
            parts = [split_high(share[k : k + 1] * surface) for k in range(intersections)]
            left = [parts[0], parts[1], blank, blank]
            right = [blank, blank, parts[2], parts[3]]
            parts = jnp.concatenate(
                [jnp.concatenate(left, axis=0), jnp.concatenate(right, axis=0)], axis=1
            ).astype(jnp.bfloat16)
            parts_ref[step] = parts
        return carry

    lax.fori_loop(0, groups, body, 0)

    def multiply(group, carry):
        fetch(group).wait()
        for inner in range(GROUP):
            step = group * GROUP + inner
            spread = jnp.dot(
                parts_ref[step], held_ref[step], preferred_element_type=jnp.float32
            )
            for k in range(intersections):
                side = slice((k % 2) * LANES, (k % 2 + 1) * LANES)
                at = 2 * fields * k
                value_ref[place_ref[k, step]] = (
                    spread[at : at + fields, side] + spread[at + fields : at + 2 * fields, side]
                )
        return carry

    lax.fori_loop(0, groups, multiply, 0)
    far = far_ref[0]
    shards = value_ref.reshape(2, near, per_owner, fields, LANES)
    copies = []
    for index, (ref, shard) in enumerate(((away_ref, 1 - far), (home_ref, far))):
        copies.append(
            pltpu.make_async_copy(
                shards.at[shard], ref.at[:, pl.ds(0, per_owner)], sent_sem.at[2 * index]
            )
        )
        copies.append(
            pltpu.make_async_copy(
                share_ref.at[shard],
                ref.at[:, pl.ds(per_owner, rows)],
                sent_sem.at[2 * index + 1],
            )
        )
    for copy in copies:
        copy.start()
    for copy in copies:
        copy.wait()


def ocean_kernel(mix_ref, forcing_ref, mask_ref, *refs):
    x_refs, (out_ref, high_ref, low_ref) = refs[:-3], refs[-3:]
    levels, fields, block = out_ref.shape
    rows = levels * fields

    @pl.when(pl.program_id(0) == 0)
    def _():
        level = lax.broadcasted_iota(jnp.int32, (rows, levels), 0) // fields
        pick = (level == lax.broadcasted_iota(jnp.int32, (rows, levels), 1)).astype(jnp.float32)
        tall = jnp.dot(pick, mix_ref[...], precision=lax.Precision.HIGHEST)
        wide = lax.dot_general(
            tall, pick, (((1,), (1,)), ((), ())), precision=lax.Precision.HIGHEST
        )
        down = lax.broadcasted_iota(jnp.int32, (rows, rows), 0) % fields
        across = lax.broadcasted_iota(jnp.int32, (rows, rows), 1) % fields
        wide = jnp.where(down == across, wide, 0.0)
        high = wide.astype(jnp.bfloat16)
        high_ref[...] = high
        low_ref[...] = (wide - high.astype(jnp.float32)).astype(jnp.bfloat16)

    flat = jnp.concatenate(
        [ref[...].reshape(rows // len(x_refs), block) for ref in x_refs], axis=0
    )
    push = jnp.concatenate(
        [forcing_ref[...], jnp.zeros((rows - fields, block), jnp.float32)], axis=0
    )
    loaded = flat + push
    high = loaded.astype(jnp.bfloat16)
    low = (loaded - high.astype(jnp.float32)).astype(jnp.bfloat16)
    mixed = (
        jnp.dot(high_ref[...], high, preferred_element_type=jnp.float32)
        + jnp.dot(high_ref[...], low, preferred_element_type=jnp.float32)
        + jnp.dot(low_ref[...], high, preferred_element_type=jnp.float32)
    )
    out_ref[...] = jnp.where(mask_ref[...] == 1, mixed, flat).reshape(levels, fields, block)


def diffuse_ocean(state, mixing, forcing, mask):
    levels, fields, cells = state.shape
    block = min(1024, cells)
    rows = levels * fields
    specs = level_specs(levels, fields, block)
    return pl.pallas_call(
        ocean_kernel,
        grid=(cells // block,),
        in_specs=[
            pl.BlockSpec(mixing.shape, lambda i: (0, 0)),
            pl.BlockSpec((fields, block), lambda i: (0, i)),
            pl.BlockSpec((1, block), lambda i: (0, i)),
        ]
        + specs,
        out_specs=pl.BlockSpec((levels, fields, block), lambda i: (0, 0, i)),
        out_shape=jax.ShapeDtypeStruct(state.shape, jnp.float32),
        scratch_shapes=[pltpu.VMEM((rows, rows), jnp.bfloat16)] * 2,
        compiler_params=stream_params,
        cost_estimate=pl.CostEstimate(
            flops=6 * rows * rows * cells,
            bytes_accessed=8 * rows * cells,
            transcendentals=0,
        ),
        name="diffuse_ocean",
    )(mixing, forcing, mask, *[state] * len(specs))


def collect_kernel(per_owner, far_ref, asked_ref, back_ref, *refs):
    near, _, fields, _ = back_ref.shape
    chains = 4
    sums = refs[-2 * chains :]
    rest = refs[: -2 * chains]
    home = len(rest) > 1
    columns = sums[0].shape[1]
    quarter = columns // fields
    far = far_ref[0]
    first = (far if home else 1 - far) * per_owner
    for ref in sums:
        ref[...] = jnp.zeros(ref.shape, jnp.float32)

    def body(step, carry):
        for slot in range(per_owner):
            for chain in range(chains):
                peer = step * chains + chain
                at = window(asked_ref[peer, first + slot])
                tile, row = per_owner + slot // fields, slot % fields
                sums[chain][:, at] += back_ref[peer, slot]
                sums[chains + chain][:, at] += back_ref[peer, tile, row : row + 1]
        return carry

    lax.fori_loop(0, near // chains, body, 0)
    values, shares = sums[0][...], sums[chains][...]
    for chain in range(1, chains):
        values = values + sums[chain][...]
        shares = shares + sums[chains + chain][...]
    out_ref = rest[-1]
    if home:
        other_ref, land_weight_ref, land_ref = rest[:3]
        land_weight = land_weight_ref[...]
        total = values + other_ref[:, :columns] + land_weight * land_ref[...]
        weight = shares + land_weight
        for row in range(fields):
            part = slice(row * quarter, (row + 1) * quarter)
            other_shares = other_ref[row : row + 1, columns:]
            out_ref[:, part] = total[:, part] / (weight[:, part] + other_shares)
    else:
        out_ref[:, :columns] = values
        for row in range(fields):
            out_ref[row : row + 1, columns:] = shares[:, row * quarter : (row + 1) * quarter]


def collect(asked, far, back, per_owner, columns, rest):
    fields = back.shape[2]
    chains = 4
    width = columns if rest else columns + columns // fields
    return pl.pallas_call(
        functools.partial(collect_kernel, per_owner),
        in_specs=[smem, smem, vmem] + [vmem] * len(rest),
        out_specs=vmem,
        out_shape=jax.ShapeDtypeStruct((fields, width), jnp.float32),
        scratch_shapes=[pltpu.VMEM((fields, columns), jnp.float32)] * chains
        + [pltpu.VMEM((1, columns), jnp.float32)] * chains,
        compiler_params=params,
        name="surface_state" if rest else "collect_away",
    )(far, asked, back, *rest)


def per_device(
    atmos_profiles,
    atmos_mixing,
    drag_factor,
    surface_before,
    downward_fluxes,
    land_weight,
    land_surface,
    ocean_state,
    ocean_mixing,
    sea_mask,
    exchange_slot,
    parent_column,
    ocean_weight,
    atmos_weight,
):
    near = lax.axis_size("near") * lax.axis_size("sub")
    devices = 2 * near
    fields, _, columns = atmos_profiles.shape
    intersections, cells = exchange_slot.shape
    capacity = 2 * intersections * cells // devices
    per_owner = capacity // LANES
    spots = 2 * per_owner
    mask = sea_mask.reshape(1, cells)
    state = ocean_state.transpose(1, 0, 2)
    far = lax.axis_index("far").astype(jnp.int32).reshape(1)

    def to_near(values):
        return lax.all_to_all(values, ("near", "sub"), split_axis=0, concat_axis=0, tiled=True)

    def to_far(values):
        return lax.ppermute(values, "far", ((0, 1), (1, 0)))

    place, spot, wanted, forcing_rows, tendency = start(
        near,
        per_owner,
        exchange_slot,
        parent_column,
        atmos_profiles,
        drag_factor,
        surface_before,
        downward_fluxes,
    )
    asked = to_near(wanted)
    other_rows = to_far(forcing_rows)
    base, first_level = top_level(state, ocean_mixing)
    asked, base, first_level = lax.optimization_barrier((asked, base, first_level))
    served = pl.pallas_call(
        functools.partial(serve_kernel, per_owner),
        in_specs=[smem, smem, hbm, hbm],
        out_specs=hbm,
        out_shape=jax.ShapeDtypeStruct((near, spots, fields, LANES), jnp.float32),
        scratch_shapes=[
            pltpu.VMEM((2, fields, columns), jnp.float32),
            pltpu.VMEM((near, spots, fields, LANES), jnp.float32),
            pltpu.SemaphoreType.DMA((2,)),
            pltpu.SemaphoreType.DMA((4,)),
        ],
        compiler_params=params,
        name="serve_windows",
    )(far, asked, forcing_rows, other_rows)
    served, columns_asked = lax.optimization_barrier((served, parent_column))
    arrived = to_near(served)
    rows = per_owner // fields
    windows = cells // LANES
    hot, shares = pl.pallas_call(
        hot_kernel,
        grid=(windows // GROUP,),
        in_specs=[smem] + [vmem] * 3,
        out_specs=[
            pl.BlockSpec((GROUP, 2 * LANES, 2 * LANES), lambda i: (i, 0, 0)),
            pl.BlockSpec((2 * near * rows, fields, LANES), lambda i: (0, 0, 0)),
        ],
        out_shape=[
            jax.ShapeDtypeStruct((windows, 2 * LANES, 2 * LANES), jnp.bfloat16),
            jax.ShapeDtypeStruct((2 * near * rows, fields, LANES), jnp.float32),
        ],
        scratch_shapes=[pltpu.VMEM((windows // GROUP, LANES, LANES), jnp.bfloat16)]
        + [pltpu.VMEM((2 * near * rows, fields, LANES), jnp.float32)] * intersections,
        compiler_params=middle_params,
        name="one_hot_and_shares",
    )(place, columns_asked, atmos_weight, mask)
    arrived, hot, shares = lax.optimization_barrier((arrived, hot, shares))
    sent = (near, per_owner + rows, fields, LANES)
    forcing, away, home = pl.pallas_call(
        middle_kernel,
        in_specs=[smem] * 4 + [vmem] * 7 + [hbm, vmem],
        out_specs=[vmem, hbm, hbm],
        out_shape=[
            jax.ShapeDtypeStruct((fields, cells), jnp.float32),
            jax.ShapeDtypeStruct(sent, jnp.float32),
            jax.ShapeDtypeStruct(sent, jnp.float32),
        ],
        scratch_shapes=[
            pltpu.VMEM((near * spots, fields, LANES), jnp.float32),
            pltpu.VMEM((windows, 2 * fields * intersections, 2 * LANES), jnp.bfloat16),
            pltpu.VMEM((windows, 2 * LANES, 2 * LANES), jnp.bfloat16),
            pltpu.SemaphoreType.DMA((windows // GROUP,)),
            pltpu.SemaphoreType.DMA((4,)),
        ],
        compiler_params=middle_params,
        name="forcing_and_windows",
    )(
        far,
        place,
        spot,
        ocean_mixing,
        arrived.reshape(near * spots, fields, LANES),
        parent_column,
        ocean_weight,
        atmos_weight,
        mask,
        base,
        first_level,
        hot,
        shares.reshape(2, near, rows, fields, LANES),
    )
    ocean_updated = diffuse_ocean(state, ocean_mixing, forcing, mask).transpose(1, 0, 2)
    back_away, ocean_updated, home = lax.optimization_barrier(
        (to_near(away), ocean_updated, home)
    )
    back_home = to_near(home)
    sums_away = collect(asked, far, back_away, per_owner, columns, ())
    tendency, sums_away = lax.optimization_barrier((tendency, sums_away))
    other_sums = to_far(sums_away)
    atmos_updated = diffuse_atmos(atmos_profiles, atmos_mixing, tendency)
    back_home, atmos_updated = lax.optimization_barrier((back_home, atmos_updated))
    surface_state = collect(
        asked,
        far,
        back_home,
        per_owner,
        columns,
        (other_sums, land_weight.reshape(1, columns), land_surface),
    )
    return (atmos_updated, ocean_updated, surface_state)


def solution(mesh):
    comp, sub = mesh.devices.shape
    halves = jax.sharding.Mesh(mesh.devices.reshape(2, comp // 2, sub), AXES)
    split = P(None, AXES)
    return jax.shard_map(
        per_device,
        mesh=halves,
        in_specs=(
            P(None, None, AXES),
            P(),
            P(AXES),
            split,
            split,
            P(AXES),
            split,
            P(None, None, AXES),
            P(),
            P(AXES),
            split,
            split,
            split,
            split,
        ),
        out_specs=(P(None, None, AXES), P(None, None, AXES), split),
        check_vma=False,
    )
```

```python
import functools

import jax
import jax.numpy as jnp
from jax import lax
from jax.experimental import pallas as pl
from jax.experimental.pallas import tpu as pltpu
from jax.sharding import PartitionSpec as P

couple_rate = 0.5
LANES = 128
params = pltpu.CompilerParams(vmem_limit_bytes=24 * 1024 * 1024)
stream_params = pltpu.CompilerParams(vmem_limit_bytes=52 * 1024 * 1024)
middle_params = pltpu.CompilerParams(vmem_limit_bytes=48 * 1024 * 1024)
first_params = pltpu.CompilerParams(vmem_limit_bytes=56 * 1024 * 1024)
vmem = pl.BlockSpec(memory_space=pltpu.VMEM)
smem = pl.BlockSpec(memory_space=pltpu.SMEM)
hbm = pl.BlockSpec(memory_space=pl.ANY)
AXES = ("far", "near", "sub")


def window(index):
    return pl.ds(pl.multiple_of(index * LANES, LANES), LANES)


def make_requests(per_owner, slot_ref, column_ref, place_ref, spot_ref, wanted_ref):
    intersections, cells = slot_ref.shape
    near, spots = wanted_ref.shape
    windows = cells // LANES
    lane = lax.broadcasted_iota(jnp.int32, (intersections, windows), 1)

    def heads(ref):
        found = jnp.zeros((intersections, windows), jnp.int32)
        for step in range(windows):
            head = ref[:, step * LANES : step * LANES + 1]
            found = jnp.where(lane == step, head, found)
        return found // LANES

    place = heads(slot_ref)
    column_window = heads(column_ref)
    owner = place // per_owner
    peer = owner % near
    spot = owner // near * per_owner + place % per_owner
    place_ref[...] = place
    spot_ref[...] = peer * spots + spot
    peer_ids = lax.broadcasted_iota(jnp.int32, (near, windows), 0)
    spot_ids = lax.broadcasted_iota(jnp.int32, (spots, windows), 0)
    wanted = jnp.zeros((near, spots), jnp.float32)
    for k in range(intersections):
        row = slice(k, k + 1)
        peer_hot = jnp.where(peer_ids == peer[row], 1.0, 0.0)
        spot_hot = jnp.where(
            spot_ids == spot[row], column_window[row].astype(jnp.float32), 0.0
        )
        wanted = wanted + lax.dot_general(
            peer_hot.astype(jnp.bfloat16),
            spot_hot.astype(jnp.bfloat16),
            (((1,), (1,)), ((), ())),
            preferred_element_type=jnp.float32,
        )
    wanted_ref[...] = wanted.astype(jnp.int32)


def start_kernel(
    last,
    per_owner,
    slot_ref,
    column_ref,
    x_ref,
    drag_ref,
    before_ref,
    down_ref,
    place_ref,
    spot_ref,
    wanted_ref,
    forcing_ref,
    tend_ref,
):
    @pl.when(pl.program_id(0) == 0)
    def _():
        make_requests(per_owner, slot_ref, column_ref, place_ref, spot_ref, wanted_ref)

    def row(ref, index):
        return ref[index : index + 1, :]

    bottom = [x_ref[member].astype(jnp.float32)[last : last + 1, :] for member in range(4)]
    east = bottom[2] - row(before_ref, 2)
    north = bottom[3] - row(before_ref, 3)
    transfer = drag_ref[...] * jnp.sqrt(1.0 + east * east + north * north)
    sensible = transfer * (row(before_ref, 0) - bottom[0])
    latent = transfer * (row(before_ref, 1) - bottom[1])
    east_stress = couple_rate * (transfer * east)
    north_stress = couple_rate * (transfer * north)
    forcing_ref[0:1, :] = couple_rate * (
        row(down_ref, 0) + row(down_ref, 1) - sensible - latent
    )
    forcing_ref[1:2, :] = couple_rate * (latent - row(down_ref, 2) - row(down_ref, 3))
    forcing_ref[2:3, :] = east_stress
    forcing_ref[3:4, :] = north_stress
    tend_ref[0:1, :] = couple_rate * sensible
    tend_ref[1:2, :] = couple_rate * latent
    tend_ref[2:3, :] = -east_stress
    tend_ref[3:4, :] = -north_stress


def start(near, per_owner, slots, parents, profiles, drag_factor, surface_before, downward):
    fields, levels, columns = profiles.shape
    intersections, cells = slots.shape
    block = min(4096, columns)
    tall = 16
    at = (levels - 1) // tall
    rows = pl.BlockSpec((fields, block), lambda i: (0, i))
    tiles = (intersections, cells // LANES)
    asked = (near, 2 * per_owner)

    def whole(shape):
        return pl.BlockSpec(shape, lambda i: (0, 0))

    return pl.pallas_call(
        functools.partial(start_kernel, levels - 1 - at * tall, per_owner),
        grid=(columns // block,),
        in_specs=[
            whole(slots.shape),
            whole(slots.shape),
            pl.BlockSpec((fields, tall, block), lambda i: (0, at, i)),
            pl.BlockSpec((1, block), lambda i: (0, i)),
            rows,
            rows,
        ],
        out_specs=[whole(tiles), whole(tiles), whole(asked), rows, rows],
        out_shape=[
            jax.ShapeDtypeStruct(tiles, jnp.int32),
            jax.ShapeDtypeStruct(tiles, jnp.int32),
            jax.ShapeDtypeStruct(asked, jnp.int32),
            jax.ShapeDtypeStruct((fields, columns), jnp.float32),
            jax.ShapeDtypeStruct((fields, columns), jnp.float32),
        ],
        compiler_params=first_params,
        name="requests_and_rates",
    )(slots, parents, profiles, drag_factor.reshape(1, columns), surface_before, downward)


def atmos_kernel(mix_ref, tend_ref, *refs):
    mix = mix_ref[...]
    lowest = mix[:, mix.shape[1] - 1 :].astype(jnp.float32)
    out_ref = refs[-1]
    for member, x_ref in enumerate(refs[:-1]):
        mixed = jnp.dot(mix, x_ref[0], preferred_element_type=jnp.float32)
        out_ref[member] = (mixed + lowest * tend_ref[member : member + 1, :]).astype(jnp.bfloat16)


def diffuse_atmos(profiles, mixing, tendency):
    fields, levels, columns = profiles.shape
    block = min(2048, columns)

    def field(member):
        return pl.BlockSpec((1, levels, block), lambda i: (member, 0, i))

    return pl.pallas_call(
        atmos_kernel,
        grid=(columns // block,),
        in_specs=[
            pl.BlockSpec((levels, levels), lambda i: (0, 0)),
            pl.BlockSpec((fields, block), lambda i: (0, i)),
        ]
        + [field(member) for member in range(fields)],
        out_specs=pl.BlockSpec((fields, levels, block), lambda i: (0, 0, i)),
        out_shape=jax.ShapeDtypeStruct(profiles.shape, jnp.bfloat16),
        compiler_params=stream_params,
        cost_estimate=pl.CostEstimate(
            flops=2 * fields * levels * levels * columns,
            bytes_accessed=4 * fields * levels * columns,
            transcendentals=0,
        ),
        name="diffuse_atmos",
    )(mixing, tendency, *[profiles] * fields)


def level_specs(levels, fields, block):
    count = 4 if levels % 4 == 0 else 1

    def part(number):
        return pl.BlockSpec((levels // count, fields, block), lambda i: (number, 0, i))

    return [part(number) for number in range(count)]


def top_kernel(mix_ref, *refs):
    state_refs, base_ref, first_ref = refs[:-2], refs[-2], refs[-1]
    total = None
    level = 0
    for ref in state_refs:
        for inner in range(ref.shape[0]):
            term = mix_ref[0, level] * ref[inner]
            total = term if total is None else total + term
            level += 1
    base_ref[...] = total
    first_ref[...] = state_refs[0][0]


def top_level(state, mixing):
    levels, fields, cells = state.shape
    block = min(2048, cells)
    specs = level_specs(levels, fields, block)
    return pl.pallas_call(
        top_kernel,
        grid=(cells // block,),
        in_specs=[smem] + specs,
        out_specs=[pl.BlockSpec((fields, block), lambda i: (0, i))] * 2,
        out_shape=[jax.ShapeDtypeStruct((fields, cells), jnp.float32)] * 2,
        compiler_params=stream_params,
        cost_estimate=pl.CostEstimate(
            flops=2 * fields * levels * cells,
            bytes_accessed=4 * fields * levels * cells,
            transcendentals=0,
        ),
        name="top_level",
    )(mixing, *[state] * len(specs))


def serve_kernel(
    per_owner,
    far_ref,
    asked_ref,
    own_ref,
    other_ref,
    out_ref,
    blocks_ref,
    filled_ref,
    arrived_sem,
    sent_sem,
):
    copies = [
        pltpu.make_async_copy(ref, blocks_ref.at[index], arrived_sem.at[index])
        for index, ref in enumerate((own_ref, other_ref))
    ]
    for copy in copies:
        copy.start()
    for copy in copies:
        copy.wait()
    far = far_ref[0]

    def body(peer, carry):
        for shard in range(2):
            for slot in range(per_owner):
                spot = shard * per_owner + slot
                filled_ref[peer, spot] = blocks_ref[
                    shard ^ far, :, window(asked_ref[peer, spot])
                ]
        return carry

    sends = []
    parts = sent_sem.shape[0]
    peers = filled_ref.shape[0] // parts
    for part in range(parts):
        lax.fori_loop(part * peers, (part + 1) * peers, body, 0)
        at = pl.ds(part * peers, peers)
        send = pltpu.make_async_copy(filled_ref.at[at], out_ref.at[at], sent_sem.at[part])
        send.start()
        sends.append(send)
    for send in sends:
        send.wait()


def split_high(values):
    high = values.astype(jnp.bfloat16).astype(jnp.float32)
    return jnp.concatenate([high, values - high], axis=0)


GROUP = 8
hot_type = jnp.float8_e4m3fn


def hot_kernel(
    place_ref,
    column_ref,
    atmos_weight_ref,
    mask_ref,
    hot_ref,
    share_ref,
    lanes_ref,
    *sums,
):
    intersections, cells = column_ref.shape
    windows = cells // LANES
    fields = share_ref.shape[1]
    group_tiles = GROUP * intersections
    steps = LANES // intersections
    group = pl.program_id(0)
    @pl.when(group == 0)
    def _():
        for ref in sums:
            ref[...] = jnp.zeros(ref.shape, jnp.float32)
        for first in range(0, windows, steps):
            tall = jnp.concatenate(
                [
                    column_ref[:, (first + step) * LANES : (first + step + 1) * LANES] & (LANES - 1)
                    for step in range(steps)
                ],
                axis=0,
            )
            turned = tall.astype(jnp.float32).T.astype(jnp.bfloat16)
            for part in range(steps // GROUP):
                lanes_ref[first // GROUP + part, :, :group_tiles] = turned[
                    :, part * group_tiles : (part + 1) * group_tiles
                ]

    column_ids = lax.broadcasted_iota(jnp.int32, (LANES, LANES), 1)
    column_ids = column_ids.astype(jnp.float32).astype(jnp.bfloat16)
    one, zero = jnp.bfloat16(1.0), jnp.bfloat16(0.0)
    field_ids = lax.broadcasted_iota(jnp.int32, (fields, LANES), 0)
    share_rows = lax.broadcasted_iota(jnp.int32, (2 * intersections, LANES), 0)
    first_half = share_rows % intersections < 2

    turned = lanes_ref[group]
    for inner in range(GROUP):
        step = group * GROUP + inner
        here = window(step)
        share = atmos_weight_ref[:, here] * mask_ref[:, here].astype(jnp.float32)
        hot = []
        for k in range(intersections):
            tile = inner * intersections + k
            lane_of = jnp.broadcast_to(turned[:, tile : tile + 1], (LANES, LANES))
            hot.append(jnp.where(lane_of == column_ids, one, zero))
        hot = jnp.concatenate(
            [
                jnp.concatenate([hot[0], hot[1]], axis=1),
                jnp.concatenate([hot[2], hot[3]], axis=1),
            ],
            axis=0,
        )
        hot_ref[inner] = hot.astype(hot_type)
        parts = split_high(share)
        rows = jnp.concatenate(
            [jnp.where(first_half, parts, 0.0), jnp.where(first_half, 0.0, parts)], axis=1
        ).astype(jnp.bfloat16)
        spread = jnp.dot(rows, hot, preferred_element_type=jnp.float32)
        for k in range(intersections):
            side = slice((k % 2) * LANES, (k % 2 + 1) * LANES)
            low = intersections + k
            shared = spread[k : k + 1, side] + spread[low : low + 1, side]
            place = place_ref[k, step]
            sums[k][lax.div(place, fields)] += jnp.where(
                field_ids == lax.rem(place, fields), shared, 0.0
            )

    @pl.when(group == pl.num_programs(0) - 1)
    def _():
        total = sums[0][...]
        for ref in sums[1:]:
            total = total + ref[...]
        share_ref[...] = total


def middle_kernel(
    far_ref,
    place_ref,
    spot_ref,
    mix_ref,
    arrived_ref,
    column_ref,
    ocean_weight_ref,
    atmos_weight_ref,
    mask_ref,
    base_ref,
    state_ref,
    hot_ref,
    share_ref,
    forcing_ref,
    away_ref,
    home_ref,
    value_ref,
    parts_ref,
    held_ref,
    held_sem,
    sent_sem,
):
    intersections, cells = column_ref.shape
    windows = cells // LANES
    fields = base_ref.shape[0]
    near, packed = away_ref.shape[:2]
    per_owner = packed * fields // (fields + 1)
    rows = per_owner // fields

    def fetch(group):
        part = pl.ds(group * GROUP, GROUP)
        return pltpu.make_async_copy(hot_ref.at[part], held_ref.at[part], held_sem.at[group])

    groups = windows // GROUP
    for group in range(groups):
        fetch(group).start()
    value_ref[...] = jnp.zeros(value_ref.shape, jnp.float32)
    corner = mix_ref[0, 0]
    blank = jnp.zeros((2 * fields, LANES), jnp.float32)

    def body(group, carry):
        for inner in range(GROUP):
            step = group * GROUP + inner
            here = window(step)
            lanes = column_ref[:, here] & (LANES - 1)
            ocean_weight = ocean_weight_ref[:, here]
            total = jnp.zeros((fields, LANES), jnp.float32)
            weight = jnp.zeros((1, LANES), jnp.float32)
            for k in range(intersections):
                picked = jnp.take_along_axis(
                    arrived_ref[spot_ref[k, step]],
                    jnp.broadcast_to(lanes[k : k + 1], (fields, LANES)),
                    axis=1,
                    mode="promise_in_bounds",
                )
                total = total + ocean_weight[k : k + 1] * picked
                weight = weight + ocean_weight[k : k + 1]
            forcing = total / weight
            forcing_ref[:, here] = forcing
            mask = mask_ref[:, here]
            surface = jnp.where(
                mask == 1, base_ref[:, here] + corner * forcing, state_ref[:, here]
            )
            share = atmos_weight_ref[:, here] * mask.astype(jnp.float32)
            parts = [split_high(share[k : k + 1] * surface) for k in range(intersections)]
            left = [parts[0], parts[1], blank, blank]
            right = [blank, blank, parts[2], parts[3]]
            parts = jnp.concatenate(
                [jnp.concatenate(left, axis=0), jnp.concatenate(right, axis=0)], axis=1
            ).astype(jnp.bfloat16)
            parts_ref[step] = parts
        return carry

    lax.fori_loop(0, groups, body, 0)

    def multiply(group, carry):
        fetch(group).wait()
        for inner in range(GROUP):
            step = group * GROUP + inner
            spread = jnp.dot(
                parts_ref[step],
                held_ref[step].astype(jnp.bfloat16),
                preferred_element_type=jnp.float32,
            )
            for k in range(intersections):
                side = slice((k % 2) * LANES, (k % 2 + 1) * LANES)
                at = 2 * fields * k
                value_ref[place_ref[k, step]] = (
                    spread[at : at + fields, side] + spread[at + fields : at + 2 * fields, side]
                )
        return carry

    lax.fori_loop(0, groups, multiply, 0)
    far = far_ref[0]
    shards = value_ref.reshape(2, near, per_owner, fields, LANES)
    copies = []
    for index, (ref, shard) in enumerate(((away_ref, 1 - far), (home_ref, far))):
        copies.append(
            pltpu.make_async_copy(
                shards.at[shard], ref.at[:, pl.ds(0, per_owner)], sent_sem.at[2 * index]
            )
        )
        copies.append(
            pltpu.make_async_copy(
                share_ref.at[shard],
                ref.at[:, pl.ds(per_owner, rows)],
                sent_sem.at[2 * index + 1],
            )
        )
    for copy in copies:
        copy.start()
    for copy in copies:
        copy.wait()


def ocean_kernel(mix_ref, forcing_ref, mask_ref, *refs):
    x_refs, (out_ref, high_ref, low_ref) = refs[:-3], refs[-3:]
    levels, fields, block = out_ref.shape
    rows = levels * fields

    @pl.when(pl.program_id(0) == 0)
    def _():
        level = lax.broadcasted_iota(jnp.int32, (rows, levels), 0) // fields
        pick = (level == lax.broadcasted_iota(jnp.int32, (rows, levels), 1)).astype(jnp.float32)
        tall = jnp.dot(pick, mix_ref[...], precision=lax.Precision.HIGHEST)
        wide = lax.dot_general(
            tall, pick, (((1,), (1,)), ((), ())), precision=lax.Precision.HIGHEST
        )
        down = lax.broadcasted_iota(jnp.int32, (rows, rows), 0) % fields
        across = lax.broadcasted_iota(jnp.int32, (rows, rows), 1) % fields
        wide = jnp.where(down == across, wide, 0.0)
        high = wide.astype(jnp.bfloat16)
        high_ref[...] = high
        low_ref[...] = (wide - high.astype(jnp.float32)).astype(jnp.bfloat16)

    flat = jnp.concatenate(
        [ref[...].reshape(rows // len(x_refs), block) for ref in x_refs], axis=0
    )
    push = jnp.concatenate(
        [forcing_ref[...], jnp.zeros((rows - fields, block), jnp.float32)], axis=0
    )
    loaded = flat + push
    high = loaded.astype(jnp.bfloat16)
    low = (loaded - high.astype(jnp.float32)).astype(jnp.bfloat16)
    mixed = (
        jnp.dot(high_ref[...], high, preferred_element_type=jnp.float32)
        + jnp.dot(high_ref[...], low, preferred_element_type=jnp.float32)
        + jnp.dot(low_ref[...], high, preferred_element_type=jnp.float32)
    )
    out_ref[...] = jnp.where(mask_ref[...] == 1, mixed, flat).reshape(levels, fields, block)


def diffuse_ocean(state, mixing, forcing, mask):
    levels, fields, cells = state.shape
    block = min(1024, cells)
    rows = levels * fields
    specs = level_specs(levels, fields, block)
    return pl.pallas_call(
        ocean_kernel,
        grid=(cells // block,),
        in_specs=[
            pl.BlockSpec(mixing.shape, lambda i: (0, 0)),
            pl.BlockSpec((fields, block), lambda i: (0, i)),
            pl.BlockSpec((1, block), lambda i: (0, i)),
        ]
        + specs,
        out_specs=pl.BlockSpec((levels, fields, block), lambda i: (0, 0, i)),
        out_shape=jax.ShapeDtypeStruct(state.shape, jnp.float32),
        scratch_shapes=[pltpu.VMEM((rows, rows), jnp.bfloat16)] * 2,
        compiler_params=stream_params,
        cost_estimate=pl.CostEstimate(
            flops=6 * rows * rows * cells,
            bytes_accessed=8 * rows * cells,
            transcendentals=0,
        ),
        name="diffuse_ocean",
    )(mixing, forcing, mask, *[state] * len(specs))


def collect_kernel(per_owner, columns, far_ref, asked_ref, back_ref, *refs):
    near, _, fields, _ = back_ref.shape
    chains = 2
    sums = refs[-chains:]
    rest = refs[:-chains]
    home = len(rest) > 1
    windows = columns // LANES
    quarter = windows // fields
    far = far_ref[0]
    first = (far if home else 1 - far) * per_owner
    for ref in sums:
        ref[...] = jnp.zeros(ref.shape, jnp.float32)

    def body(step, carry):
        for slot in range(per_owner):
            for chain in range(chains):
                peer = step * chains + chain
                tile, row = per_owner + slot // fields, slot % fields
                share = back_ref[peer, tile, row : row + 1]
                block = jnp.concatenate(
                    [back_ref[peer, slot], jnp.broadcast_to(share, (fields, LANES))], axis=0
                )
                sums[chain][asked_ref[peer, first + slot]] += block
        return carry

    lax.fori_loop(0, near // chains, body, 0)
    out_ref = rest[-1]
    for spot in range(windows):
        block = sums[0][spot]
        for ref in sums[1:]:
            block = block + ref[spot]
        here = slice(spot * LANES, (spot + 1) * LANES)
        row = slice(spot // quarter, spot // quarter + 1)
        side = spot % quarter * LANES
        beside = slice(columns + side, columns + side + LANES)
        if home:
            other_ref, land_weight_ref, land_ref = rest[:3]
            land_weight = land_weight_ref[:, here]
            total = block[:fields] + other_ref[:, here] + land_weight * land_ref[:, here]
            out_ref[:, here] = total / (block[fields:] + (other_ref[row, beside] + land_weight))
        else:
            out_ref[:, here] = block[:fields]
            out_ref[row, beside] = block[fields : fields + 1]


def collect(asked, far, back, per_owner, columns, rest):
    fields = back.shape[2]
    width = columns if rest else columns + columns // fields
    return pl.pallas_call(
        functools.partial(collect_kernel, per_owner, columns),
        in_specs=[smem, smem, vmem] + [vmem] * len(rest),
        out_specs=vmem,
        out_shape=jax.ShapeDtypeStruct((fields, width), jnp.float32),
        scratch_shapes=[pltpu.VMEM((columns // LANES, 2 * fields, LANES), jnp.float32)] * 2,
        compiler_params=params,
        name="surface_state" if rest else "collect_away",
    )(far, asked, back, *rest)


def per_device(
    atmos_profiles,
    atmos_mixing,
    drag_factor,
    surface_before,
    downward_fluxes,
    land_weight,
    land_surface,
    ocean_state,
    ocean_mixing,
    sea_mask,
    exchange_slot,
    parent_column,
    ocean_weight,
    atmos_weight,
):
    near = lax.axis_size("near") * lax.axis_size("sub")
    devices = 2 * near
    fields, _, columns = atmos_profiles.shape
    intersections, cells = exchange_slot.shape
    capacity = 2 * intersections * cells // devices
    per_owner = capacity // LANES
    spots = 2 * per_owner
    mask = sea_mask.reshape(1, cells)
    state = ocean_state.transpose(1, 0, 2)
    far = lax.axis_index("far").astype(jnp.int32).reshape(1)

    def to_near(values):
        return lax.all_to_all(values, ("near", "sub"), split_axis=0, concat_axis=0, tiled=True)

    def to_far(values):
        return lax.ppermute(values, "far", ((0, 1), (1, 0)))

    place, spot, wanted, forcing_rows, tendency = start(
        near,
        per_owner,
        exchange_slot,
        parent_column,
        atmos_profiles,
        drag_factor,
        surface_before,
        downward_fluxes,
    )
    asked = to_near(wanted)
    other_rows = to_far(forcing_rows)
    base, first_level = top_level(state, ocean_mixing)
    asked, base, first_level = lax.optimization_barrier((asked, base, first_level))
    served = pl.pallas_call(
        functools.partial(serve_kernel, per_owner),
        in_specs=[smem, smem, hbm, hbm],
        out_specs=hbm,
        out_shape=jax.ShapeDtypeStruct((near, spots, fields, LANES), jnp.float32),
        scratch_shapes=[
            pltpu.VMEM((2, fields, columns), jnp.float32),
            pltpu.VMEM((near, spots, fields, LANES), jnp.float32),
            pltpu.SemaphoreType.DMA((2,)),
            pltpu.SemaphoreType.DMA((4,)),
        ],
        compiler_params=params,
        name="serve_windows",
    )(far, asked, forcing_rows, other_rows)
    served, columns_asked = lax.optimization_barrier((served, parent_column))
    arrived = to_near(served)
    rows = per_owner // fields
    windows = cells // LANES
    hot, shares = pl.pallas_call(
        hot_kernel,
        grid=(windows // GROUP,),
        in_specs=[smem] + [vmem] * 3,
        out_specs=[
            pl.BlockSpec((GROUP, 2 * LANES, 2 * LANES), lambda i: (i, 0, 0)),
            pl.BlockSpec((2 * near * rows, fields, LANES), lambda i: (0, 0, 0)),
        ],
        out_shape=[
            jax.ShapeDtypeStruct((windows, 2 * LANES, 2 * LANES), hot_type),
            jax.ShapeDtypeStruct((2 * near * rows, fields, LANES), jnp.float32),
        ],
        scratch_shapes=[pltpu.VMEM((windows // GROUP, LANES, LANES), jnp.bfloat16)]
        + [pltpu.VMEM((2 * near * rows, fields, LANES), jnp.float32)] * intersections,
        compiler_params=middle_params,
        name="one_hot_and_shares",
    )(place, columns_asked, atmos_weight, mask)
    arrived, hot, shares = lax.optimization_barrier((arrived, hot, shares))
    sent = (near, per_owner + rows, fields, LANES)
    forcing, away, home = pl.pallas_call(
        middle_kernel,
        in_specs=[smem] * 4 + [vmem] * 7 + [hbm, vmem],
        out_specs=[vmem, hbm, hbm],
        out_shape=[
            jax.ShapeDtypeStruct((fields, cells), jnp.float32),
            jax.ShapeDtypeStruct(sent, jnp.float32),
            jax.ShapeDtypeStruct(sent, jnp.float32),
        ],
        scratch_shapes=[
            pltpu.VMEM((near * spots, fields, LANES), jnp.float32),
            pltpu.VMEM((windows, 2 * fields * intersections, 2 * LANES), jnp.bfloat16),
            pltpu.VMEM((windows, 2 * LANES, 2 * LANES), hot_type),
            pltpu.SemaphoreType.DMA((windows // GROUP,)),
            pltpu.SemaphoreType.DMA((4,)),
        ],
        compiler_params=middle_params,
        name="forcing_and_windows",
    )(
        far,
        place,
        spot,
        ocean_mixing,
        arrived.reshape(near * spots, fields, LANES),
        parent_column,
        ocean_weight,
        atmos_weight,
        mask,
        base,
        first_level,
        hot,
        shares.reshape(2, near, rows, fields, LANES),
    )
    tendency, forcing = lax.optimization_barrier((tendency, forcing))
    atmos_updated = diffuse_atmos(atmos_profiles, atmos_mixing, tendency)
    back_away, atmos_updated, home = lax.optimization_barrier(
        (to_near(away), atmos_updated, home)
    )
    back_home = to_near(home)
    sums_away = collect(asked, far, back_away, per_owner, columns, ())
    other_sums = to_far(sums_away)
    ocean_updated = diffuse_ocean(state, ocean_mixing, forcing, mask).transpose(1, 0, 2)
    back_home, ocean_updated = lax.optimization_barrier((back_home, ocean_updated))
    surface_state = collect(
        asked,
        far,
        back_home,
        per_owner,
        columns,
        (other_sums, land_weight.reshape(1, columns), land_surface),
    )
    return (atmos_updated, ocean_updated, surface_state)


def solution(mesh):
    comp, sub = mesh.devices.shape
    halves = jax.sharding.Mesh(mesh.devices.reshape(2, comp // 2, sub), AXES)
    split = P(None, AXES)
    return jax.shard_map(
        per_device,
        mesh=halves,
        in_specs=(
            P(None, None, AXES),
            P(),
            P(AXES),
            split,
            split,
            P(AXES),
            split,
            P(None, None, AXES),
            P(),
            P(AXES),
            split,
            split,
            split,
            split,
        ),
        out_specs=(P(None, None, AXES), P(None, None, AXES), split),
        check_vma=False,
    )
```

```python
import functools

import jax
import jax.numpy as jnp
from jax import lax
from jax.experimental import pallas as pl
from jax.experimental.pallas import tpu as pltpu
from jax.sharding import PartitionSpec as P

couple_rate = 0.5
LANES = 128
params = pltpu.CompilerParams(vmem_limit_bytes=24 * 1024 * 1024)
stream_params = pltpu.CompilerParams(vmem_limit_bytes=52 * 1024 * 1024)
middle_params = pltpu.CompilerParams(vmem_limit_bytes=48 * 1024 * 1024)
first_params = pltpu.CompilerParams(vmem_limit_bytes=56 * 1024 * 1024)
vmem = pl.BlockSpec(memory_space=pltpu.VMEM)
smem = pl.BlockSpec(memory_space=pltpu.SMEM)
hbm = pl.BlockSpec(memory_space=pl.ANY)
AXES = ("far", "near", "sub")


def window(index):
    return pl.ds(pl.multiple_of(index * LANES, LANES), LANES)


def make_requests(per_owner, slot_ref, column_ref, place_ref, spot_ref, wanted_ref):
    intersections, cells = slot_ref.shape
    near, spots = wanted_ref.shape
    windows = cells // LANES
    lane = lax.broadcasted_iota(jnp.int32, (intersections, windows), 1)

    def heads(ref):
        found = jnp.zeros((intersections, windows), jnp.int32)
        for step in range(windows):
            head = ref[:, step * LANES : step * LANES + 1]
            found = jnp.where(lane == step, head, found)
        return found // LANES

    place = heads(slot_ref)
    column_window = heads(column_ref)
    owner = place // per_owner
    peer = owner % near
    spot = owner // near * per_owner + place % per_owner
    place_ref[...] = place
    spot_ref[...] = peer * spots + spot
    peer_ids = lax.broadcasted_iota(jnp.int32, (near, windows), 0)
    spot_ids = lax.broadcasted_iota(jnp.int32, (spots, windows), 0)
    wanted = jnp.zeros((near, spots), jnp.float32)
    for k in range(intersections):
        row = slice(k, k + 1)
        peer_hot = jnp.where(peer_ids == peer[row], 1.0, 0.0)
        spot_hot = jnp.where(
            spot_ids == spot[row], column_window[row].astype(jnp.float32), 0.0
        )
        wanted = wanted + lax.dot_general(
            peer_hot.astype(jnp.bfloat16),
            spot_hot.astype(jnp.bfloat16),
            (((1,), (1,)), ((), ())),
            preferred_element_type=jnp.float32,
        )
    wanted_ref[...] = wanted.astype(jnp.int32)


def start_kernel(
    last,
    per_owner,
    slot_ref,
    column_ref,
    x_ref,
    drag_ref,
    before_ref,
    down_ref,
    place_ref,
    spot_ref,
    wanted_ref,
    forcing_ref,
    tend_ref,
):
    @pl.when(pl.program_id(0) == 0)
    def _():
        make_requests(per_owner, slot_ref, column_ref, place_ref, spot_ref, wanted_ref)

    def row(ref, index):
        return ref[index : index + 1, :]

    bottom = [x_ref[member].astype(jnp.float32)[last : last + 1, :] for member in range(4)]
    east = bottom[2] - row(before_ref, 2)
    north = bottom[3] - row(before_ref, 3)
    transfer = drag_ref[...] * jnp.sqrt(1.0 + east * east + north * north)
    sensible = transfer * (row(before_ref, 0) - bottom[0])
    latent = transfer * (row(before_ref, 1) - bottom[1])
    east_stress = couple_rate * (transfer * east)
    north_stress = couple_rate * (transfer * north)
    forcing_ref[0:1, :] = couple_rate * (
        row(down_ref, 0) + row(down_ref, 1) - sensible - latent
    )
    forcing_ref[1:2, :] = couple_rate * (latent - row(down_ref, 2) - row(down_ref, 3))
    forcing_ref[2:3, :] = east_stress
    forcing_ref[3:4, :] = north_stress
    tend_ref[0:1, :] = couple_rate * sensible
    tend_ref[1:2, :] = couple_rate * latent
    tend_ref[2:3, :] = -east_stress
    tend_ref[3:4, :] = -north_stress


def start(near, per_owner, slots, parents, profiles, drag_factor, surface_before, downward):
    fields, levels, columns = profiles.shape
    intersections, cells = slots.shape
    block = min(4096, columns)
    tall = 16
    at = (levels - 1) // tall
    rows = pl.BlockSpec((fields, block), lambda i: (0, i))
    tiles = (intersections, cells // LANES)
    asked = (near, 2 * per_owner)

    def whole(shape):
        return pl.BlockSpec(shape, lambda i: (0, 0))

    return pl.pallas_call(
        functools.partial(start_kernel, levels - 1 - at * tall, per_owner),
        grid=(columns // block,),
        in_specs=[
            whole(slots.shape),
            whole(slots.shape),
            pl.BlockSpec((fields, tall, block), lambda i: (0, at, i)),
            pl.BlockSpec((1, block), lambda i: (0, i)),
            rows,
            rows,
        ],
        out_specs=[whole(tiles), whole(tiles), whole(asked), rows, rows],
        out_shape=[
            jax.ShapeDtypeStruct(tiles, jnp.int32),
            jax.ShapeDtypeStruct(tiles, jnp.int32),
            jax.ShapeDtypeStruct(asked, jnp.int32),
            jax.ShapeDtypeStruct((fields, columns), jnp.float32),
            jax.ShapeDtypeStruct((fields, columns), jnp.float32),
        ],
        compiler_params=first_params,
        name="requests_and_rates",
    )(slots, parents, profiles, drag_factor.reshape(1, columns), surface_before, downward)


def atmos_kernel(mix_ref, tend_ref, *refs):
    mix = mix_ref[...]
    lowest = mix[:, mix.shape[1] - 1 :].astype(jnp.float32)
    out_ref = refs[-1]
    for member, x_ref in enumerate(refs[:-1]):
        mixed = jnp.dot(mix, x_ref[0], preferred_element_type=jnp.float32)
        out_ref[member] = (mixed + lowest * tend_ref[member : member + 1, :]).astype(jnp.bfloat16)


def diffuse_atmos(profiles, mixing, tendency):
    fields, levels, columns = profiles.shape
    block = min(2048, columns)

    def field(member):
        return pl.BlockSpec((1, levels, block), lambda i: (member, 0, i))

    return pl.pallas_call(
        atmos_kernel,
        grid=(columns // block,),
        in_specs=[
            pl.BlockSpec((levels, levels), lambda i: (0, 0)),
            pl.BlockSpec((fields, block), lambda i: (0, i)),
        ]
        + [field(member) for member in range(fields)],
        out_specs=pl.BlockSpec((fields, levels, block), lambda i: (0, 0, i)),
        out_shape=jax.ShapeDtypeStruct(profiles.shape, jnp.bfloat16),
        compiler_params=stream_params,
        cost_estimate=pl.CostEstimate(
            flops=2 * fields * levels * levels * columns,
            bytes_accessed=4 * fields * levels * columns,
            transcendentals=0,
        ),
        name="diffuse_atmos",
    )(mixing, tendency, *[profiles] * fields)


def level_specs(levels, fields, block):
    count = 4 if levels % 4 == 0 else 1

    def part(number):
        return pl.BlockSpec((levels // count, fields, block), lambda i: (number, 0, i))

    return [part(number) for number in range(count)]


def top_kernel(mix_ref, *refs):
    state_refs, base_ref, first_ref = refs[:-2], refs[-2], refs[-1]
    total = None
    level = 0
    for ref in state_refs:
        for inner in range(ref.shape[0]):
            term = mix_ref[0, level] * ref[inner]
            total = term if total is None else total + term
            level += 1
    base_ref[...] = total
    first_ref[...] = state_refs[0][0]


def top_level(state, mixing):
    levels, fields, cells = state.shape
    block = min(2048, cells)
    specs = level_specs(levels, fields, block)
    return pl.pallas_call(
        top_kernel,
        grid=(cells // block,),
        in_specs=[smem] + specs,
        out_specs=[pl.BlockSpec((fields, block), lambda i: (0, i))] * 2,
        out_shape=[jax.ShapeDtypeStruct((fields, cells), jnp.float32)] * 2,
        compiler_params=stream_params,
        cost_estimate=pl.CostEstimate(
            flops=2 * fields * levels * cells,
            bytes_accessed=4 * fields * levels * cells,
            transcendentals=0,
        ),
        name="top_level",
    )(mixing, *[state] * len(specs))


def serve_kernel(
    per_owner,
    far_ref,
    asked_ref,
    own_ref,
    other_ref,
    out_ref,
    blocks_ref,
    filled_ref,
    arrived_sem,
    sent_sem,
):
    copies = [
        pltpu.make_async_copy(ref, blocks_ref.at[index], arrived_sem.at[index])
        for index, ref in enumerate((own_ref, other_ref))
    ]
    for copy in copies:
        copy.start()
    for copy in copies:
        copy.wait()
    far = far_ref[0]

    def body(peer, carry):
        for shard in range(2):
            for slot in range(per_owner):
                spot = shard * per_owner + slot
                filled_ref[peer, spot] = blocks_ref[
                    shard ^ far, :, window(asked_ref[peer, spot])
                ]
        return carry

    sends = []
    parts = sent_sem.shape[0]
    peers = filled_ref.shape[0] // parts
    for part in range(parts):
        lax.fori_loop(part * peers, (part + 1) * peers, body, 0)
        at = pl.ds(part * peers, peers)
        send = pltpu.make_async_copy(filled_ref.at[at], out_ref.at[at], sent_sem.at[part])
        send.start()
        sends.append(send)
    for send in sends:
        send.wait()


def split_high(values):
    high = values.astype(jnp.bfloat16).astype(jnp.float32)
    return jnp.concatenate([high, values - high], axis=0)


GROUP = 8


def hot_kernel(
    place_ref,
    column_ref,
    atmos_weight_ref,
    mask_ref,
    hot_ref,
    share_ref,
    lanes_ref,
    *sums,
):
    intersections, cells = column_ref.shape
    windows = cells // LANES
    fields = share_ref.shape[1]
    group_tiles = GROUP * intersections
    steps = LANES // intersections
    group = pl.program_id(0)
    @pl.when(group == 0)
    def _():
        for ref in sums:
            ref[...] = jnp.zeros(ref.shape, jnp.float32)
        for first in range(0, windows, steps):
            tall = jnp.concatenate(
                [
                    column_ref[:, (first + step) * LANES : (first + step + 1) * LANES] & (LANES - 1)
                    for step in range(steps)
                ],
                axis=0,
            )
            turned = tall.astype(jnp.float32).T.astype(jnp.bfloat16)
            for part in range(steps // GROUP):
                lanes_ref[first // GROUP + part, :, :group_tiles] = turned[
                    :, part * group_tiles : (part + 1) * group_tiles
                ]

    column_ids = lax.broadcasted_iota(jnp.int32, (LANES, LANES), 1)
    column_ids = column_ids.astype(jnp.float32).astype(jnp.bfloat16)
    one, zero = jnp.bfloat16(1.0), jnp.bfloat16(0.0)
    field_ids = lax.broadcasted_iota(jnp.int32, (fields, LANES), 0)
    share_rows = lax.broadcasted_iota(jnp.int32, (2 * intersections, LANES), 0)
    first_half = share_rows % intersections < 2

    turned = lanes_ref[group]
    for inner in range(GROUP):
        step = group * GROUP + inner
        here = window(step)
        share = atmos_weight_ref[:, here] * mask_ref[:, here].astype(jnp.float32)
        hot = []
        for k in range(intersections):
            tile = inner * intersections + k
            lane_of = jnp.broadcast_to(turned[:, tile : tile + 1], (LANES, LANES))
            hot.append(jnp.where(lane_of == column_ids, one, zero))
        hot = jnp.concatenate(
            [
                jnp.concatenate([hot[0], hot[1]], axis=1),
                jnp.concatenate([hot[2], hot[3]], axis=1),
            ],
            axis=0,
        )
        hot_ref[inner] = hot
        parts = split_high(share)
        rows = jnp.concatenate(
            [jnp.where(first_half, parts, 0.0), jnp.where(first_half, 0.0, parts)], axis=1
        ).astype(jnp.bfloat16)
        spread = jnp.dot(rows, hot, preferred_element_type=jnp.float32)
        for k in range(intersections):
            side = slice((k % 2) * LANES, (k % 2 + 1) * LANES)
            low = intersections + k
            shared = spread[k : k + 1, side] + spread[low : low + 1, side]
            place = place_ref[k, step]
            sums[k][lax.div(place, fields)] += jnp.where(
                field_ids == lax.rem(place, fields), shared, 0.0
            )

    @pl.when(group == pl.num_programs(0) - 1)
    def _():
        total = sums[0][...]
        for ref in sums[1:]:
            total = total + ref[...]
        share_ref[...] = total


def middle_kernel(
    far_ref,
    place_ref,
    spot_ref,
    mix_ref,
    arrived_ref,
    column_ref,
    ocean_weight_ref,
    atmos_weight_ref,
    mask_ref,
    base_ref,
    state_ref,
    hot_ref,
    share_ref,
    forcing_ref,
    away_ref,
    home_ref,
    value_ref,
    held_ref,
    held_sem,
    sent_sem,
):
    intersections, cells = column_ref.shape
    windows = cells // LANES
    fields = base_ref.shape[0]
    near, packed = away_ref.shape[:2]
    per_owner = packed * fields // (fields + 1)
    rows = per_owner // fields

    def fetch(step):
        return pltpu.make_async_copy(hot_ref.at[step], held_ref.at[step], held_sem.at[step])

    groups = windows // GROUP
    for step in range(windows):
        fetch(step).start()
    value_ref[...] = jnp.zeros(value_ref.shape, jnp.float32)
    corner = mix_ref[0, 0]
    blank = jnp.zeros((2 * fields, LANES), jnp.float32)

    def body(group, carry):
        for inner in range(GROUP):
            fetch(group * GROUP + inner).wait()
        for inner in range(GROUP):
            step = group * GROUP + inner
            here = window(step)
            lanes = column_ref[:, here] & (LANES - 1)
            ocean_weight = ocean_weight_ref[:, here]
            total = jnp.zeros((fields, LANES), jnp.float32)
            weight = jnp.zeros((1, LANES), jnp.float32)
            for k in range(intersections):
                picked = jnp.take_along_axis(
                    arrived_ref[spot_ref[k, step]],
                    jnp.broadcast_to(lanes[k : k + 1], (fields, LANES)),
                    axis=1,
                    mode="promise_in_bounds",
                )
                total = total + ocean_weight[k : k + 1] * picked
                weight = weight + ocean_weight[k : k + 1]
            forcing = total / weight
            forcing_ref[:, here] = forcing
            mask = mask_ref[:, here]
            surface = jnp.where(
                mask == 1, base_ref[:, here] + corner * forcing, state_ref[:, here]
            )
            share = atmos_weight_ref[:, here] * mask.astype(jnp.float32)
            parts = [split_high(share[k : k + 1] * surface) for k in range(intersections)]
            left = [parts[0], parts[1], blank, blank]
            right = [blank, blank, parts[2], parts[3]]
            parts = jnp.concatenate(
                [jnp.concatenate(left, axis=0), jnp.concatenate(right, axis=0)], axis=1
            ).astype(jnp.bfloat16)
            spread = jnp.dot(parts, held_ref[step], preferred_element_type=jnp.float32)
            for k in range(intersections):
                side = slice((k % 2) * LANES, (k % 2 + 1) * LANES)
                at = 2 * fields * k
                value_ref[place_ref[k, step]] = (
                    spread[at : at + fields, side] + spread[at + fields : at + 2 * fields, side]
                )
        return carry

    lax.fori_loop(0, windows // GROUP, body, 0)
    far = far_ref[0]
    shards = value_ref.reshape(2, near, per_owner, fields, LANES)
    copies = []
    for index, (ref, shard) in enumerate(((away_ref, 1 - far), (home_ref, far))):
        copies.append(
            pltpu.make_async_copy(
                shards.at[shard], ref.at[:, pl.ds(0, per_owner)], sent_sem.at[2 * index]
            )
        )
        copies.append(
            pltpu.make_async_copy(
                share_ref.at[shard],
                ref.at[:, pl.ds(per_owner, rows)],
                sent_sem.at[2 * index + 1],
            )
        )
    for copy in copies:
        copy.start()
    for copy in copies:
        copy.wait()


def ocean_kernel(mix_ref, forcing_ref, mask_ref, *refs):
    x_refs, (out_ref, high_ref, low_ref) = refs[:-3], refs[-3:]
    levels, fields, block = out_ref.shape
    rows = levels * fields

    @pl.when(pl.program_id(0) == 0)
    def _():
        level = lax.broadcasted_iota(jnp.int32, (rows, levels), 0) // fields
        pick = (level == lax.broadcasted_iota(jnp.int32, (rows, levels), 1)).astype(jnp.float32)
        tall = jnp.dot(pick, mix_ref[...], precision=lax.Precision.HIGHEST)
        wide = lax.dot_general(
            tall, pick, (((1,), (1,)), ((), ())), precision=lax.Precision.HIGHEST
        )
        down = lax.broadcasted_iota(jnp.int32, (rows, rows), 0) % fields
        across = lax.broadcasted_iota(jnp.int32, (rows, rows), 1) % fields
        wide = jnp.where(down == across, wide, 0.0)
        high = wide.astype(jnp.bfloat16)
        high_ref[...] = high
        low_ref[...] = (wide - high.astype(jnp.float32)).astype(jnp.bfloat16)

    flat = jnp.concatenate(
        [ref[...].reshape(rows // len(x_refs), block) for ref in x_refs], axis=0
    )
    push = jnp.concatenate(
        [forcing_ref[...], jnp.zeros((rows - fields, block), jnp.float32)], axis=0
    )
    loaded = flat + push
    high = loaded.astype(jnp.bfloat16)
    low = (loaded - high.astype(jnp.float32)).astype(jnp.bfloat16)
    mixed = (
        jnp.dot(high_ref[...], high, preferred_element_type=jnp.float32)
        + jnp.dot(high_ref[...], low, preferred_element_type=jnp.float32)
        + jnp.dot(low_ref[...], high, preferred_element_type=jnp.float32)
    )
    out_ref[...] = jnp.where(mask_ref[...] == 1, mixed, flat).reshape(levels, fields, block)


def diffuse_ocean(state, mixing, forcing, mask):
    levels, fields, cells = state.shape
    block = min(1024, cells)
    rows = levels * fields
    specs = level_specs(levels, fields, block)
    return pl.pallas_call(
        ocean_kernel,
        grid=(cells // block,),
        in_specs=[
            pl.BlockSpec(mixing.shape, lambda i: (0, 0)),
            pl.BlockSpec((fields, block), lambda i: (0, i)),
            pl.BlockSpec((1, block), lambda i: (0, i)),
        ]
        + specs,
        out_specs=pl.BlockSpec((levels, fields, block), lambda i: (0, 0, i)),
        out_shape=jax.ShapeDtypeStruct(state.shape, jnp.float32),
        scratch_shapes=[pltpu.VMEM((rows, rows), jnp.bfloat16)] * 2,
        compiler_params=stream_params,
        cost_estimate=pl.CostEstimate(
            flops=6 * rows * rows * cells,
            bytes_accessed=8 * rows * cells,
            transcendentals=0,
        ),
        name="diffuse_ocean",
    )(mixing, forcing, mask, *[state] * len(specs))


def collect_kernel(per_owner, far_ref, asked_ref, back_ref, *refs):
    near, _, fields, _ = back_ref.shape
    chains = 4
    sums = refs[-2 * chains :]
    rest = refs[: -2 * chains]
    home = len(rest) > 1
    columns = sums[0].shape[1]
    quarter = columns // fields
    far = far_ref[0]
    first = (far if home else 1 - far) * per_owner
    for ref in sums:
        ref[...] = jnp.zeros(ref.shape, jnp.float32)

    def body(step, carry):
        for slot in range(per_owner):
            for chain in range(chains):
                peer = step * chains + chain
                at = window(asked_ref[peer, first + slot])
                tile, row = per_owner + slot // fields, slot % fields
                sums[chain][:, at] += back_ref[peer, slot]
                sums[chains + chain][:, at] += back_ref[peer, tile, row : row + 1]
        return carry

    lax.fori_loop(0, near // chains, body, 0)
    values, shares = sums[0][...], sums[chains][...]
    for chain in range(1, chains):
        values = values + sums[chain][...]
        shares = shares + sums[chains + chain][...]
    out_ref = rest[-1]
    if home:
        other_ref, land_weight_ref, land_ref = rest[:3]
        land_weight = land_weight_ref[...]
        total = values + other_ref[:, :columns] + land_weight * land_ref[...]
        weight = shares + land_weight
        for row in range(fields):
            part = slice(row * quarter, (row + 1) * quarter)
            other_shares = other_ref[row : row + 1, columns:]
            out_ref[:, part] = total[:, part] / (weight[:, part] + other_shares)
    else:
        out_ref[:, :columns] = values
        for row in range(fields):
            out_ref[row : row + 1, columns:] = shares[:, row * quarter : (row + 1) * quarter]


def collect(asked, far, back, per_owner, columns, rest):
    fields = back.shape[2]
    chains = 4
    width = columns if rest else columns + columns // fields
    return pl.pallas_call(
        functools.partial(collect_kernel, per_owner),
        in_specs=[smem, smem, vmem] + [vmem] * len(rest),
        out_specs=vmem,
        out_shape=jax.ShapeDtypeStruct((fields, width), jnp.float32),
        scratch_shapes=[pltpu.VMEM((fields, columns), jnp.float32)] * chains
        + [pltpu.VMEM((1, columns), jnp.float32)] * chains,
        compiler_params=params,
        name="surface_state" if rest else "collect_away",
    )(far, asked, back, *rest)


def per_device(
    atmos_profiles,
    atmos_mixing,
    drag_factor,
    surface_before,
    downward_fluxes,
    land_weight,
    land_surface,
    ocean_state,
    ocean_mixing,
    sea_mask,
    exchange_slot,
    parent_column,
    ocean_weight,
    atmos_weight,
):
    near = lax.axis_size("near") * lax.axis_size("sub")
    devices = 2 * near
    fields, _, columns = atmos_profiles.shape
    intersections, cells = exchange_slot.shape
    capacity = 2 * intersections * cells // devices
    per_owner = capacity // LANES
    spots = 2 * per_owner
    mask = sea_mask.reshape(1, cells)
    state = ocean_state.transpose(1, 0, 2)
    far = lax.axis_index("far").astype(jnp.int32).reshape(1)

    def to_near(values):
        return lax.all_to_all(values, ("near", "sub"), split_axis=0, concat_axis=0, tiled=True)

    def to_far(values):
        return lax.ppermute(values, "far", ((0, 1), (1, 0)))

    place, spot, wanted, forcing_rows, tendency = start(
        near,
        per_owner,
        exchange_slot,
        parent_column,
        atmos_profiles,
        drag_factor,
        surface_before,
        downward_fluxes,
    )
    asked = to_near(wanted)
    other_rows = to_far(forcing_rows)
    base, first_level = top_level(state, ocean_mixing)
    asked, base, first_level = lax.optimization_barrier((asked, base, first_level))
    served = pl.pallas_call(
        functools.partial(serve_kernel, per_owner),
        in_specs=[smem, smem, hbm, hbm],
        out_specs=hbm,
        out_shape=jax.ShapeDtypeStruct((near, spots, fields, LANES), jnp.float32),
        scratch_shapes=[
            pltpu.VMEM((2, fields, columns), jnp.float32),
            pltpu.VMEM((near, spots, fields, LANES), jnp.float32),
            pltpu.SemaphoreType.DMA((2,)),
            pltpu.SemaphoreType.DMA((4,)),
        ],
        compiler_params=params,
        name="serve_windows",
    )(far, asked, forcing_rows, other_rows)
    served, columns_asked = lax.optimization_barrier((served, parent_column))
    arrived = to_near(served)
    rows = per_owner // fields
    windows = cells // LANES
    hot, shares = pl.pallas_call(
        hot_kernel,
        grid=(windows // GROUP,),
        in_specs=[smem] + [vmem] * 3,
        out_specs=[
            pl.BlockSpec((GROUP, 2 * LANES, 2 * LANES), lambda i: (i, 0, 0)),
            pl.BlockSpec((2 * near * rows, fields, LANES), lambda i: (0, 0, 0)),
        ],
        out_shape=[
            jax.ShapeDtypeStruct((windows, 2 * LANES, 2 * LANES), jnp.bfloat16),
            jax.ShapeDtypeStruct((2 * near * rows, fields, LANES), jnp.float32),
        ],
        scratch_shapes=[pltpu.VMEM((windows // GROUP, LANES, LANES), jnp.bfloat16)]
        + [pltpu.VMEM((2 * near * rows, fields, LANES), jnp.float32)] * intersections,
        compiler_params=middle_params,
        name="one_hot_and_shares",
    )(place, columns_asked, atmos_weight, mask)
    arrived, hot, shares = lax.optimization_barrier((arrived, hot, shares))
    sent = (near, per_owner + rows, fields, LANES)
    forcing, away, home = pl.pallas_call(
        middle_kernel,
        in_specs=[smem] * 4 + [vmem] * 7 + [hbm, vmem],
        out_specs=[vmem, hbm, hbm],
        out_shape=[
            jax.ShapeDtypeStruct((fields, cells), jnp.float32),
            jax.ShapeDtypeStruct(sent, jnp.float32),
            jax.ShapeDtypeStruct(sent, jnp.float32),
        ],
        scratch_shapes=[
            pltpu.VMEM((near * spots, fields, LANES), jnp.float32),
            pltpu.VMEM((windows, 2 * LANES, 2 * LANES), jnp.bfloat16),
            pltpu.SemaphoreType.DMA((windows,)),
            pltpu.SemaphoreType.DMA((4,)),
        ],
        compiler_params=middle_params,
        name="forcing_and_windows",
    )(
        far,
        place,
        spot,
        ocean_mixing,
        arrived.reshape(near * spots, fields, LANES),
        parent_column,
        ocean_weight,
        atmos_weight,
        mask,
        base,
        first_level,
        hot,
        shares.reshape(2, near, rows, fields, LANES),
    )
    tendency, forcing = lax.optimization_barrier((tendency, forcing))
    atmos_updated = diffuse_atmos(atmos_profiles, atmos_mixing, tendency)
    back_away, atmos_updated, home = lax.optimization_barrier(
        (to_near(away), atmos_updated, home)
    )
    back_home = to_near(home)
    sums_away = collect(asked, far, back_away, per_owner, columns, ())
    other_sums = to_far(sums_away)
    ocean_updated = diffuse_ocean(state, ocean_mixing, forcing, mask).transpose(1, 0, 2)
    back_home, ocean_updated = lax.optimization_barrier((back_home, ocean_updated))
    surface_state = collect(
        asked,
        far,
        back_home,
        per_owner,
        columns,
        (other_sums, land_weight.reshape(1, columns), land_surface),
    )
    return (atmos_updated, ocean_updated, surface_state)


def solution(mesh):
    comp, sub = mesh.devices.shape
    halves = jax.sharding.Mesh(mesh.devices.reshape(2, comp // 2, sub), AXES)
    split = P(None, AXES)
    return jax.shard_map(
        per_device,
        mesh=halves,
        in_specs=(
            P(None, None, AXES),
            P(),
            P(AXES),
            split,
            split,
            P(AXES),
            split,
            P(None, None, AXES),
            P(),
            P(AXES),
            split,
            split,
            split,
            split,
        ),
        out_specs=(P(None, None, AXES), P(None, None, AXES), split),
        check_vma=False,
    )
```

```python
import functools

import jax
import jax.numpy as jnp
from jax import lax
from jax.experimental import pallas as pl
from jax.experimental.pallas import tpu as pltpu
from jax.sharding import PartitionSpec as P

couple_rate = 0.5
LANES = 128
params = pltpu.CompilerParams(vmem_limit_bytes=24 * 1024 * 1024)
stream_params = pltpu.CompilerParams(vmem_limit_bytes=52 * 1024 * 1024)
middle_params = pltpu.CompilerParams(vmem_limit_bytes=48 * 1024 * 1024)
first_params = pltpu.CompilerParams(vmem_limit_bytes=56 * 1024 * 1024)
vmem = pl.BlockSpec(memory_space=pltpu.VMEM)
smem = pl.BlockSpec(memory_space=pltpu.SMEM)
hbm = pl.BlockSpec(memory_space=pl.ANY)
AXES = ("far", "near", "sub")


def window(index):
    return pl.ds(pl.multiple_of(index * LANES, LANES), LANES)


def make_requests(per_owner, slot_ref, column_ref, place_ref, spot_ref, wanted_ref):
    intersections, cells = slot_ref.shape
    near, spots = wanted_ref.shape
    windows = cells // LANES
    lane = lax.broadcasted_iota(jnp.int32, (intersections, windows), 1)

    def heads(ref):
        found = jnp.zeros((intersections, windows), jnp.int32)
        for step in range(windows):
            head = ref[:, step * LANES : step * LANES + 1]
            found = jnp.where(lane == step, head, found)
        return found // LANES

    place = heads(slot_ref)
    column_window = heads(column_ref)
    owner = place // per_owner
    peer = owner % near
    spot = owner // near * per_owner + place % per_owner
    place_ref[...] = place
    spot_ref[...] = peer * spots + spot
    peer_ids = lax.broadcasted_iota(jnp.int32, (near, windows), 0)
    spot_ids = lax.broadcasted_iota(jnp.int32, (spots, windows), 0)
    wanted = jnp.zeros((near, spots), jnp.float32)
    for k in range(intersections):
        row = slice(k, k + 1)
        peer_hot = jnp.where(peer_ids == peer[row], 1.0, 0.0)
        spot_hot = jnp.where(
            spot_ids == spot[row], column_window[row].astype(jnp.float32), 0.0
        )
        wanted = wanted + lax.dot_general(
            peer_hot.astype(jnp.bfloat16),
            spot_hot.astype(jnp.bfloat16),
            (((1,), (1,)), ((), ())),
            preferred_element_type=jnp.float32,
        )
    wanted_ref[...] = wanted.astype(jnp.int32)


def start_kernel(
    last,
    per_owner,
    slot_ref,
    column_ref,
    x_ref,
    drag_ref,
    before_ref,
    down_ref,
    place_ref,
    spot_ref,
    wanted_ref,
    forcing_ref,
    tend_ref,
):
    @pl.when(pl.program_id(0) == 0)
    def _():
        make_requests(per_owner, slot_ref, column_ref, place_ref, spot_ref, wanted_ref)

    def row(ref, index):
        return ref[index : index + 1, :]

    bottom = [x_ref[member].astype(jnp.float32)[last : last + 1, :] for member in range(4)]
    east = bottom[2] - row(before_ref, 2)
    north = bottom[3] - row(before_ref, 3)
    transfer = drag_ref[...] * jnp.sqrt(1.0 + east * east + north * north)
    sensible = transfer * (row(before_ref, 0) - bottom[0])
    latent = transfer * (row(before_ref, 1) - bottom[1])
    east_stress = couple_rate * (transfer * east)
    north_stress = couple_rate * (transfer * north)
    forcing_ref[0:1, :] = couple_rate * (
        row(down_ref, 0) + row(down_ref, 1) - sensible - latent
    )
    forcing_ref[1:2, :] = couple_rate * (latent - row(down_ref, 2) - row(down_ref, 3))
    forcing_ref[2:3, :] = east_stress
    forcing_ref[3:4, :] = north_stress
    tend_ref[0:1, :] = couple_rate * sensible
    tend_ref[1:2, :] = couple_rate * latent
    tend_ref[2:3, :] = -east_stress
    tend_ref[3:4, :] = -north_stress


def start(near, per_owner, slots, parents, profiles, drag_factor, surface_before, downward):
    fields, levels, columns = profiles.shape
    intersections, cells = slots.shape
    block = min(4096, columns)
    tall = 16
    at = (levels - 1) // tall
    rows = pl.BlockSpec((fields, block), lambda i: (0, i))
    tiles = (intersections, cells // LANES)
    asked = (near, 2 * per_owner)

    def whole(shape):
        return pl.BlockSpec(shape, lambda i: (0, 0))

    return pl.pallas_call(
        functools.partial(start_kernel, levels - 1 - at * tall, per_owner),
        grid=(columns // block,),
        in_specs=[
            whole(slots.shape),
            whole(slots.shape),
            pl.BlockSpec((fields, tall, block), lambda i: (0, at, i)),
            pl.BlockSpec((1, block), lambda i: (0, i)),
            rows,
            rows,
        ],
        out_specs=[whole(tiles), whole(tiles), whole(asked), rows, rows],
        out_shape=[
            jax.ShapeDtypeStruct(tiles, jnp.int32),
            jax.ShapeDtypeStruct(tiles, jnp.int32),
            jax.ShapeDtypeStruct(asked, jnp.int32),
            jax.ShapeDtypeStruct((fields, columns), jnp.float32),
            jax.ShapeDtypeStruct((fields, columns), jnp.float32),
        ],
        compiler_params=first_params,
        name="requests_and_rates",
    )(slots, parents, profiles, drag_factor.reshape(1, columns), surface_before, downward)


def atmos_kernel(mix_ref, tend_ref, *refs):
    mix = mix_ref[...]
    lowest = mix[:, mix.shape[1] - 1 :].astype(jnp.float32)
    out_ref = refs[-1]
    for member, x_ref in enumerate(refs[:-1]):
        mixed = jnp.dot(mix, x_ref[0], preferred_element_type=jnp.float32)
        out_ref[member] = (mixed + lowest * tend_ref[member : member + 1, :]).astype(jnp.bfloat16)


def diffuse_atmos(profiles, mixing, tendency):
    fields, levels, columns = profiles.shape
    block = min(2048, columns)

    def field(member):
        return pl.BlockSpec((1, levels, block), lambda i: (member, 0, i))

    return pl.pallas_call(
        atmos_kernel,
        grid=(columns // block,),
        in_specs=[
            pl.BlockSpec((levels, levels), lambda i: (0, 0)),
            pl.BlockSpec((fields, block), lambda i: (0, i)),
        ]
        + [field(member) for member in range(fields)],
        out_specs=pl.BlockSpec((fields, levels, block), lambda i: (0, 0, i)),
        out_shape=jax.ShapeDtypeStruct(profiles.shape, jnp.bfloat16),
        compiler_params=stream_params,
        cost_estimate=pl.CostEstimate(
            flops=2 * fields * levels * levels * columns,
            bytes_accessed=4 * fields * levels * columns,
            transcendentals=0,
        ),
        name="diffuse_atmos",
    )(mixing, tendency, *[profiles] * fields)


def level_specs(levels, fields, block):
    count = 4 if levels % 4 == 0 else 1

    def part(number):
        return pl.BlockSpec((levels // count, fields, block), lambda i: (number, 0, i))

    return [part(number) for number in range(count)]


def top_kernel(mix_ref, *refs):
    state_refs, base_ref, first_ref = refs[:-2], refs[-2], refs[-1]
    total = None
    level = 0
    for ref in state_refs:
        for inner in range(ref.shape[0]):
            term = mix_ref[0, level] * ref[inner]
            total = term if total is None else total + term
            level += 1
    base_ref[...] = total
    first_ref[...] = state_refs[0][0]


def top_level(state, mixing):
    levels, fields, cells = state.shape
    block = min(2048, cells)
    specs = level_specs(levels, fields, block)
    return pl.pallas_call(
        top_kernel,
        grid=(cells // block,),
        in_specs=[smem] + specs,
        out_specs=[pl.BlockSpec((fields, block), lambda i: (0, i))] * 2,
        out_shape=[jax.ShapeDtypeStruct((fields, cells), jnp.float32)] * 2,
        compiler_params=stream_params,
        cost_estimate=pl.CostEstimate(
            flops=2 * fields * levels * cells,
            bytes_accessed=4 * fields * levels * cells,
            transcendentals=0,
        ),
        name="top_level",
    )(mixing, *[state] * len(specs))


def serve_kernel(
    per_owner,
    far_ref,
    asked_ref,
    own_ref,
    other_ref,
    out_ref,
    blocks_ref,
    filled_ref,
    arrived_sem,
    sent_sem,
):
    copies = [
        pltpu.make_async_copy(ref, blocks_ref.at[index], arrived_sem.at[index])
        for index, ref in enumerate((own_ref, other_ref))
    ]
    for copy in copies:
        copy.start()
    for copy in copies:
        copy.wait()
    far = far_ref[0]

    def body(peer, carry):
        for shard in range(2):
            for slot in range(per_owner):
                spot = shard * per_owner + slot
                filled_ref[peer, spot] = blocks_ref[
                    shard ^ far, :, window(asked_ref[peer, spot])
                ]
        return carry

    sends = []
    parts = sent_sem.shape[0]
    peers = filled_ref.shape[0] // parts
    for part in range(parts):
        lax.fori_loop(part * peers, (part + 1) * peers, body, 0)
        at = pl.ds(part * peers, peers)
        send = pltpu.make_async_copy(filled_ref.at[at], out_ref.at[at], sent_sem.at[part])
        send.start()
        sends.append(send)
    for send in sends:
        send.wait()


def split_high(values):
    high = values.astype(jnp.bfloat16).astype(jnp.float32)
    return jnp.concatenate([high, values - high], axis=0)


GROUP = 8
hot_type = jnp.float8_e4m3fn


def hot_kernel(
    place_ref,
    column_ref,
    atmos_weight_ref,
    mask_ref,
    hot_ref,
    share_ref,
    lanes_ref,
    *sums,
):
    intersections, cells = column_ref.shape
    windows = cells // LANES
    fields = share_ref.shape[1]
    group_tiles = GROUP * intersections
    steps = LANES // intersections
    group = pl.program_id(0)
    @pl.when(group == 0)
    def _():
        for ref in sums:
            ref[...] = jnp.zeros(ref.shape, jnp.float32)
        for first in range(0, windows, steps):
            tall = jnp.concatenate(
                [
                    column_ref[:, (first + step) * LANES : (first + step + 1) * LANES] & (LANES - 1)
                    for step in range(steps)
                ],
                axis=0,
            )
            turned = tall.astype(jnp.float32).T.astype(jnp.bfloat16)
            for part in range(steps // GROUP):
                lanes_ref[first // GROUP + part, :, :group_tiles] = turned[
                    :, part * group_tiles : (part + 1) * group_tiles
                ]

    column_ids = lax.broadcasted_iota(jnp.int32, (LANES, LANES), 1)
    column_ids = column_ids.astype(jnp.float32).astype(jnp.bfloat16)
    one, zero = jnp.bfloat16(1.0), jnp.bfloat16(0.0)
    field_ids = lax.broadcasted_iota(jnp.int32, (fields, LANES), 0)
    share_rows = lax.broadcasted_iota(jnp.int32, (2 * intersections, LANES), 0)
    first_half = share_rows % intersections < 2

    turned = lanes_ref[group]
    for inner in range(GROUP):
        step = group * GROUP + inner
        here = window(step)
        share = atmos_weight_ref[:, here] * mask_ref[:, here].astype(jnp.float32)
        hot = []
        for k in range(intersections):
            tile = inner * intersections + k
            lane_of = jnp.broadcast_to(turned[:, tile : tile + 1], (LANES, LANES))
            hot.append(jnp.where(lane_of == column_ids, one, zero))
        hot = jnp.concatenate(
            [
                jnp.concatenate([hot[0], hot[1]], axis=1),
                jnp.concatenate([hot[2], hot[3]], axis=1),
            ],
            axis=0,
        )
        hot_ref[inner] = hot.astype(hot_type)
        parts = split_high(share)
        rows = jnp.concatenate(
            [jnp.where(first_half, parts, 0.0), jnp.where(first_half, 0.0, parts)], axis=1
        ).astype(jnp.bfloat16)
        spread = jnp.dot(rows, hot, preferred_element_type=jnp.float32)
        for k in range(intersections):
            side = slice((k % 2) * LANES, (k % 2 + 1) * LANES)
            low = intersections + k
            shared = spread[k : k + 1, side] + spread[low : low + 1, side]
            place = place_ref[k, step]
            sums[k][lax.div(place, fields)] += jnp.where(
                field_ids == lax.rem(place, fields), shared, 0.0
            )

    @pl.when(group == pl.num_programs(0) - 1)
    def _():
        total = sums[0][...]
        for ref in sums[1:]:
            total = total + ref[...]
        share_ref[...] = total


def middle_kernel(
    far_ref,
    place_ref,
    spot_ref,
    mix_ref,
    arrived_ref,
    column_ref,
    ocean_weight_ref,
    atmos_weight_ref,
    mask_ref,
    base_ref,
    state_ref,
    hot_ref,
    share_ref,
    forcing_ref,
    send_ref,
    value_ref,
    held_ref,
    held_sem,
    sent_sem,
):
    intersections, cells = column_ref.shape
    windows = cells // LANES
    fields = base_ref.shape[0]
    near, _, packed = send_ref.shape[:3]
    per_owner = packed * fields // (fields + 1)
    rows = per_owner // fields

    def fetch(group):
        part = pl.ds(group * GROUP, GROUP)
        return pltpu.make_async_copy(hot_ref.at[part], held_ref.at[part], held_sem.at[group])

    groups = windows // GROUP
    for group in range(groups):
        fetch(group).start()
    value_ref[...] = jnp.zeros(value_ref.shape, jnp.float32)
    corner = mix_ref[0, 0]
    blank = jnp.zeros((2 * fields, LANES), jnp.float32)

    def body(group, carry):
        fetch(group).wait()
        for inner in range(GROUP):
            step = group * GROUP + inner
            here = window(step)
            lanes = column_ref[:, here] & (LANES - 1)
            ocean_weight = ocean_weight_ref[:, here]
            total = jnp.zeros((fields, LANES), jnp.float32)
            weight = jnp.zeros((1, LANES), jnp.float32)
            for k in range(intersections):
                picked = jnp.take_along_axis(
                    arrived_ref[spot_ref[k, step]],
                    jnp.broadcast_to(lanes[k : k + 1], (fields, LANES)),
                    axis=1,
                    mode="promise_in_bounds",
                )
                total = total + ocean_weight[k : k + 1] * picked
                weight = weight + ocean_weight[k : k + 1]
            forcing = total / weight
            forcing_ref[:, here] = forcing
            mask = mask_ref[:, here]
            surface = jnp.where(
                mask == 1, base_ref[:, here] + corner * forcing, state_ref[:, here]
            )
            share = atmos_weight_ref[:, here] * mask.astype(jnp.float32)
            parts = [split_high(share[k : k + 1] * surface) for k in range(intersections)]
            left = [parts[0], parts[1], blank, blank]
            right = [blank, blank, parts[2], parts[3]]
            parts = jnp.concatenate(
                [jnp.concatenate(left, axis=0), jnp.concatenate(right, axis=0)], axis=1
            ).astype(jnp.bfloat16)
            spread = jnp.dot(
                parts, held_ref[step].astype(jnp.bfloat16), preferred_element_type=jnp.float32
            )
            for k in range(intersections):
                side = slice((k % 2) * LANES, (k % 2 + 1) * LANES)
                at = 2 * fields * k
                value_ref[place_ref[k, step]] = (
                    spread[at : at + fields, side] + spread[at + fields : at + 2 * fields, side]
                )
        return carry

    lax.fori_loop(0, groups, body, 0)
    far = far_ref[0]
    shards = value_ref.reshape(2, near, per_owner, fields, LANES)
    copies = []
    for index, shard in enumerate((1 - far, far)):
        copies.append(
            pltpu.make_async_copy(
                shards.at[shard],
                send_ref.at[:, index, pl.ds(0, per_owner)],
                sent_sem.at[2 * index],
            )
        )
        copies.append(
            pltpu.make_async_copy(
                share_ref.at[shard],
                send_ref.at[:, index, pl.ds(per_owner, rows)],
                sent_sem.at[2 * index + 1],
            )
        )
    for copy in copies:
        copy.start()
    for copy in copies:
        copy.wait()


def ocean_kernel(mix_ref, forcing_ref, mask_ref, *refs):
    x_refs, (out_ref, high_ref, low_ref) = refs[:-3], refs[-3:]
    levels, fields, block = out_ref.shape
    rows = levels * fields

    @pl.when(pl.program_id(0) == 0)
    def _():
        level = lax.broadcasted_iota(jnp.int32, (rows, levels), 0) // fields
        pick = (level == lax.broadcasted_iota(jnp.int32, (rows, levels), 1)).astype(jnp.float32)
        tall = jnp.dot(pick, mix_ref[...], precision=lax.Precision.HIGHEST)
        wide = lax.dot_general(
            tall, pick, (((1,), (1,)), ((), ())), precision=lax.Precision.HIGHEST
        )
        down = lax.broadcasted_iota(jnp.int32, (rows, rows), 0) % fields
        across = lax.broadcasted_iota(jnp.int32, (rows, rows), 1) % fields
        wide = jnp.where(down == across, wide, 0.0)
        high = wide.astype(jnp.bfloat16)
        high_ref[...] = high
        low_ref[...] = (wide - high.astype(jnp.float32)).astype(jnp.bfloat16)

    flat = jnp.concatenate(
        [ref[...].reshape(rows // len(x_refs), block) for ref in x_refs], axis=0
    )
    push = jnp.concatenate(
        [forcing_ref[...], jnp.zeros((rows - fields, block), jnp.float32)], axis=0
    )
    loaded = flat + push
    high = loaded.astype(jnp.bfloat16)
    low = (loaded - high.astype(jnp.float32)).astype(jnp.bfloat16)
    mixed = (
        jnp.dot(high_ref[...], high, preferred_element_type=jnp.float32)
        + jnp.dot(high_ref[...], low, preferred_element_type=jnp.float32)
        + jnp.dot(low_ref[...], high, preferred_element_type=jnp.float32)
    )
    out_ref[...] = jnp.where(mask_ref[...] == 1, mixed, flat).reshape(levels, fields, block)


def diffuse_ocean(state, mixing, forcing, mask):
    levels, fields, cells = state.shape
    block = min(1024, cells)
    rows = levels * fields
    specs = level_specs(levels, fields, block)
    return pl.pallas_call(
        ocean_kernel,
        grid=(cells // block,),
        in_specs=[
            pl.BlockSpec(mixing.shape, lambda i: (0, 0)),
            pl.BlockSpec((fields, block), lambda i: (0, i)),
            pl.BlockSpec((1, block), lambda i: (0, i)),
        ]
        + specs,
        out_specs=pl.BlockSpec((levels, fields, block), lambda i: (0, 0, i)),
        out_shape=jax.ShapeDtypeStruct(state.shape, jnp.float32),
        scratch_shapes=[pltpu.VMEM((rows, rows), jnp.bfloat16)] * 2,
        compiler_params=stream_params,
        cost_estimate=pl.CostEstimate(
            flops=6 * rows * rows * cells,
            bytes_accessed=8 * rows * cells,
            transcendentals=0,
        ),
        name="diffuse_ocean",
    )(mixing, forcing, mask, *[state] * len(specs))


def collect_kernel(per_owner, home, far_ref, asked_ref, back_ref, out_ref, *sums):
    near, _, _, fields, _ = back_ref.shape
    columns = sums[0].shape[1]
    quarter = columns // fields
    chains = len(sums) // 2
    half = 1 if home else 0
    far = far_ref[0]
    first = (far if home else 1 - far) * per_owner
    for ref in sums:
        ref[...] = jnp.zeros(ref.shape, jnp.float32)

    def body(step, carry):
        for slot in range(per_owner):
            for chain in range(chains):
                peer = step * chains + chain
                at = window(asked_ref[peer, first + slot])
                tile, row = per_owner + slot // fields, slot % fields
                sums[chain][:, at] += back_ref[peer, half, slot]
                sums[chains + chain][:, at] += back_ref[peer, half, tile, row : row + 1]
        return carry

    lax.fori_loop(0, near // chains, body, 0)
    values, shares = sums[0][...], sums[chains][...]
    for chain in range(1, chains):
        values = values + sums[chain][...]
        shares = shares + sums[chains + chain][...]
    out_ref[:, :columns] = values
    for row in range(fields):
        out_ref[row : row + 1, columns:] = shares[:, row * quarter : (row + 1) * quarter]


def collect(asked, far, back, per_owner, columns, home):
    fields = back.shape[3]
    chains = 4
    return pl.pallas_call(
        functools.partial(collect_kernel, per_owner, home),
        in_specs=[smem, smem, vmem],
        out_specs=vmem,
        out_shape=jax.ShapeDtypeStruct((fields, columns + columns // fields), jnp.float32),
        scratch_shapes=[pltpu.VMEM((fields, columns), jnp.float32)] * chains
        + [pltpu.VMEM((1, columns), jnp.float32)] * chains,
        compiler_params=params,
        name="collect_home" if home else "collect_away",
    )(far, asked, back)


def final_kernel(keep_ref, other_ref, land_weight_ref, land_ref, out_ref):
    fields, columns = out_ref.shape
    quarter = columns // fields
    both = keep_ref[:, :columns] + other_ref[:, :columns]
    shares = keep_ref[:, columns:] + other_ref[:, columns:]
    land_weight = land_weight_ref[...]
    total = both + land_weight * land_ref[...]
    for row in range(fields):
        part = slice(row * quarter, (row + 1) * quarter)
        out_ref[:, part] = total[:, part] / (shares[row : row + 1] + land_weight[:, part])


def per_device(
    atmos_profiles,
    atmos_mixing,
    drag_factor,
    surface_before,
    downward_fluxes,
    land_weight,
    land_surface,
    ocean_state,
    ocean_mixing,
    sea_mask,
    exchange_slot,
    parent_column,
    ocean_weight,
    atmos_weight,
):
    near = lax.axis_size("near") * lax.axis_size("sub")
    devices = 2 * near
    fields, _, columns = atmos_profiles.shape
    intersections, cells = exchange_slot.shape
    capacity = 2 * intersections * cells // devices
    per_owner = capacity // LANES
    spots = 2 * per_owner
    mask = sea_mask.reshape(1, cells)
    state = ocean_state.transpose(1, 0, 2)
    far = lax.axis_index("far").astype(jnp.int32).reshape(1)

    def to_near(values):
        return lax.all_to_all(values, ("near", "sub"), split_axis=0, concat_axis=0, tiled=True)

    def to_far(values):
        return lax.ppermute(values, "far", ((0, 1), (1, 0)))

    place, spot, wanted, forcing_rows, tendency = start(
        near,
        per_owner,
        exchange_slot,
        parent_column,
        atmos_profiles,
        drag_factor,
        surface_before,
        downward_fluxes,
    )
    asked = to_near(wanted)
    other_rows = to_far(forcing_rows)
    base, first_level = top_level(state, ocean_mixing)
    asked, base, first_level = lax.optimization_barrier((asked, base, first_level))
    served = pl.pallas_call(
        functools.partial(serve_kernel, per_owner),
        in_specs=[smem, smem, hbm, hbm],
        out_specs=hbm,
        out_shape=jax.ShapeDtypeStruct((near, spots, fields, LANES), jnp.float32),
        scratch_shapes=[
            pltpu.VMEM((2, fields, columns), jnp.float32),
            pltpu.VMEM((near, spots, fields, LANES), jnp.float32),
            pltpu.SemaphoreType.DMA((2,)),
            pltpu.SemaphoreType.DMA((4,)),
        ],
        compiler_params=params,
        name="serve_windows",
    )(far, asked, forcing_rows, other_rows)
    served, columns_asked = lax.optimization_barrier((served, parent_column))
    arrived = to_near(served)
    rows = per_owner // fields
    windows = cells // LANES
    hot, shares = pl.pallas_call(
        hot_kernel,
        grid=(windows // GROUP,),
        in_specs=[smem] + [vmem] * 3,
        out_specs=[
            pl.BlockSpec((GROUP, 2 * LANES, 2 * LANES), lambda i: (i, 0, 0)),
            pl.BlockSpec((2 * near * rows, fields, LANES), lambda i: (0, 0, 0)),
        ],
        out_shape=[
            jax.ShapeDtypeStruct((windows, 2 * LANES, 2 * LANES), hot_type),
            jax.ShapeDtypeStruct((2 * near * rows, fields, LANES), jnp.float32),
        ],
        scratch_shapes=[pltpu.VMEM((windows // GROUP, LANES, LANES), jnp.bfloat16)]
        + [pltpu.VMEM((2 * near * rows, fields, LANES), jnp.float32)] * intersections,
        compiler_params=middle_params,
        name="one_hot_and_shares",
    )(place, columns_asked, atmos_weight, mask)
    arrived, hot, shares = lax.optimization_barrier((arrived, hot, shares))
    sent = (near, 2, per_owner + rows, fields, LANES)
    forcing, send = pl.pallas_call(
        middle_kernel,
        in_specs=[smem] * 4 + [vmem] * 7 + [hbm, vmem],
        out_specs=[vmem, hbm],
        out_shape=[
            jax.ShapeDtypeStruct((fields, cells), jnp.float32),
            jax.ShapeDtypeStruct(sent, jnp.float32),
        ],
        scratch_shapes=[
            pltpu.VMEM((near * spots, fields, LANES), jnp.float32),
            pltpu.VMEM((windows, 2 * LANES, 2 * LANES), hot_type),
            pltpu.SemaphoreType.DMA((windows // GROUP,)),
            pltpu.SemaphoreType.DMA((4,)),
        ],
        compiler_params=middle_params,
        name="forcing_and_windows",
    )(
        far,
        place,
        spot,
        ocean_mixing,
        arrived.reshape(near * spots, fields, LANES),
        parent_column,
        ocean_weight,
        atmos_weight,
        mask,
        base,
        first_level,
        hot,
        shares.reshape(2, near, rows, fields, LANES),
    )
    ocean_updated = diffuse_ocean(state, ocean_mixing, forcing, mask).transpose(1, 0, 2)
    back, ocean_updated = lax.optimization_barrier((to_near(send), ocean_updated))
    sums_away = collect(asked, far, back, per_owner, columns, False)
    sums_away, back, tendency = lax.optimization_barrier((sums_away, back, tendency))
    other_sums = to_far(sums_away)
    sums_home = collect(asked, far, back, per_owner, columns, True)
    atmos_updated = diffuse_atmos(atmos_profiles, atmos_mixing, tendency)
    other_sums, sums_home, atmos_updated = lax.optimization_barrier(
        (other_sums, sums_home, atmos_updated)
    )
    surface_state = pl.pallas_call(
        final_kernel,
        in_specs=[vmem] * 4,
        out_specs=vmem,
        out_shape=jax.ShapeDtypeStruct((fields, columns), jnp.float32),
        compiler_params=params,
        name="surface_state",
    )(sums_home, other_sums, land_weight.reshape(1, columns), land_surface)
    return (atmos_updated, ocean_updated, surface_state)


def solution(mesh):
    comp, sub = mesh.devices.shape
    halves = jax.sharding.Mesh(mesh.devices.reshape(2, comp // 2, sub), AXES)
    split = P(None, AXES)
    return jax.shard_map(
        per_device,
        mesh=halves,
        in_specs=(
            P(None, None, AXES),
            P(),
            P(AXES),
            split,
            split,
            P(AXES),
            split,
            P(None, None, AXES),
            P(),
            P(AXES),
            split,
            split,
            split,
            split,
        ),
        out_specs=(P(None, None, AXES), P(None, None, AXES), split),
        check_vma=False,
    )
```

```python
import functools

import jax
import jax.numpy as jnp
from jax import lax
from jax.experimental import pallas as pl
from jax.experimental.pallas import tpu as pltpu
from jax.sharding import PartitionSpec as P

couple_rate = 0.5
LANES = 128
params = pltpu.CompilerParams(vmem_limit_bytes=24 * 1024 * 1024)
stream_params = pltpu.CompilerParams(vmem_limit_bytes=52 * 1024 * 1024)
middle_params = pltpu.CompilerParams(vmem_limit_bytes=48 * 1024 * 1024)
first_params = pltpu.CompilerParams(vmem_limit_bytes=56 * 1024 * 1024)
vmem = pl.BlockSpec(memory_space=pltpu.VMEM)
smem = pl.BlockSpec(memory_space=pltpu.SMEM)
hbm = pl.BlockSpec(memory_space=pl.ANY)
AXES = ("far", "near", "sub")


def window(index):
    return pl.ds(pl.multiple_of(index * LANES, LANES), LANES)


def make_requests(per_owner, slot_ref, column_ref, place_ref, spot_ref, wanted_ref):
    intersections, cells = slot_ref.shape
    near, spots = wanted_ref.shape
    windows = cells // LANES
    lane = lax.broadcasted_iota(jnp.int32, (intersections, windows), 1)

    def heads(ref):
        found = jnp.zeros((intersections, windows), jnp.int32)
        for step in range(windows):
            head = ref[:, step * LANES : step * LANES + 1]
            found = jnp.where(lane == step, head, found)
        return found // LANES

    place = heads(slot_ref)
    column_window = heads(column_ref)
    owner = place // per_owner
    peer = owner % near
    spot = owner // near * per_owner + place % per_owner
    place_ref[...] = place
    spot_ref[...] = peer * spots + spot
    peer_ids = lax.broadcasted_iota(jnp.int32, (near, windows), 0)
    spot_ids = lax.broadcasted_iota(jnp.int32, (spots, windows), 0)
    wanted = jnp.zeros((near, spots), jnp.float32)
    for k in range(intersections):
        row = slice(k, k + 1)
        peer_hot = jnp.where(peer_ids == peer[row], 1.0, 0.0)
        spot_hot = jnp.where(
            spot_ids == spot[row], column_window[row].astype(jnp.float32), 0.0
        )
        wanted = wanted + lax.dot_general(
            peer_hot.astype(jnp.bfloat16),
            spot_hot.astype(jnp.bfloat16),
            (((1,), (1,)), ((), ())),
            preferred_element_type=jnp.float32,
        )
    wanted_ref[...] = wanted.astype(jnp.int32)


def start_kernel(
    last,
    per_owner,
    slot_ref,
    column_ref,
    x_ref,
    drag_ref,
    before_ref,
    down_ref,
    place_ref,
    spot_ref,
    wanted_ref,
    forcing_ref,
    tend_ref,
):
    @pl.when(pl.program_id(0) == 0)
    def _():
        make_requests(per_owner, slot_ref, column_ref, place_ref, spot_ref, wanted_ref)

    def row(ref, index):
        return ref[index : index + 1, :]

    bottom = [x_ref[member].astype(jnp.float32)[last : last + 1, :] for member in range(4)]
    east = bottom[2] - row(before_ref, 2)
    north = bottom[3] - row(before_ref, 3)
    transfer = drag_ref[...] * jnp.sqrt(1.0 + east * east + north * north)
    sensible = transfer * (row(before_ref, 0) - bottom[0])
    latent = transfer * (row(before_ref, 1) - bottom[1])
    east_stress = couple_rate * (transfer * east)
    north_stress = couple_rate * (transfer * north)
    forcing_ref[0:1, :] = couple_rate * (
        row(down_ref, 0) + row(down_ref, 1) - sensible - latent
    )
    forcing_ref[1:2, :] = couple_rate * (latent - row(down_ref, 2) - row(down_ref, 3))
    forcing_ref[2:3, :] = east_stress
    forcing_ref[3:4, :] = north_stress
    tend_ref[0:1, :] = couple_rate * sensible
    tend_ref[1:2, :] = couple_rate * latent
    tend_ref[2:3, :] = -east_stress
    tend_ref[3:4, :] = -north_stress


def start(near, per_owner, slots, parents, profiles, drag_factor, surface_before, downward):
    fields, levels, columns = profiles.shape
    intersections, cells = slots.shape
    block = min(4096, columns)
    tall = 16
    at = (levels - 1) // tall
    rows = pl.BlockSpec((fields, block), lambda i: (0, i))
    tiles = (intersections, cells // LANES)
    asked = (near, 2 * per_owner)

    def whole(shape):
        return pl.BlockSpec(shape, lambda i: (0, 0))

    return pl.pallas_call(
        functools.partial(start_kernel, levels - 1 - at * tall, per_owner),
        grid=(columns // block,),
        in_specs=[
            whole(slots.shape),
            whole(slots.shape),
            pl.BlockSpec((fields, tall, block), lambda i: (0, at, i)),
            pl.BlockSpec((1, block), lambda i: (0, i)),
            rows,
            rows,
        ],
        out_specs=[whole(tiles), whole(tiles), whole(asked), rows, rows],
        out_shape=[
            jax.ShapeDtypeStruct(tiles, jnp.int32),
            jax.ShapeDtypeStruct(tiles, jnp.int32),
            jax.ShapeDtypeStruct(asked, jnp.int32),
            jax.ShapeDtypeStruct((fields, columns), jnp.float32),
            jax.ShapeDtypeStruct((fields, columns), jnp.float32),
        ],
        compiler_params=first_params,
        name="requests_and_rates",
    )(slots, parents, profiles, drag_factor.reshape(1, columns), surface_before, downward)


def atmos_kernel(mix_ref, tend_ref, *refs):
    mix = mix_ref[...]
    lowest = mix[:, mix.shape[1] - 1 :].astype(jnp.float32)
    out_ref = refs[-1]
    for member, x_ref in enumerate(refs[:-1]):
        mixed = jnp.dot(mix, x_ref[0], preferred_element_type=jnp.float32)
        out_ref[member] = (mixed + lowest * tend_ref[member : member + 1, :]).astype(jnp.bfloat16)


def diffuse_atmos(profiles, mixing, tendency):
    fields, levels, columns = profiles.shape
    block = min(2048, columns)

    def field(member):
        return pl.BlockSpec((1, levels, block), lambda i: (member, 0, i))

    return pl.pallas_call(
        atmos_kernel,
        grid=(columns // block,),
        in_specs=[
            pl.BlockSpec((levels, levels), lambda i: (0, 0)),
            pl.BlockSpec((fields, block), lambda i: (0, i)),
        ]
        + [field(member) for member in range(fields)],
        out_specs=pl.BlockSpec((fields, levels, block), lambda i: (0, 0, i)),
        out_shape=jax.ShapeDtypeStruct(profiles.shape, jnp.bfloat16),
        compiler_params=stream_params,
        cost_estimate=pl.CostEstimate(
            flops=2 * fields * levels * levels * columns,
            bytes_accessed=4 * fields * levels * columns,
            transcendentals=0,
        ),
        name="diffuse_atmos",
    )(mixing, tendency, *[profiles] * fields)


def level_specs(levels, fields, block):
    count = 4 if levels % 4 == 0 else 1

    def part(number):
        return pl.BlockSpec((levels // count, fields, block), lambda i: (number, 0, i))

    return [part(number) for number in range(count)]


def top_kernel(mix_ref, *refs):
    state_refs, base_ref, first_ref = refs[:-2], refs[-2], refs[-1]
    total = None
    level = 0
    for ref in state_refs:
        for inner in range(ref.shape[0]):
            term = mix_ref[0, level] * ref[inner]
            total = term if total is None else total + term
            level += 1
    base_ref[...] = total
    first_ref[...] = state_refs[0][0]


def top_level(state, mixing):
    levels, fields, cells = state.shape
    block = min(2048, cells)
    specs = level_specs(levels, fields, block)
    return pl.pallas_call(
        top_kernel,
        grid=(cells // block,),
        in_specs=[smem] + specs,
        out_specs=[pl.BlockSpec((fields, block), lambda i: (0, i))] * 2,
        out_shape=[jax.ShapeDtypeStruct((fields, cells), jnp.float32)] * 2,
        compiler_params=stream_params,
        cost_estimate=pl.CostEstimate(
            flops=2 * fields * levels * cells,
            bytes_accessed=4 * fields * levels * cells,
            transcendentals=0,
        ),
        name="top_level",
    )(mixing, *[state] * len(specs))


def serve_kernel(
    per_owner,
    far_ref,
    asked_ref,
    own_ref,
    other_ref,
    out_ref,
    blocks_ref,
    filled_ref,
    arrived_sem,
    sent_sem,
):
    copies = [
        pltpu.make_async_copy(ref, blocks_ref.at[index], arrived_sem.at[index])
        for index, ref in enumerate((own_ref, other_ref))
    ]
    for copy in copies:
        copy.start()
    for copy in copies:
        copy.wait()
    far = far_ref[0]

    def body(peer, carry):
        for shard in range(2):
            for slot in range(per_owner):
                spot = shard * per_owner + slot
                filled_ref[peer, spot] = blocks_ref[
                    shard ^ far, :, window(asked_ref[peer, spot])
                ]
        return carry

    sends = []
    parts = sent_sem.shape[0]
    peers = filled_ref.shape[0] // parts
    for part in range(parts):
        lax.fori_loop(part * peers, (part + 1) * peers, body, 0)
        at = pl.ds(part * peers, peers)
        send = pltpu.make_async_copy(filled_ref.at[at], out_ref.at[at], sent_sem.at[part])
        send.start()
        sends.append(send)
    for send in sends:
        send.wait()


def split_high(values):
    high = values.astype(jnp.bfloat16).astype(jnp.float32)
    return jnp.concatenate([high, values - high], axis=0)


GROUP = 8
hot_type = jnp.float8_e4m3fn


def hot_kernel(
    place_ref,
    column_ref,
    atmos_weight_ref,
    mask_ref,
    hot_ref,
    share_ref,
    lanes_ref,
    *sums,
):
    intersections, cells = column_ref.shape
    windows = cells // LANES
    fields = share_ref.shape[1]
    group_tiles = GROUP * intersections
    steps = LANES // intersections
    group = pl.program_id(0)
    @pl.when(group == 0)
    def _():
        for ref in sums:
            ref[...] = jnp.zeros(ref.shape, jnp.float32)
        for first in range(0, windows, steps):
            tall = jnp.concatenate(
                [
                    column_ref[:, (first + step) * LANES : (first + step + 1) * LANES] & (LANES - 1)
                    for step in range(steps)
                ],
                axis=0,
            )
            turned = tall.astype(jnp.float32).T.astype(jnp.bfloat16)
            for part in range(steps // GROUP):
                lanes_ref[first // GROUP + part, :, :group_tiles] = turned[
                    :, part * group_tiles : (part + 1) * group_tiles
                ]

    column_ids = lax.broadcasted_iota(jnp.int32, (LANES, LANES), 1)
    column_ids = column_ids.astype(jnp.float32).astype(jnp.bfloat16)
    one, zero = jnp.bfloat16(1.0), jnp.bfloat16(0.0)
    field_ids = lax.broadcasted_iota(jnp.int32, (fields, LANES), 0)
    share_rows = lax.broadcasted_iota(jnp.int32, (2 * intersections, LANES), 0)
    first_half = share_rows % intersections < 2

    turned = lanes_ref[group]
    for inner in range(GROUP):
        step = group * GROUP + inner
        here = window(step)
        share = atmos_weight_ref[:, here] * mask_ref[:, here].astype(jnp.float32)
        hot = []
        for k in range(intersections):
            tile = inner * intersections + k
            lane_of = jnp.broadcast_to(turned[:, tile : tile + 1], (LANES, LANES))
            hot.append(jnp.where(lane_of == column_ids, one, zero))
        hot = jnp.concatenate(
            [
                jnp.concatenate([hot[0], hot[1]], axis=1),
                jnp.concatenate([hot[2], hot[3]], axis=1),
            ],
            axis=0,
        )
        hot_ref[inner] = hot.astype(hot_type)
        parts = split_high(share)
        rows = jnp.concatenate(
            [jnp.where(first_half, parts, 0.0), jnp.where(first_half, 0.0, parts)], axis=1
        ).astype(jnp.bfloat16)
        spread = jnp.dot(rows, hot, preferred_element_type=jnp.float32)
        for k in range(intersections):
            side = slice((k % 2) * LANES, (k % 2 + 1) * LANES)
            low = intersections + k
            shared = spread[k : k + 1, side] + spread[low : low + 1, side]
            place = place_ref[k, step]
            sums[k][lax.div(place, fields)] += jnp.where(
                field_ids == lax.rem(place, fields), shared, 0.0
            )

    @pl.when(group == pl.num_programs(0) - 1)
    def _():
        total = sums[0][...]
        for ref in sums[1:]:
            total = total + ref[...]
        share_ref[...] = total


def middle_kernel(
    far_ref,
    target_ref,
    spot_ref,
    mix_ref,
    arrived_ref,
    column_ref,
    ocean_weight_ref,
    atmos_weight_ref,
    mask_ref,
    base_ref,
    state_ref,
    hot_ref,
    share_ref,
    forcing_ref,
    send_ref,
    held_ref,
    held_sem,
):
    intersections, cells = column_ref.shape
    windows = cells // LANES
    fields = base_ref.shape[0]

    def fetch(group):
        part = pl.ds(group * GROUP, GROUP)
        return pltpu.make_async_copy(hot_ref.at[part], held_ref.at[part], held_sem.at[group])

    groups = windows // GROUP
    for group in range(groups):
        fetch(group).start()
    send_ref[...] = jnp.zeros(send_ref.shape, jnp.float32)
    corner = mix_ref[0, 0]
    blank = jnp.zeros((2 * fields, LANES), jnp.float32)

    def body(group, carry):
        fetch(group).wait()
        for inner in range(GROUP):
            step = group * GROUP + inner
            here = window(step)
            lanes = column_ref[:, here] & (LANES - 1)
            ocean_weight = ocean_weight_ref[:, here]
            total = jnp.zeros((fields, LANES), jnp.float32)
            weight = jnp.zeros((1, LANES), jnp.float32)
            for k in range(intersections):
                picked = jnp.take_along_axis(
                    arrived_ref[spot_ref[k, step]],
                    jnp.broadcast_to(lanes[k : k + 1], (fields, LANES)),
                    axis=1,
                    mode="promise_in_bounds",
                )
                total = total + ocean_weight[k : k + 1] * picked
                weight = weight + ocean_weight[k : k + 1]
            forcing = total / weight
            forcing_ref[:, here] = forcing
            mask = mask_ref[:, here]
            surface = jnp.where(
                mask == 1, base_ref[:, here] + corner * forcing, state_ref[:, here]
            )
            share = atmos_weight_ref[:, here] * mask.astype(jnp.float32)
            parts = [split_high(share[k : k + 1] * surface) for k in range(intersections)]
            left = [parts[0], parts[1], blank, blank]
            right = [blank, blank, parts[2], parts[3]]
            parts = jnp.concatenate(
                [jnp.concatenate(left, axis=0), jnp.concatenate(right, axis=0)], axis=1
            ).astype(jnp.bfloat16)
            spread = jnp.dot(
                parts, held_ref[step].astype(jnp.bfloat16), preferred_element_type=jnp.float32
            )
            for k in range(intersections):
                side = slice((k % 2) * LANES, (k % 2 + 1) * LANES)
                at = 2 * fields * k
                send_ref[target_ref[k, step]] = (
                    spread[at : at + fields, side] + spread[at + fields : at + 2 * fields, side]
                )
        return carry

    lax.fori_loop(0, groups, body, 0)
    far = far_ref[0]
    near, rows = share_ref.shape[1:3]
    packed = send_ref.shape[0] // (2 * near)
    for half, shard in enumerate((1 - far, far)):
        for peer in range(near):
            first = (2 * peer + half + 1) * packed - rows
            send_ref[first : first + rows] = share_ref[shard, peer]


def ocean_kernel(mix_ref, forcing_ref, mask_ref, *refs):
    x_refs, (out_ref, high_ref, low_ref) = refs[:-3], refs[-3:]
    levels, fields, block = out_ref.shape
    rows = levels * fields

    @pl.when(pl.program_id(0) == 0)
    def _():
        level = lax.broadcasted_iota(jnp.int32, (rows, levels), 0) // fields
        pick = (level == lax.broadcasted_iota(jnp.int32, (rows, levels), 1)).astype(jnp.float32)
        tall = jnp.dot(pick, mix_ref[...], precision=lax.Precision.HIGHEST)
        wide = lax.dot_general(
            tall, pick, (((1,), (1,)), ((), ())), precision=lax.Precision.HIGHEST
        )
        down = lax.broadcasted_iota(jnp.int32, (rows, rows), 0) % fields
        across = lax.broadcasted_iota(jnp.int32, (rows, rows), 1) % fields
        wide = jnp.where(down == across, wide, 0.0)
        high = wide.astype(jnp.bfloat16)
        high_ref[...] = high
        low_ref[...] = (wide - high.astype(jnp.float32)).astype(jnp.bfloat16)

    flat = jnp.concatenate(
        [ref[...].reshape(rows // len(x_refs), block) for ref in x_refs], axis=0
    )
    push = jnp.concatenate(
        [forcing_ref[...], jnp.zeros((rows - fields, block), jnp.float32)], axis=0
    )
    loaded = flat + push
    high = loaded.astype(jnp.bfloat16)
    low = (loaded - high.astype(jnp.float32)).astype(jnp.bfloat16)
    mixed = (
        jnp.dot(high_ref[...], high, preferred_element_type=jnp.float32)
        + jnp.dot(high_ref[...], low, preferred_element_type=jnp.float32)
        + jnp.dot(low_ref[...], high, preferred_element_type=jnp.float32)
    )
    out_ref[...] = jnp.where(mask_ref[...] == 1, mixed, flat).reshape(levels, fields, block)


def diffuse_ocean(state, mixing, forcing, mask):
    levels, fields, cells = state.shape
    block = min(1024, cells)
    rows = levels * fields
    specs = level_specs(levels, fields, block)
    return pl.pallas_call(
        ocean_kernel,
        grid=(cells // block,),
        in_specs=[
            pl.BlockSpec(mixing.shape, lambda i: (0, 0)),
            pl.BlockSpec((fields, block), lambda i: (0, i)),
            pl.BlockSpec((1, block), lambda i: (0, i)),
        ]
        + specs,
        out_specs=pl.BlockSpec((levels, fields, block), lambda i: (0, 0, i)),
        out_shape=jax.ShapeDtypeStruct(state.shape, jnp.float32),
        scratch_shapes=[pltpu.VMEM((rows, rows), jnp.bfloat16)] * 2,
        compiler_params=stream_params,
        cost_estimate=pl.CostEstimate(
            flops=6 * rows * rows * cells,
            bytes_accessed=8 * rows * cells,
            transcendentals=0,
        ),
        name="diffuse_ocean",
    )(mixing, forcing, mask, *[state] * len(specs))


def collect_kernel(per_owner, home, far_ref, asked_ref, back_ref, out_ref, *sums):
    near, _, _, fields, _ = back_ref.shape
    columns = sums[0].shape[1]
    quarter = columns // fields
    chains = len(sums) // 2
    half = 1 if home else 0
    far = far_ref[0]
    first = (far if home else 1 - far) * per_owner
    for ref in sums:
        ref[...] = jnp.zeros(ref.shape, jnp.float32)

    def body(step, carry):
        for slot in range(per_owner):
            for chain in range(chains):
                peer = step * chains + chain
                at = window(asked_ref[peer, first + slot])
                tile, row = per_owner + slot // fields, slot % fields
                sums[chain][:, at] += back_ref[peer, half, slot]
                sums[chains + chain][:, at] += back_ref[peer, half, tile, row : row + 1]
        return carry

    lax.fori_loop(0, near // chains, body, 0)
    values, shares = sums[0][...], sums[chains][...]
    for chain in range(1, chains):
        values = values + sums[chain][...]
        shares = shares + sums[chains + chain][...]
    out_ref[:, :columns] = values
    for row in range(fields):
        out_ref[row : row + 1, columns:] = shares[:, row * quarter : (row + 1) * quarter]


def collect(asked, far, back, per_owner, columns, home):
    fields = back.shape[3]
    chains = 4
    return pl.pallas_call(
        functools.partial(collect_kernel, per_owner, home),
        in_specs=[smem, smem, vmem],
        out_specs=vmem,
        out_shape=jax.ShapeDtypeStruct((fields, columns + columns // fields), jnp.float32),
        scratch_shapes=[pltpu.VMEM((fields, columns), jnp.float32)] * chains
        + [pltpu.VMEM((1, columns), jnp.float32)] * chains,
        compiler_params=params,
        name="collect_home" if home else "collect_away",
    )(far, asked, back)


def final_kernel(keep_ref, other_ref, land_weight_ref, land_ref, out_ref):
    fields, columns = out_ref.shape
    quarter = columns // fields
    both = keep_ref[:, :columns] + other_ref[:, :columns]
    shares = keep_ref[:, columns:] + other_ref[:, columns:]
    land_weight = land_weight_ref[...]
    total = both + land_weight * land_ref[...]
    for row in range(fields):
        part = slice(row * quarter, (row + 1) * quarter)
        out_ref[:, part] = total[:, part] / (shares[row : row + 1] + land_weight[:, part])


def per_device(
    atmos_profiles,
    atmos_mixing,
    drag_factor,
    surface_before,
    downward_fluxes,
    land_weight,
    land_surface,
    ocean_state,
    ocean_mixing,
    sea_mask,
    exchange_slot,
    parent_column,
    ocean_weight,
    atmos_weight,
):
    near = lax.axis_size("near") * lax.axis_size("sub")
    devices = 2 * near
    fields, _, columns = atmos_profiles.shape
    intersections, cells = exchange_slot.shape
    capacity = 2 * intersections * cells // devices
    per_owner = capacity // LANES
    spots = 2 * per_owner
    mask = sea_mask.reshape(1, cells)
    state = ocean_state.transpose(1, 0, 2)
    far = lax.axis_index("far").astype(jnp.int32).reshape(1)

    def to_near(values):
        return lax.all_to_all(values, ("near", "sub"), split_axis=0, concat_axis=0, tiled=True)

    def to_far(values):
        return lax.ppermute(values, "far", ((0, 1), (1, 0)))

    place, spot, wanted, forcing_rows, tendency = start(
        near,
        per_owner,
        exchange_slot,
        parent_column,
        atmos_profiles,
        drag_factor,
        surface_before,
        downward_fluxes,
    )
    asked = to_near(wanted)
    other_rows = to_far(forcing_rows)
    base, first_level = top_level(state, ocean_mixing)
    asked, base, first_level = lax.optimization_barrier((asked, base, first_level))
    served = pl.pallas_call(
        functools.partial(serve_kernel, per_owner),
        in_specs=[smem, smem, hbm, hbm],
        out_specs=hbm,
        out_shape=jax.ShapeDtypeStruct((near, spots, fields, LANES), jnp.float32),
        scratch_shapes=[
            pltpu.VMEM((2, fields, columns), jnp.float32),
            pltpu.VMEM((near, spots, fields, LANES), jnp.float32),
            pltpu.SemaphoreType.DMA((2,)),
            pltpu.SemaphoreType.DMA((4,)),
        ],
        compiler_params=params,
        name="serve_windows",
    )(far, asked, forcing_rows, other_rows)
    served, columns_asked = lax.optimization_barrier((served, parent_column))
    arrived = to_near(served)
    rows = per_owner // fields
    windows = cells // LANES
    hot, shares = pl.pallas_call(
        hot_kernel,
        grid=(windows // GROUP,),
        in_specs=[smem] + [vmem] * 3,
        out_specs=[
            pl.BlockSpec((GROUP, 2 * LANES, 2 * LANES), lambda i: (i, 0, 0)),
            pl.BlockSpec((2 * near * rows, fields, LANES), lambda i: (0, 0, 0)),
        ],
        out_shape=[
            jax.ShapeDtypeStruct((windows, 2 * LANES, 2 * LANES), hot_type),
            jax.ShapeDtypeStruct((2 * near * rows, fields, LANES), jnp.float32),
        ],
        scratch_shapes=[pltpu.VMEM((windows // GROUP, LANES, LANES), jnp.bfloat16)]
        + [pltpu.VMEM((2 * near * rows, fields, LANES), jnp.float32)] * intersections,
        compiler_params=middle_params,
        name="one_hot_and_shares",
    )(place, columns_asked, atmos_weight, mask)
    arrived, hot, shares = lax.optimization_barrier((arrived, hot, shares))
    packed = per_owner + rows
    shard, within = place // (near * per_owner), place % (near * per_owner)
    half = jnp.where(shard == far, 1, 0)
    target = (within // per_owner * 2 + half) * packed + within % per_owner
    sent = (near * 2 * packed, fields, LANES)
    forcing, send = pl.pallas_call(
        middle_kernel,
        in_specs=[smem] * 4 + [vmem] * 7 + [hbm, vmem],
        out_specs=[vmem, vmem],
        out_shape=[
            jax.ShapeDtypeStruct((fields, cells), jnp.float32),
            jax.ShapeDtypeStruct(sent, jnp.float32),
        ],
        scratch_shapes=[
            pltpu.VMEM((windows, 2 * LANES, 2 * LANES), hot_type),
            pltpu.SemaphoreType.DMA((windows // GROUP,)),
        ],
        compiler_params=middle_params,
        name="forcing_and_windows",
    )(
        far,
        target,
        spot,
        ocean_mixing,
        arrived.reshape(near * spots, fields, LANES),
        parent_column,
        ocean_weight,
        atmos_weight,
        mask,
        base,
        first_level,
        hot,
        shares.reshape(2, near, rows, fields, LANES),
    )
    ocean_updated = diffuse_ocean(state, ocean_mixing, forcing, mask).transpose(1, 0, 2)
    tendency, forcing = lax.optimization_barrier((tendency, forcing))
    atmos_updated = diffuse_atmos(atmos_profiles, atmos_mixing, tendency)
    back = to_near(send.reshape(near, 2, packed, fields, LANES))
    back, ocean_updated, atmos_updated = lax.optimization_barrier(
        (back, ocean_updated, atmos_updated)
    )
    sums_away = collect(asked, far, back, per_owner, columns, False)
    sums_away, back = lax.optimization_barrier((sums_away, back))
    other_sums = to_far(sums_away)
    sums_home = collect(asked, far, back, per_owner, columns, True)
    other_sums, sums_home = lax.optimization_barrier((other_sums, sums_home))
    surface_state = pl.pallas_call(
        final_kernel,
        in_specs=[vmem] * 4,
        out_specs=vmem,
        out_shape=jax.ShapeDtypeStruct((fields, columns), jnp.float32),
        compiler_params=params,
        name="surface_state",
    )(sums_home, other_sums, land_weight.reshape(1, columns), land_surface)
    return (atmos_updated, ocean_updated, surface_state)


def solution(mesh):
    comp, sub = mesh.devices.shape
    halves = jax.sharding.Mesh(mesh.devices.reshape(2, comp // 2, sub), AXES)
    split = P(None, AXES)
    return jax.shard_map(
        per_device,
        mesh=halves,
        in_specs=(
            P(None, None, AXES),
            P(),
            P(AXES),
            split,
            split,
            P(AXES),
            split,
            P(None, None, AXES),
            P(),
            P(AXES),
            split,
            split,
            split,
            split,
        ),
        out_specs=(P(None, None, AXES), P(None, None, AXES), split),
        check_vma=False,
    )
```

```python
import functools

import jax
import jax.numpy as jnp
from jax import lax
from jax.experimental import pallas as pl
from jax.experimental.pallas import tpu as pltpu
from jax.sharding import PartitionSpec as P

couple_rate = 0.5
LANES = 128
params = pltpu.CompilerParams(vmem_limit_bytes=24 * 1024 * 1024)
stream_params = pltpu.CompilerParams(vmem_limit_bytes=52 * 1024 * 1024)
middle_params = pltpu.CompilerParams(vmem_limit_bytes=48 * 1024 * 1024)
first_params = pltpu.CompilerParams(vmem_limit_bytes=56 * 1024 * 1024)
vmem = pl.BlockSpec(memory_space=pltpu.VMEM)
smem = pl.BlockSpec(memory_space=pltpu.SMEM)
hbm = pl.BlockSpec(memory_space=pl.ANY)
AXES = ("far", "near", "sub")


def window(index):
    return pl.ds(pl.multiple_of(index * LANES, LANES), LANES)


def make_requests(per_owner, slot_ref, column_ref, place_ref, spot_ref, wanted_ref):
    intersections, cells = slot_ref.shape
    near, spots = wanted_ref.shape
    windows = cells // LANES
    lane = lax.broadcasted_iota(jnp.int32, (intersections, windows), 1)

    def heads(ref):
        found = jnp.zeros((intersections, windows), jnp.int32)
        for step in range(windows):
            head = ref[:, step * LANES : step * LANES + 1]
            found = jnp.where(lane == step, head, found)
        return found // LANES

    place = heads(slot_ref)
    column_window = heads(column_ref)
    owner = place // per_owner
    peer = owner % near
    spot = owner // near * per_owner + place % per_owner
    place_ref[...] = place
    spot_ref[...] = peer * spots + spot
    peer_ids = lax.broadcasted_iota(jnp.int32, (near, windows), 0)
    spot_ids = lax.broadcasted_iota(jnp.int32, (spots, windows), 0)
    wanted = jnp.zeros((near, spots), jnp.float32)
    for k in range(intersections):
        row = slice(k, k + 1)
        peer_hot = jnp.where(peer_ids == peer[row], 1.0, 0.0)
        spot_hot = jnp.where(
            spot_ids == spot[row], column_window[row].astype(jnp.float32), 0.0
        )
        wanted = wanted + lax.dot_general(
            peer_hot.astype(jnp.bfloat16),
            spot_hot.astype(jnp.bfloat16),
            (((1,), (1,)), ((), ())),
            preferred_element_type=jnp.float32,
        )
    wanted_ref[...] = wanted.astype(jnp.int32)


def start_kernel(
    last,
    per_owner,
    slot_ref,
    column_ref,
    x_ref,
    drag_ref,
    before_ref,
    down_ref,
    place_ref,
    spot_ref,
    wanted_ref,
    forcing_ref,
    tend_ref,
):
    @pl.when(pl.program_id(0) == 0)
    def _():
        make_requests(per_owner, slot_ref, column_ref, place_ref, spot_ref, wanted_ref)

    def row(ref, index):
        return ref[index : index + 1, :]

    bottom = [x_ref[member].astype(jnp.float32)[last : last + 1, :] for member in range(4)]
    east = bottom[2] - row(before_ref, 2)
    north = bottom[3] - row(before_ref, 3)
    transfer = drag_ref[...] * jnp.sqrt(1.0 + east * east + north * north)
    sensible = transfer * (row(before_ref, 0) - bottom[0])
    latent = transfer * (row(before_ref, 1) - bottom[1])
    east_stress = couple_rate * (transfer * east)
    north_stress = couple_rate * (transfer * north)
    forcing_ref[0:1, :] = couple_rate * (
        row(down_ref, 0) + row(down_ref, 1) - sensible - latent
    )
    forcing_ref[1:2, :] = couple_rate * (latent - row(down_ref, 2) - row(down_ref, 3))
    forcing_ref[2:3, :] = east_stress
    forcing_ref[3:4, :] = north_stress
    tend_ref[0:1, :] = couple_rate * sensible
    tend_ref[1:2, :] = couple_rate * latent
    tend_ref[2:3, :] = -east_stress
    tend_ref[3:4, :] = -north_stress


def start(near, per_owner, slots, parents, profiles, drag_factor, surface_before, downward):
    fields, levels, columns = profiles.shape
    intersections, cells = slots.shape
    block = min(4096, columns)
    tall = 16
    at = (levels - 1) // tall
    rows = pl.BlockSpec((fields, block), lambda i: (0, i))
    tiles = (intersections, cells // LANES)
    asked = (near, 2 * per_owner)

    def whole(shape):
        return pl.BlockSpec(shape, lambda i: (0, 0))

    return pl.pallas_call(
        functools.partial(start_kernel, levels - 1 - at * tall, per_owner),
        grid=(columns // block,),
        in_specs=[
            whole(slots.shape),
            whole(slots.shape),
            pl.BlockSpec((fields, tall, block), lambda i: (0, at, i)),
            pl.BlockSpec((1, block), lambda i: (0, i)),
            rows,
            rows,
        ],
        out_specs=[whole(tiles), whole(tiles), whole(asked), rows, rows],
        out_shape=[
            jax.ShapeDtypeStruct(tiles, jnp.int32),
            jax.ShapeDtypeStruct(tiles, jnp.int32),
            jax.ShapeDtypeStruct(asked, jnp.int32),
            jax.ShapeDtypeStruct((fields, columns), jnp.float32),
            jax.ShapeDtypeStruct((fields, columns), jnp.float32),
        ],
        compiler_params=first_params,
        name="requests_and_rates",
    )(slots, parents, profiles, drag_factor.reshape(1, columns), surface_before, downward)


def atmos_kernel(mix_ref, tend_ref, *refs):
    mix = mix_ref[...]
    lowest = mix[:, mix.shape[1] - 1 :].astype(jnp.float32)
    out_ref = refs[-1]
    for member, x_ref in enumerate(refs[:-1]):
        mixed = jnp.dot(mix, x_ref[0], preferred_element_type=jnp.float32)
        out_ref[member] = (mixed + lowest * tend_ref[member : member + 1, :]).astype(jnp.bfloat16)


def diffuse_atmos(profiles, mixing, tendency):
    fields, levels, columns = profiles.shape
    block = min(2048, columns)

    def field(member):
        return pl.BlockSpec((1, levels, block), lambda i: (member, 0, i))

    return pl.pallas_call(
        atmos_kernel,
        grid=(columns // block,),
        in_specs=[
            pl.BlockSpec((levels, levels), lambda i: (0, 0)),
            pl.BlockSpec((fields, block), lambda i: (0, i)),
        ]
        + [field(member) for member in range(fields)],
        out_specs=pl.BlockSpec((fields, levels, block), lambda i: (0, 0, i)),
        out_shape=jax.ShapeDtypeStruct(profiles.shape, jnp.bfloat16),
        compiler_params=stream_params,
        cost_estimate=pl.CostEstimate(
            flops=2 * fields * levels * levels * columns,
            bytes_accessed=4 * fields * levels * columns,
            transcendentals=0,
        ),
        name="diffuse_atmos",
    )(mixing, tendency, *[profiles] * fields)


def level_specs(levels, fields, block):
    count = 4 if levels % 4 == 0 else 1

    def part(number):
        return pl.BlockSpec((levels // count, fields, block), lambda i: (number, 0, i))

    return [part(number) for number in range(count)]


def top_kernel(mix_ref, *refs):
    state_refs, base_ref = refs[:-1], refs[-1]
    total = None
    level = 0
    for ref in state_refs:
        for inner in range(ref.shape[0]):
            term = mix_ref[0, level] * ref[inner]
            total = term if total is None else total + term
            level += 1
    base_ref[...] = total


def top_level(state, mixing):
    levels, fields, cells = state.shape
    block = min(2048, cells)
    specs = level_specs(levels, fields, block)
    return pl.pallas_call(
        top_kernel,
        grid=(cells // block,),
        in_specs=[smem] + specs,
        out_specs=pl.BlockSpec((fields, block), lambda i: (0, i)),
        out_shape=jax.ShapeDtypeStruct((fields, cells), jnp.float32),
        compiler_params=stream_params,
        cost_estimate=pl.CostEstimate(
            flops=2 * fields * levels * cells,
            bytes_accessed=4 * fields * levels * cells,
            transcendentals=0,
        ),
        name="top_level",
    )(mixing, *[state] * len(specs))


def serve_kernel(
    per_owner,
    far_ref,
    asked_ref,
    own_ref,
    other_ref,
    out_ref,
    blocks_ref,
    filled_ref,
    arrived_sem,
    sent_sem,
):
    copies = [
        pltpu.make_async_copy(ref, blocks_ref.at[index], arrived_sem.at[index])
        for index, ref in enumerate((own_ref, other_ref))
    ]
    for copy in copies:
        copy.start()
    for copy in copies:
        copy.wait()
    far = far_ref[0]

    def body(peer, carry):
        for shard in range(2):
            for slot in range(per_owner):
                spot = shard * per_owner + slot
                filled_ref[peer, spot] = blocks_ref[
                    shard ^ far, :, window(asked_ref[peer, spot])
                ]
        return carry

    sends = []
    parts = sent_sem.shape[0]
    peers = filled_ref.shape[0] // parts
    for part in range(parts):
        lax.fori_loop(part * peers, (part + 1) * peers, body, 0)
        at = pl.ds(part * peers, peers)
        send = pltpu.make_async_copy(filled_ref.at[at], out_ref.at[at], sent_sem.at[part])
        send.start()
        sends.append(send)
    for send in sends:
        send.wait()


def split_high(values):
    high = values.astype(jnp.bfloat16).astype(jnp.float32)
    return jnp.concatenate([high, values - high], axis=0)


GROUP = 8
hot_type = jnp.float8_e4m3fn


def hot_kernel(
    place_ref,
    column_ref,
    ocean_weight_ref,
    atmos_weight_ref,
    mask_ref,
    hot_ref,
    share_ref,
    scaled_ref,
    sea_share_ref,
    lanes_ref,
    *sums,
):
    intersections, cells = column_ref.shape
    windows = cells // LANES
    fields = share_ref.shape[1]
    group_tiles = GROUP * intersections
    steps = LANES // intersections
    group = pl.program_id(0)
    @pl.when(group == 0)
    def _():
        for ref in sums:
            ref[...] = jnp.zeros(ref.shape, jnp.float32)
        for first in range(0, windows, steps):
            tall = jnp.concatenate(
                [
                    column_ref[:, (first + step) * LANES : (first + step + 1) * LANES] & (LANES - 1)
                    for step in range(steps)
                ],
                axis=0,
            )
            turned = tall.astype(jnp.float32).T.astype(jnp.bfloat16)
            for part in range(steps // GROUP):
                lanes_ref[first // GROUP + part, :, :group_tiles] = turned[
                    :, part * group_tiles : (part + 1) * group_tiles
                ]

    column_ids = lax.broadcasted_iota(jnp.int32, (LANES, LANES), 1)
    column_ids = column_ids.astype(jnp.float32).astype(jnp.bfloat16)
    one, zero = jnp.bfloat16(1.0), jnp.bfloat16(0.0)
    field_ids = lax.broadcasted_iota(jnp.int32, (fields, LANES), 0)
    share_rows = lax.broadcasted_iota(jnp.int32, (2 * intersections, LANES), 0)
    first_half = share_rows % intersections < 2

    turned = lanes_ref[group]
    for inner in range(GROUP):
        step = group * GROUP + inner
        here = window(step)
        share = atmos_weight_ref[:, here] * mask_ref[:, here].astype(jnp.float32)
        block = slice(inner * LANES, (inner + 1) * LANES)
        sea_share_ref[:, block] = share
        ocean_weight = ocean_weight_ref[:, here]
        scaled_ref[:, block] = ocean_weight / jnp.sum(ocean_weight, axis=0, keepdims=True)
        hot = []
        for k in range(intersections):
            tile = inner * intersections + k
            lane_of = jnp.broadcast_to(turned[:, tile : tile + 1], (LANES, LANES))
            hot.append(jnp.where(lane_of == column_ids, one, zero))
        hot = jnp.concatenate(
            [
                jnp.concatenate([hot[0], hot[1]], axis=1),
                jnp.concatenate([hot[2], hot[3]], axis=1),
            ],
            axis=0,
        )
        hot_ref[inner] = hot.astype(hot_type)
        parts = split_high(share)
        rows = jnp.concatenate(
            [jnp.where(first_half, parts, 0.0), jnp.where(first_half, 0.0, parts)], axis=1
        ).astype(jnp.bfloat16)
        spread = jnp.dot(rows, hot, preferred_element_type=jnp.float32)
        for k in range(intersections):
            side = slice((k % 2) * LANES, (k % 2 + 1) * LANES)
            low = intersections + k
            shared = spread[k : k + 1, side] + spread[low : low + 1, side]
            place = place_ref[k, step]
            sums[k][lax.div(place, fields)] += jnp.where(
                field_ids == lax.rem(place, fields), shared, 0.0
            )

    @pl.when(group == pl.num_programs(0) - 1)
    def _():
        total = sums[0][...]
        for ref in sums[1:]:
            total = total + ref[...]
        share_ref[...] = total


def middle_kernel(
    far_ref,
    target_ref,
    spot_ref,
    mix_ref,
    arrived_ref,
    column_ref,
    scaled_ref,
    sea_share_ref,
    base_ref,
    hot_ref,
    share_ref,
    forcing_ref,
    send_ref,
    held_ref,
    held_sem,
):
    intersections, cells = column_ref.shape
    windows = cells // LANES
    fields = base_ref.shape[0]

    def fetch(group):
        part = pl.ds(group * GROUP, GROUP)
        return pltpu.make_async_copy(hot_ref.at[part], held_ref.at[part], held_sem.at[group])

    groups = windows // GROUP
    for group in range(groups):
        fetch(group).start()
    send_ref[...] = jnp.zeros(send_ref.shape, jnp.float32)
    corner = mix_ref[0, 0]
    blank = jnp.zeros((2 * fields, LANES), jnp.float32)

    def body(group, carry):
        fetch(group).wait()
        for inner in range(GROUP):
            step = group * GROUP + inner
            here = window(step)
            lanes = column_ref[:, here] & (LANES - 1)
            scaled = scaled_ref[:, here]
            forcing = jnp.zeros((fields, LANES), jnp.float32)
            for k in range(intersections):
                picked = jnp.take_along_axis(
                    arrived_ref[spot_ref[k, step]],
                    jnp.broadcast_to(lanes[k : k + 1], (fields, LANES)),
                    axis=1,
                    mode="promise_in_bounds",
                )
                forcing = forcing + scaled[k : k + 1] * picked
            forcing_ref[:, here] = forcing
            surface = base_ref[:, here] + corner * forcing
            share = sea_share_ref[:, here]
            parts = [split_high(share[k : k + 1] * surface) for k in range(intersections)]
            left = [parts[0], parts[1], blank, blank]
            right = [blank, blank, parts[2], parts[3]]
            parts = jnp.concatenate(
                [jnp.concatenate(left, axis=0), jnp.concatenate(right, axis=0)], axis=1
            ).astype(jnp.bfloat16)
            spread = jnp.dot(
                parts, held_ref[step].astype(jnp.bfloat16), preferred_element_type=jnp.float32
            )
            for k in range(intersections):
                side = slice((k % 2) * LANES, (k % 2 + 1) * LANES)
                at = 2 * fields * k
                send_ref[target_ref[k, step]] = (
                    spread[at : at + fields, side] + spread[at + fields : at + 2 * fields, side]
                )
        return carry

    lax.fori_loop(0, groups, body, 0)
    far = far_ref[0]
    near, rows = share_ref.shape[1:3]
    packed = send_ref.shape[0] // (2 * near)
    for half, shard in enumerate((1 - far, far)):
        for peer in range(near):
            first = (2 * peer + half + 1) * packed - rows
            send_ref[first : first + rows] = share_ref[shard, peer]


def ocean_kernel(mix_ref, forcing_ref, mask_ref, *refs):
    x_refs, (out_ref, high_ref, low_ref) = refs[:-3], refs[-3:]
    levels, fields, block = out_ref.shape
    rows = levels * fields

    @pl.when(pl.program_id(0) == 0)
    def _():
        level = lax.broadcasted_iota(jnp.int32, (rows, levels), 0) // fields
        pick = (level == lax.broadcasted_iota(jnp.int32, (rows, levels), 1)).astype(jnp.float32)
        tall = jnp.dot(pick, mix_ref[...], precision=lax.Precision.HIGHEST)
        wide = lax.dot_general(
            tall, pick, (((1,), (1,)), ((), ())), precision=lax.Precision.HIGHEST
        )
        down = lax.broadcasted_iota(jnp.int32, (rows, rows), 0) % fields
        across = lax.broadcasted_iota(jnp.int32, (rows, rows), 1) % fields
        wide = jnp.where(down == across, wide, 0.0)
        high = wide.astype(jnp.bfloat16)
        high_ref[...] = high
        low_ref[...] = (wide - high.astype(jnp.float32)).astype(jnp.bfloat16)

    flat = jnp.concatenate(
        [ref[...].reshape(rows // len(x_refs), block) for ref in x_refs], axis=0
    )
    push = jnp.concatenate(
        [forcing_ref[...], jnp.zeros((rows - fields, block), jnp.float32)], axis=0
    )
    loaded = flat + push
    high = loaded.astype(jnp.bfloat16)
    low = (loaded - high.astype(jnp.float32)).astype(jnp.bfloat16)
    mixed = (
        jnp.dot(high_ref[...], high, preferred_element_type=jnp.float32)
        + jnp.dot(high_ref[...], low, preferred_element_type=jnp.float32)
        + jnp.dot(low_ref[...], high, preferred_element_type=jnp.float32)
    )
    out_ref[...] = jnp.where(mask_ref[...] == 1, mixed, flat).reshape(levels, fields, block)


def diffuse_ocean(state, mixing, forcing, mask):
    levels, fields, cells = state.shape
    block = min(1024, cells)
    rows = levels * fields
    specs = level_specs(levels, fields, block)
    return pl.pallas_call(
        ocean_kernel,
        grid=(cells // block,),
        in_specs=[
            pl.BlockSpec(mixing.shape, lambda i: (0, 0)),
            pl.BlockSpec((fields, block), lambda i: (0, i)),
            pl.BlockSpec((1, block), lambda i: (0, i)),
        ]
        + specs,
        out_specs=pl.BlockSpec((levels, fields, block), lambda i: (0, 0, i)),
        out_shape=jax.ShapeDtypeStruct(state.shape, jnp.float32),
        scratch_shapes=[pltpu.VMEM((rows, rows), jnp.bfloat16)] * 2,
        compiler_params=stream_params,
        cost_estimate=pl.CostEstimate(
            flops=6 * rows * rows * cells,
            bytes_accessed=8 * rows * cells,
            transcendentals=0,
        ),
        name="diffuse_ocean",
    )(mixing, forcing, mask, *[state] * len(specs))


def collect_kernel(per_owner, home, far_ref, asked_ref, back_ref, out_ref, *sums):
    near, _, _, fields, _ = back_ref.shape
    columns = sums[0].shape[1]
    quarter = columns // fields
    chains = len(sums) // 2
    half = 1 if home else 0
    far = far_ref[0]
    first = (far if home else 1 - far) * per_owner
    for ref in sums:
        ref[...] = jnp.zeros(ref.shape, jnp.float32)

    def body(step, carry):
        for slot in range(per_owner):
            for chain in range(chains):
                peer = step * chains + chain
                at = window(asked_ref[peer, first + slot])
                tile, row = per_owner + slot // fields, slot % fields
                sums[chain][:, at] += back_ref[peer, half, slot]
                sums[chains + chain][:, at] += back_ref[peer, half, tile, row : row + 1]
        return carry

    lax.fori_loop(0, near // chains, body, 0)
    values, shares = sums[0][...], sums[chains][...]
    for chain in range(1, chains):
        values = values + sums[chain][...]
        shares = shares + sums[chains + chain][...]
    out_ref[:, :columns] = values
    for row in range(fields):
        out_ref[row : row + 1, columns:] = shares[:, row * quarter : (row + 1) * quarter]


def collect(asked, far, back, per_owner, columns, home):
    fields = back.shape[3]
    chains = 4
    return pl.pallas_call(
        functools.partial(collect_kernel, per_owner, home),
        in_specs=[smem, smem, vmem],
        out_specs=vmem,
        out_shape=jax.ShapeDtypeStruct((fields, columns + columns // fields), jnp.float32),
        scratch_shapes=[pltpu.VMEM((fields, columns), jnp.float32)] * chains
        + [pltpu.VMEM((1, columns), jnp.float32)] * chains,
        compiler_params=params,
        name="collect_home" if home else "collect_away",
    )(far, asked, back)


def final_kernel(keep_ref, other_ref, land_weight_ref, land_ref, out_ref):
    fields, columns = out_ref.shape
    quarter = columns // fields
    both = keep_ref[:, :columns] + other_ref[:, :columns]
    shares = keep_ref[:, columns:] + other_ref[:, columns:]
    land_weight = land_weight_ref[...]
    total = both + land_weight * land_ref[...]
    for row in range(fields):
        part = slice(row * quarter, (row + 1) * quarter)
        out_ref[:, part] = total[:, part] / (shares[row : row + 1] + land_weight[:, part])


def per_device(
    atmos_profiles,
    atmos_mixing,
    drag_factor,
    surface_before,
    downward_fluxes,
    land_weight,
    land_surface,
    ocean_state,
    ocean_mixing,
    sea_mask,
    exchange_slot,
    parent_column,
    ocean_weight,
    atmos_weight,
):
    near = lax.axis_size("near") * lax.axis_size("sub")
    devices = 2 * near
    fields, _, columns = atmos_profiles.shape
    intersections, cells = exchange_slot.shape
    capacity = 2 * intersections * cells // devices
    per_owner = capacity // LANES
    spots = 2 * per_owner
    mask = sea_mask.reshape(1, cells)
    state = ocean_state.transpose(1, 0, 2)
    far = lax.axis_index("far").astype(jnp.int32).reshape(1)

    def to_near(values):
        return lax.all_to_all(values, ("near", "sub"), split_axis=0, concat_axis=0, tiled=True)

    def to_far(values):
        return lax.ppermute(values, "far", ((0, 1), (1, 0)))

    place, spot, wanted, forcing_rows, tendency = start(
        near,
        per_owner,
        exchange_slot,
        parent_column,
        atmos_profiles,
        drag_factor,
        surface_before,
        downward_fluxes,
    )
    asked = to_near(wanted)
    other_rows = to_far(forcing_rows)
    base = top_level(state, ocean_mixing)
    asked, base = lax.optimization_barrier((asked, base))
    served = pl.pallas_call(
        functools.partial(serve_kernel, per_owner),
        in_specs=[smem, smem, hbm, hbm],
        out_specs=hbm,
        out_shape=jax.ShapeDtypeStruct((near, spots, fields, LANES), jnp.float32),
        scratch_shapes=[
            pltpu.VMEM((2, fields, columns), jnp.float32),
            pltpu.VMEM((near, spots, fields, LANES), jnp.float32),
            pltpu.SemaphoreType.DMA((2,)),
            pltpu.SemaphoreType.DMA((4,)),
        ],
        compiler_params=params,
        name="serve_windows",
    )(far, asked, forcing_rows, other_rows)
    served, columns_asked = lax.optimization_barrier((served, parent_column))
    arrived = to_near(served)
    rows = per_owner // fields
    windows = cells // LANES
    hot, shares, scaled, sea_share = pl.pallas_call(
        hot_kernel,
        grid=(windows // GROUP,),
        in_specs=[smem] + [vmem] * 4,
        out_specs=[
            pl.BlockSpec((GROUP, 2 * LANES, 2 * LANES), lambda i: (i, 0, 0)),
            pl.BlockSpec((2 * near * rows, fields, LANES), lambda i: (0, 0, 0)),
            pl.BlockSpec((intersections, GROUP * LANES), lambda i: (0, i)),
            pl.BlockSpec((intersections, GROUP * LANES), lambda i: (0, i)),
        ],
        out_shape=[
            jax.ShapeDtypeStruct((windows, 2 * LANES, 2 * LANES), hot_type),
            jax.ShapeDtypeStruct((2 * near * rows, fields, LANES), jnp.float32),
            jax.ShapeDtypeStruct((intersections, cells), jnp.float32),
            jax.ShapeDtypeStruct((intersections, cells), jnp.float32),
        ],
        scratch_shapes=[pltpu.VMEM((windows // GROUP, LANES, LANES), jnp.bfloat16)]
        + [pltpu.VMEM((2 * near * rows, fields, LANES), jnp.float32)] * intersections,
        compiler_params=middle_params,
        name="one_hot_and_shares",
    )(place, columns_asked, ocean_weight, atmos_weight, mask)
    arrived, hot, shares, scaled, sea_share = lax.optimization_barrier(
        (arrived, hot, shares, scaled, sea_share)
    )
    packed = per_owner + rows
    shard, within = place // (near * per_owner), place % (near * per_owner)
    half = jnp.where(shard == far, 1, 0)
    target = (within // per_owner * 2 + half) * packed + within % per_owner
    sent = (near * 2 * packed, fields, LANES)
    forcing, send = pl.pallas_call(
        middle_kernel,
        in_specs=[smem] * 4 + [vmem] * 5 + [hbm, vmem],
        out_specs=[vmem, vmem],
        out_shape=[
            jax.ShapeDtypeStruct((fields, cells), jnp.float32),
            jax.ShapeDtypeStruct(sent, jnp.float32),
        ],
        scratch_shapes=[
            pltpu.VMEM((windows, 2 * LANES, 2 * LANES), hot_type),
            pltpu.SemaphoreType.DMA((windows // GROUP,)),
        ],
        compiler_params=middle_params,
        name="forcing_and_windows",
    )(
        far,
        target,
        spot,
        ocean_mixing,
        arrived.reshape(near * spots, fields, LANES),
        parent_column,
        scaled,
        sea_share,
        base,
        hot,
        shares.reshape(2, near, rows, fields, LANES),
    )
    ocean_updated = diffuse_ocean(state, ocean_mixing, forcing, mask).transpose(1, 0, 2)
    tendency, forcing = lax.optimization_barrier((tendency, forcing))
    atmos_updated = diffuse_atmos(atmos_profiles, atmos_mixing, tendency)
    back = to_near(send.reshape(near, 2, packed, fields, LANES))
    back, ocean_updated, atmos_updated = lax.optimization_barrier(
        (back, ocean_updated, atmos_updated)
    )
    sums_away = collect(asked, far, back, per_owner, columns, False)
    sums_away, back = lax.optimization_barrier((sums_away, back))
    other_sums = to_far(sums_away)
    sums_home = collect(asked, far, back, per_owner, columns, True)
    other_sums, sums_home = lax.optimization_barrier((other_sums, sums_home))
    surface_state = pl.pallas_call(
        final_kernel,
        in_specs=[vmem] * 4,
        out_specs=vmem,
        out_shape=jax.ShapeDtypeStruct((fields, columns), jnp.float32),
        compiler_params=params,
        name="surface_state",
    )(sums_home, other_sums, land_weight.reshape(1, columns), land_surface)
    return (atmos_updated, ocean_updated, surface_state)


def solution(mesh):
    comp, sub = mesh.devices.shape
    halves = jax.sharding.Mesh(mesh.devices.reshape(2, comp // 2, sub), AXES)
    split = P(None, AXES)
    return jax.shard_map(
        per_device,
        mesh=halves,
        in_specs=(
            P(None, None, AXES),
            P(),
            P(AXES),
            split,
            split,
            P(AXES),
            split,
            P(None, None, AXES),
            P(),
            P(AXES),
            split,
            split,
            split,
            split,
        ),
        out_specs=(P(None, None, AXES), P(None, None, AXES), split),
        check_vma=False,
    )
```

```python
import functools

import jax
import jax.numpy as jnp
from jax import lax
from jax.experimental import pallas as pl
from jax.experimental.pallas import tpu as pltpu
from jax.sharding import PartitionSpec as P

couple_rate = 0.5
LANES = 128
params = pltpu.CompilerParams(vmem_limit_bytes=24 * 1024 * 1024)
stream_params = pltpu.CompilerParams(vmem_limit_bytes=52 * 1024 * 1024)
middle_params = pltpu.CompilerParams(vmem_limit_bytes=48 * 1024 * 1024)
first_params = pltpu.CompilerParams(vmem_limit_bytes=56 * 1024 * 1024)
vmem = pl.BlockSpec(memory_space=pltpu.VMEM)
smem = pl.BlockSpec(memory_space=pltpu.SMEM)
hbm = pl.BlockSpec(memory_space=pl.ANY)
AXES = ("far", "near", "sub")


def window(index):
    return pl.ds(pl.multiple_of(index * LANES, LANES), LANES)


def make_requests(per_owner, slot_ref, column_ref, place_ref, spot_ref, wanted_ref):
    intersections, cells = slot_ref.shape
    near, spots = wanted_ref.shape
    windows = cells // LANES
    lane = lax.broadcasted_iota(jnp.int32, (intersections, windows), 1)

    def heads(ref):
        found = jnp.zeros((intersections, windows), jnp.int32)
        for step in range(windows):
            head = ref[:, step * LANES : step * LANES + 1]
            found = jnp.where(lane == step, head, found)
        return found // LANES

    place = heads(slot_ref)
    column_window = heads(column_ref)
    owner = place // per_owner
    peer = owner % near
    spot = owner // near * per_owner + place % per_owner
    place_ref[...] = place
    spot_ref[...] = peer * spots + spot
    peer_ids = lax.broadcasted_iota(jnp.int32, (near, windows), 0)
    spot_ids = lax.broadcasted_iota(jnp.int32, (spots, windows), 0)
    wanted = jnp.zeros((near, spots), jnp.float32)
    for k in range(intersections):
        row = slice(k, k + 1)
        peer_hot = jnp.where(peer_ids == peer[row], 1.0, 0.0)
        spot_hot = jnp.where(
            spot_ids == spot[row], column_window[row].astype(jnp.float32), 0.0
        )
        wanted = wanted + lax.dot_general(
            peer_hot.astype(jnp.bfloat16),
            spot_hot.astype(jnp.bfloat16),
            (((1,), (1,)), ((), ())),
            preferred_element_type=jnp.float32,
        )
    wanted_ref[...] = wanted.astype(jnp.int32)


def start_kernel(
    last,
    per_owner,
    slot_ref,
    column_ref,
    x_ref,
    drag_ref,
    before_ref,
    down_ref,
    place_ref,
    spot_ref,
    wanted_ref,
    forcing_ref,
    tend_ref,
):
    @pl.when(pl.program_id(0) == 0)
    def _():
        make_requests(per_owner, slot_ref, column_ref, place_ref, spot_ref, wanted_ref)

    def row(ref, index):
        return ref[index : index + 1, :]

    bottom = [x_ref[member].astype(jnp.float32)[last : last + 1, :] for member in range(4)]
    east = bottom[2] - row(before_ref, 2)
    north = bottom[3] - row(before_ref, 3)
    transfer = drag_ref[...] * jnp.sqrt(1.0 + east * east + north * north)
    sensible = transfer * (row(before_ref, 0) - bottom[0])
    latent = transfer * (row(before_ref, 1) - bottom[1])
    east_stress = couple_rate * (transfer * east)
    north_stress = couple_rate * (transfer * north)
    forcing_ref[0:1, :] = couple_rate * (
        row(down_ref, 0) + row(down_ref, 1) - sensible - latent
    )
    forcing_ref[1:2, :] = couple_rate * (latent - row(down_ref, 2) - row(down_ref, 3))
    forcing_ref[2:3, :] = east_stress
    forcing_ref[3:4, :] = north_stress
    tend_ref[0:1, :] = couple_rate * sensible
    tend_ref[1:2, :] = couple_rate * latent
    tend_ref[2:3, :] = -east_stress
    tend_ref[3:4, :] = -north_stress


def start(near, per_owner, slots, parents, profiles, drag_factor, surface_before, downward):
    fields, levels, columns = profiles.shape
    intersections, cells = slots.shape
    block = min(4096, columns)
    tall = 16
    at = (levels - 1) // tall
    rows = pl.BlockSpec((fields, block), lambda i: (0, i))
    tiles = (intersections, cells // LANES)
    asked = (near, 2 * per_owner)

    def whole(shape):
        return pl.BlockSpec(shape, lambda i: (0, 0))

    return pl.pallas_call(
        functools.partial(start_kernel, levels - 1 - at * tall, per_owner),
        grid=(columns // block,),
        in_specs=[
            whole(slots.shape),
            whole(slots.shape),
            pl.BlockSpec((fields, tall, block), lambda i: (0, at, i)),
            pl.BlockSpec((1, block), lambda i: (0, i)),
            rows,
            rows,
        ],
        out_specs=[whole(tiles), whole(tiles), whole(asked), rows, rows],
        out_shape=[
            jax.ShapeDtypeStruct(tiles, jnp.int32),
            jax.ShapeDtypeStruct(tiles, jnp.int32),
            jax.ShapeDtypeStruct(asked, jnp.int32),
            jax.ShapeDtypeStruct((fields, columns), jnp.float32),
            jax.ShapeDtypeStruct((fields, columns), jnp.float32),
        ],
        compiler_params=first_params,
        name="requests_and_rates",
    )(slots, parents, profiles, drag_factor.reshape(1, columns), surface_before, downward)


def atmos_kernel(mix_ref, tend_ref, *refs):
    mix = mix_ref[...]
    lowest = mix[:, mix.shape[1] - 1 :].astype(jnp.float32)
    out_ref = refs[-1]
    for member, x_ref in enumerate(refs[:-1]):
        mixed = jnp.dot(mix, x_ref[0], preferred_element_type=jnp.float32)
        out_ref[member] = (mixed + lowest * tend_ref[member : member + 1, :]).astype(jnp.bfloat16)


def diffuse_atmos(profiles, mixing, tendency):
    fields, levels, columns = profiles.shape
    block = min(2048, columns)

    def field(member):
        return pl.BlockSpec((1, levels, block), lambda i: (member, 0, i))

    return pl.pallas_call(
        atmos_kernel,
        grid=(columns // block,),
        in_specs=[
            pl.BlockSpec((levels, levels), lambda i: (0, 0)),
            pl.BlockSpec((fields, block), lambda i: (0, i)),
        ]
        + [field(member) for member in range(fields)],
        out_specs=pl.BlockSpec((fields, levels, block), lambda i: (0, 0, i)),
        out_shape=jax.ShapeDtypeStruct(profiles.shape, jnp.bfloat16),
        compiler_params=stream_params,
        cost_estimate=pl.CostEstimate(
            flops=2 * fields * levels * levels * columns,
            bytes_accessed=4 * fields * levels * columns,
            transcendentals=0,
        ),
        name="diffuse_atmos",
    )(mixing, tendency, *[profiles] * fields)


def level_specs(levels, fields, block):
    count = 4 if levels % 4 == 0 else 1

    def part(number):
        return pl.BlockSpec((levels // count, fields, block), lambda i: (number, 0, i))

    return [part(number) for number in range(count)]


def top_kernel(mix_ref, *refs):
    state_refs, base_ref = refs[:-1], refs[-1]
    total = None
    level = 0
    for ref in state_refs:
        for inner in range(ref.shape[0]):
            term = mix_ref[0, level] * ref[inner]
            total = term if total is None else total + term
            level += 1
    base_ref[...] = total


def top_level(state, mixing):
    levels, fields, cells = state.shape
    block = min(2048, cells)
    specs = level_specs(levels, fields, block)
    return pl.pallas_call(
        top_kernel,
        grid=(cells // block,),
        in_specs=[smem] + specs,
        out_specs=pl.BlockSpec((fields, block), lambda i: (0, i)),
        out_shape=jax.ShapeDtypeStruct((fields, cells), jnp.float32),
        compiler_params=stream_params,
        cost_estimate=pl.CostEstimate(
            flops=2 * fields * levels * cells,
            bytes_accessed=4 * fields * levels * cells,
            transcendentals=0,
        ),
        name="top_level",
    )(mixing, *[state] * len(specs))


def serve_kernel(
    per_owner,
    far_ref,
    asked_ref,
    own_ref,
    other_ref,
    out_ref,
    blocks_ref,
    filled_ref,
    arrived_sem,
    sent_sem,
):
    copies = [
        pltpu.make_async_copy(ref, blocks_ref.at[index], arrived_sem.at[index])
        for index, ref in enumerate((own_ref, other_ref))
    ]
    for copy in copies:
        copy.start()
    for copy in copies:
        copy.wait()
    far = far_ref[0]

    def body(peer, carry):
        for shard in range(2):
            for slot in range(per_owner):
                spot = shard * per_owner + slot
                filled_ref[peer, spot] = blocks_ref[
                    shard ^ far, :, window(asked_ref[peer, spot])
                ]
        return carry

    sends = []
    parts = sent_sem.shape[0]
    peers = filled_ref.shape[0] // parts
    for part in range(parts):
        lax.fori_loop(part * peers, (part + 1) * peers, body, 0)
        at = pl.ds(part * peers, peers)
        send = pltpu.make_async_copy(filled_ref.at[at], out_ref.at[at], sent_sem.at[part])
        send.start()
        sends.append(send)
    for send in sends:
        send.wait()


def split_high(values):
    high = values.astype(jnp.bfloat16).astype(jnp.float32)
    return jnp.concatenate([high, values - high], axis=0)


GROUP = 16
hot_type = jnp.float8_e4m3fn


def hot_kernel(
    place_ref,
    column_ref,
    ocean_weight_ref,
    atmos_weight_ref,
    mask_ref,
    hot_ref,
    share_ref,
    scaled_ref,
    sea_share_ref,
    lanes_ref,
    *sums,
):
    intersections, cells = column_ref.shape
    windows = cells // LANES
    fields = share_ref.shape[1]
    group_tiles = GROUP * intersections
    steps = LANES // intersections
    group = pl.program_id(0)
    @pl.when(group == 0)
    def _():
        for ref in sums:
            ref[...] = jnp.zeros(ref.shape, jnp.float32)
        for first in range(0, windows, steps):
            tall = jnp.concatenate(
                [
                    column_ref[:, (first + step) * LANES : (first + step + 1) * LANES] & (LANES - 1)
                    for step in range(steps)
                ],
                axis=0,
            )
            turned = tall.astype(jnp.float32).T.astype(jnp.bfloat16)
            for part in range(steps // GROUP):
                lanes_ref[first // GROUP + part, :, :group_tiles] = turned[
                    :, part * group_tiles : (part + 1) * group_tiles
                ]

    column_ids = lax.broadcasted_iota(jnp.int32, (LANES, LANES), 1)
    column_ids = column_ids.astype(jnp.float32).astype(jnp.bfloat16)
    one, zero = jnp.bfloat16(1.0), jnp.bfloat16(0.0)
    field_ids = lax.broadcasted_iota(jnp.int32, (fields, LANES), 0)
    share_rows = lax.broadcasted_iota(jnp.int32, (2 * intersections, LANES), 0)
    first_half = share_rows % intersections < 2

    turned = lanes_ref[group]
    for inner in range(GROUP):
        step = group * GROUP + inner
        here = window(step)
        share = atmos_weight_ref[:, here] * mask_ref[:, here].astype(jnp.float32)
        block = slice(inner * LANES, (inner + 1) * LANES)
        sea_share_ref[:, block] = share
        ocean_weight = ocean_weight_ref[:, here]
        scaled_ref[:, block] = ocean_weight / jnp.sum(ocean_weight, axis=0, keepdims=True)
        hot = []
        for k in range(intersections):
            tile = inner * intersections + k
            lane_of = jnp.broadcast_to(turned[:, tile : tile + 1], (LANES, LANES))
            hot.append(jnp.where(lane_of == column_ids, one, zero))
        hot = jnp.concatenate(
            [
                jnp.concatenate([hot[0], hot[1]], axis=1),
                jnp.concatenate([hot[2], hot[3]], axis=1),
            ],
            axis=0,
        )
        hot_ref[inner] = hot.astype(hot_type)
        parts = split_high(share)
        rows = jnp.concatenate(
            [jnp.where(first_half, parts, 0.0), jnp.where(first_half, 0.0, parts)], axis=1
        ).astype(jnp.bfloat16)
        spread = jnp.dot(rows, hot, preferred_element_type=jnp.float32)
        for k in range(intersections):
            side = slice((k % 2) * LANES, (k % 2 + 1) * LANES)
            low = intersections + k
            shared = spread[k : k + 1, side] + spread[low : low + 1, side]
            place = place_ref[k, step]
            sums[k][lax.div(place, fields)] += jnp.where(
                field_ids == lax.rem(place, fields), shared, 0.0
            )

    @pl.when(group == pl.num_programs(0) - 1)
    def _():
        total = sums[0][...]
        for ref in sums[1:]:
            total = total + ref[...]
        share_ref[...] = total


def middle_kernel(
    far_ref,
    target_ref,
    spot_ref,
    mix_ref,
    arrived_ref,
    column_ref,
    scaled_ref,
    sea_share_ref,
    base_ref,
    hot_ref,
    share_ref,
    forcing_ref,
    send_ref,
    held_ref,
    held_sem,
):
    intersections, cells = column_ref.shape
    windows = cells // LANES
    fields = base_ref.shape[0]

    def fetch(group):
        part = pl.ds(group * GROUP, GROUP)
        return pltpu.make_async_copy(hot_ref.at[part], held_ref.at[part], held_sem.at[group])

    groups = windows // GROUP
    for group in range(groups):
        fetch(group).start()
    send_ref[...] = jnp.zeros(send_ref.shape, jnp.float32)
    corner = mix_ref[0, 0]
    blank = jnp.zeros((2 * fields, LANES), jnp.float32)

    def body(group, carry):
        fetch(group).wait()
        for inner in range(GROUP):
            step = group * GROUP + inner
            here = window(step)
            lanes = column_ref[:, here] & (LANES - 1)
            scaled = scaled_ref[:, here]
            forcing = jnp.zeros((fields, LANES), jnp.float32)
            for k in range(intersections):
                picked = jnp.take_along_axis(
                    arrived_ref[spot_ref[k, step]],
                    jnp.broadcast_to(lanes[k : k + 1], (fields, LANES)),
                    axis=1,
                    mode="promise_in_bounds",
                )
                forcing = forcing + scaled[k : k + 1] * picked
            forcing_ref[:, here] = forcing
            surface = base_ref[:, here] + corner * forcing
            share = sea_share_ref[:, here]
            parts = [split_high(share[k : k + 1] * surface) for k in range(intersections)]
            left = [parts[0], parts[1], blank, blank]
            right = [blank, blank, parts[2], parts[3]]
            parts = jnp.concatenate(
                [jnp.concatenate(left, axis=0), jnp.concatenate(right, axis=0)], axis=1
            ).astype(jnp.bfloat16)
            spread = jnp.dot(
                parts, held_ref[step].astype(jnp.bfloat16), preferred_element_type=jnp.float32
            )
            for k in range(intersections):
                side = slice((k % 2) * LANES, (k % 2 + 1) * LANES)
                at = 2 * fields * k
                send_ref[target_ref[k, step]] = (
                    spread[at : at + fields, side] + spread[at + fields : at + 2 * fields, side]
                )
        return carry

    lax.fori_loop(0, groups, body, 0)
    far = far_ref[0]
    near, rows = share_ref.shape[1:3]
    packed = send_ref.shape[0] // (2 * near)
    for half, shard in enumerate((1 - far, far)):
        for peer in range(near):
            first = (2 * peer + half + 1) * packed - rows
            send_ref[first : first + rows] = share_ref[shard, peer]


def ocean_kernel(mix_ref, forcing_ref, mask_ref, *refs):
    x_refs, (out_ref, high_ref, low_ref) = refs[:-3], refs[-3:]
    levels, fields, block = out_ref.shape
    rows = levels * fields

    @pl.when(pl.program_id(0) == 0)
    def _():
        level = lax.broadcasted_iota(jnp.int32, (rows, levels), 0) // fields
        pick = (level == lax.broadcasted_iota(jnp.int32, (rows, levels), 1)).astype(jnp.float32)
        tall = jnp.dot(pick, mix_ref[...], precision=lax.Precision.HIGHEST)
        wide = lax.dot_general(
            tall, pick, (((1,), (1,)), ((), ())), precision=lax.Precision.HIGHEST
        )
        down = lax.broadcasted_iota(jnp.int32, (rows, rows), 0) % fields
        across = lax.broadcasted_iota(jnp.int32, (rows, rows), 1) % fields
        wide = jnp.where(down == across, wide, 0.0)
        high = wide.astype(jnp.bfloat16)
        high_ref[...] = high
        low_ref[...] = (wide - high.astype(jnp.float32)).astype(jnp.bfloat16)

    flat = jnp.concatenate(
        [ref[...].reshape(rows // len(x_refs), block) for ref in x_refs], axis=0
    )
    push = jnp.concatenate(
        [forcing_ref[...], jnp.zeros((rows - fields, block), jnp.float32)], axis=0
    )
    loaded = flat + push
    high = loaded.astype(jnp.bfloat16)
    low = (loaded - high.astype(jnp.float32)).astype(jnp.bfloat16)
    mixed = (
        jnp.dot(high_ref[...], high, preferred_element_type=jnp.float32)
        + jnp.dot(high_ref[...], low, preferred_element_type=jnp.float32)
        + jnp.dot(low_ref[...], high, preferred_element_type=jnp.float32)
    )
    out_ref[...] = jnp.where(mask_ref[...] == 1, mixed, flat).reshape(levels, fields, block)


def diffuse_ocean(state, mixing, forcing, mask):
    levels, fields, cells = state.shape
    block = min(1024, cells)
    rows = levels * fields
    specs = level_specs(levels, fields, block)
    return pl.pallas_call(
        ocean_kernel,
        grid=(cells // block,),
        in_specs=[
            pl.BlockSpec(mixing.shape, lambda i: (0, 0)),
            pl.BlockSpec((fields, block), lambda i: (0, i)),
            pl.BlockSpec((1, block), lambda i: (0, i)),
        ]
        + specs,
        out_specs=pl.BlockSpec((levels, fields, block), lambda i: (0, 0, i)),
        out_shape=jax.ShapeDtypeStruct(state.shape, jnp.float32),
        scratch_shapes=[pltpu.VMEM((rows, rows), jnp.bfloat16)] * 2,
        compiler_params=stream_params,
        cost_estimate=pl.CostEstimate(
            flops=6 * rows * rows * cells,
            bytes_accessed=8 * rows * cells,
            transcendentals=0,
        ),
        name="diffuse_ocean",
    )(mixing, forcing, mask, *[state] * len(specs))


def collect_kernel(per_owner, home, far_ref, asked_ref, back_ref, out_ref, *sums):
    near, _, _, fields, _ = back_ref.shape
    columns = sums[0].shape[1]
    quarter = columns // fields
    chains = len(sums) // 2
    half = 1 if home else 0
    far = far_ref[0]
    first = (far if home else 1 - far) * per_owner
    for ref in sums:
        ref[...] = jnp.zeros(ref.shape, jnp.float32)

    def body(step, carry):
        for slot in range(per_owner):
            for chain in range(chains):
                peer = step * chains + chain
                at = window(asked_ref[peer, first + slot])
                tile, row = per_owner + slot // fields, slot % fields
                sums[chain][:, at] += back_ref[peer, half, slot]
                sums[chains + chain][:, at] += back_ref[peer, half, tile, row : row + 1]
        return carry

    lax.fori_loop(0, near // chains, body, 0)
    values, shares = sums[0][...], sums[chains][...]
    for chain in range(1, chains):
        values = values + sums[chain][...]
        shares = shares + sums[chains + chain][...]
    out_ref[:, :columns] = values
    for row in range(fields):
        out_ref[row : row + 1, columns:] = shares[:, row * quarter : (row + 1) * quarter]


def collect(asked, far, back, per_owner, columns, home):
    fields = back.shape[3]
    chains = 4
    return pl.pallas_call(
        functools.partial(collect_kernel, per_owner, home),
        in_specs=[smem, smem, vmem],
        out_specs=vmem,
        out_shape=jax.ShapeDtypeStruct((fields, columns + columns // fields), jnp.float32),
        scratch_shapes=[pltpu.VMEM((fields, columns), jnp.float32)] * chains
        + [pltpu.VMEM((1, columns), jnp.float32)] * chains,
        compiler_params=params,
        name="collect_home" if home else "collect_away",
    )(far, asked, back)


def final_kernel(keep_ref, other_ref, land_weight_ref, land_ref, out_ref):
    fields, columns = out_ref.shape
    quarter = columns // fields
    both = keep_ref[:, :columns] + other_ref[:, :columns]
    shares = keep_ref[:, columns:] + other_ref[:, columns:]
    land_weight = land_weight_ref[...]
    total = both + land_weight * land_ref[...]
    for row in range(fields):
        part = slice(row * quarter, (row + 1) * quarter)
        out_ref[:, part] = total[:, part] / (shares[row : row + 1] + land_weight[:, part])


def per_device(
    atmos_profiles,
    atmos_mixing,
    drag_factor,
    surface_before,
    downward_fluxes,
    land_weight,
    land_surface,
    ocean_state,
    ocean_mixing,
    sea_mask,
    exchange_slot,
    parent_column,
    ocean_weight,
    atmos_weight,
):
    near = lax.axis_size("near") * lax.axis_size("sub")
    devices = 2 * near
    fields, _, columns = atmos_profiles.shape
    intersections, cells = exchange_slot.shape
    capacity = 2 * intersections * cells // devices
    per_owner = capacity // LANES
    spots = 2 * per_owner
    mask = sea_mask.reshape(1, cells)
    state = ocean_state.transpose(1, 0, 2)
    far = lax.axis_index("far").astype(jnp.int32).reshape(1)

    def to_near(values):
        return lax.all_to_all(values, ("near", "sub"), split_axis=0, concat_axis=0, tiled=True)

    def to_far(values):
        return lax.ppermute(values, "far", ((0, 1), (1, 0)))

    place, spot, wanted, forcing_rows, tendency = start(
        near,
        per_owner,
        exchange_slot,
        parent_column,
        atmos_profiles,
        drag_factor,
        surface_before,
        downward_fluxes,
    )
    asked = to_near(wanted)
    other_rows = to_far(forcing_rows)
    base = top_level(state, ocean_mixing)
    asked, base = lax.optimization_barrier((asked, base))
    served = pl.pallas_call(
        functools.partial(serve_kernel, per_owner),
        in_specs=[smem, smem, hbm, hbm],
        out_specs=hbm,
        out_shape=jax.ShapeDtypeStruct((near, spots, fields, LANES), jnp.float32),
        scratch_shapes=[
            pltpu.VMEM((2, fields, columns), jnp.float32),
            pltpu.VMEM((near, spots, fields, LANES), jnp.float32),
            pltpu.SemaphoreType.DMA((2,)),
            pltpu.SemaphoreType.DMA((4,)),
        ],
        compiler_params=params,
        name="serve_windows",
    )(far, asked, forcing_rows, other_rows)
    served, columns_asked = lax.optimization_barrier((served, parent_column))
    arrived = to_near(served)
    rows = per_owner // fields
    windows = cells // LANES
    hot, shares, scaled, sea_share = pl.pallas_call(
        hot_kernel,
        grid=(windows // GROUP,),
        in_specs=[smem] + [vmem] * 4,
        out_specs=[
            pl.BlockSpec((GROUP, 2 * LANES, 2 * LANES), lambda i: (i, 0, 0)),
            pl.BlockSpec((2 * near * rows, fields, LANES), lambda i: (0, 0, 0)),
            pl.BlockSpec((intersections, GROUP * LANES), lambda i: (0, i)),
            pl.BlockSpec((intersections, GROUP * LANES), lambda i: (0, i)),
        ],
        out_shape=[
            jax.ShapeDtypeStruct((windows, 2 * LANES, 2 * LANES), hot_type),
            jax.ShapeDtypeStruct((2 * near * rows, fields, LANES), jnp.float32),
            jax.ShapeDtypeStruct((intersections, cells), jnp.float32),
            jax.ShapeDtypeStruct((intersections, cells), jnp.float32),
        ],
        scratch_shapes=[pltpu.VMEM((windows // GROUP, LANES, LANES), jnp.bfloat16)]
        + [pltpu.VMEM((2 * near * rows, fields, LANES), jnp.float32)] * intersections,
        compiler_params=middle_params,
        name="one_hot_and_shares",
    )(place, columns_asked, ocean_weight, atmos_weight, mask)
    arrived, hot, shares, scaled, sea_share = lax.optimization_barrier(
        (arrived, hot, shares, scaled, sea_share)
    )
    packed = per_owner + rows
    shard, within = place // (near * per_owner), place % (near * per_owner)
    half = jnp.where(shard == far, 1, 0)
    target = (within // per_owner * 2 + half) * packed + within % per_owner
    sent = (near * 2 * packed, fields, LANES)
    forcing, send = pl.pallas_call(
        middle_kernel,
        in_specs=[smem] * 4 + [vmem] * 5 + [hbm, vmem],
        out_specs=[vmem, vmem],
        out_shape=[
            jax.ShapeDtypeStruct((fields, cells), jnp.float32),
            jax.ShapeDtypeStruct(sent, jnp.float32),
        ],
        scratch_shapes=[
            pltpu.VMEM((windows, 2 * LANES, 2 * LANES), hot_type),
            pltpu.SemaphoreType.DMA((windows // GROUP,)),
        ],
        compiler_params=middle_params,
        name="forcing_and_windows",
    )(
        far,
        target,
        spot,
        ocean_mixing,
        arrived.reshape(near * spots, fields, LANES),
        parent_column,
        scaled,
        sea_share,
        base,
        hot,
        shares.reshape(2, near, rows, fields, LANES),
    )
    ocean_updated = diffuse_ocean(state, ocean_mixing, forcing, mask).transpose(1, 0, 2)
    tendency, forcing = lax.optimization_barrier((tendency, forcing))
    atmos_updated = diffuse_atmos(atmos_profiles, atmos_mixing, tendency)
    back = to_near(send.reshape(near, 2, packed, fields, LANES))
    back, ocean_updated, atmos_updated = lax.optimization_barrier(
        (back, ocean_updated, atmos_updated)
    )
    sums_away = collect(asked, far, back, per_owner, columns, False)
    sums_away, back = lax.optimization_barrier((sums_away, back))
    other_sums = to_far(sums_away)
    sums_home = collect(asked, far, back, per_owner, columns, True)
    other_sums, sums_home = lax.optimization_barrier((other_sums, sums_home))
    surface_state = pl.pallas_call(
        final_kernel,
        in_specs=[vmem] * 4,
        out_specs=vmem,
        out_shape=jax.ShapeDtypeStruct((fields, columns), jnp.float32),
        compiler_params=params,
        name="surface_state",
    )(sums_home, other_sums, land_weight.reshape(1, columns), land_surface)
    return (atmos_updated, ocean_updated, surface_state)


def solution(mesh):
    comp, sub = mesh.devices.shape
    halves = jax.sharding.Mesh(mesh.devices.reshape(2, comp // 2, sub), AXES)
    split = P(None, AXES)
    return jax.shard_map(
        per_device,
        mesh=halves,
        in_specs=(
            P(None, None, AXES),
            P(),
            P(AXES),
            split,
            split,
            P(AXES),
            split,
            P(None, None, AXES),
            P(),
            P(AXES),
            split,
            split,
            split,
            split,
        ),
        out_specs=(P(None, None, AXES), P(None, None, AXES), split),
        check_vma=False,
    )
```
